32 devices in a mesh: tm: 8 (over y, x, core), feat: 4 (over z).
Axes of the slice: x: 2, y: 2, z: 4, core: 2. Of those that a mesh axis runs over, the one named last changes fastest.
Arguments:
- coords: int32 [4096, 3, 1500], P('tm'), may hold values from -29696 to 29696
- frame_scale: float32 [4096], P('tm'), may hold values from 1e-05 to 4e-05, as said below
- pairs: int32 [2, 8192], P(None, 'feat'), may hold values from 0 to 1499, as said below
- walker_lengths: int32 [8], replicated, may hold values from 1 to 1024, 4096 in all
Outputs:
- cov_zero: float32 [8192, 8192], P('tm', 'feat')
- cov_lag: float32 [8192, 8192], P('tm', 'feat')
The draws below stay inside these ranges and needn't reach their ends.
Inputs may be any that keep to these rules, and one draw needn't show every extreme that they name: `frame_scale`: varies smoothly over frames with frame-to-frame noise. `pairs`: the two residues of a feature differ.
All inputs are finite; a program needn't handle non-finite values.
Results may differ from the reference program's by a relative error of at most 0.0016.
Values may be sent and summed in bfloat16 or wider, within the bound.
No kernel may reach another device: no remote copies, remote signals or barrier semaphores. Data moves between devices by JAX's collectives and lax.ppermute only.
A program may use at most 192 MiB of HBM per device.

```python
import math
import jax
import jax.numpy as jnp
import numpy as np
from jax import lax

FEATS = 8192
RES = 1500
FR_DEV = 512
LAG = 384
FRAMES = 4096
WALKERS = 8


def draw_frame_scale(key, part):
    key = jax.random.fold_in(key, 11)
    steps = jnp.arange(FRAMES, dtype=jnp.float32) / jnp.float32(FRAMES)
    noise = jax.random.uniform(key, (FRAMES,), jnp.float32, 0.85, 1.15)
    drift = 0.4
    return (2.7e-05 * jnp.exp(-drift * steps) * noise).astype(jnp.float32)


def draw_pairs(key, part):
    key = jax.random.fold_in(key, 5)
    key_first, key_step = jax.random.split(key)
    first = jax.random.randint(key_first, (FEATS,), 0, RES, dtype=jnp.int32)
    step = jax.random.randint(key_step, (FEATS,), 1, RES, dtype=jnp.int32)
    second = (first + step) % RES
    return jnp.stack([first, second]).astype(jnp.int32)


def place_ends(result, stream_key, smallest, high):
    place = [jax.random.randint(jax.random.fold_in(stream_key, axis), (), 0, length) for axis, length in enumerate(result.shape)]
    main_axis = result.shape.index(max(result.shape))
    neighbour = place[:main_axis] + [(place[main_axis] + 1) % result.shape[main_axis]] + place[main_axis + 1:]
    return result.at[tuple(place)].set(smallest).at[tuple(neighbour)].set(high)


def length_profile(count, total, reach, lean):
    weights = [(1 << 20) // math.isqrt(grade ** lean) + 1 for grade in range(2, count + 1)]
    spare, holding = total - reach - (count - 1), [1] * (count - 1)
    while spare > 0:
        free = [i for i in range(count - 1) if holding[i] < reach]
        mass, budget = sum([weights[i] for i in free]), spare
        for i in free:
            addition = min(reach - holding[i], max(1, budget * weights[i] // mass), spare)
            holding[i] = holding[i] + addition
            spare = spare - addition
    return np.array([reach] + holding)


def uneven(rng, amount, total, bound, skew):
    if amount == 2:
        one = jax.random.randint(rng, (), max(1, total - bound), min(bound, total - 1) + 1)
        return jnp.stack([one, total - one])
    sizes = jnp.asarray(length_profile(amount, total, bound, skew), jnp.int32)
    twos = (amount - 1) // 2
    source_of, taker = sizes[1:1 + 2 * twos:2], sizes[2:2 + 2 * twos:2]
    room = jnp.minimum(source_of - 1, bound - taker)
    moved = jax.random.randint(jax.random.fold_in(rng, 1), (twos,), 0, 1 << 20) % (room + 1)
    sizes = sizes.at[1:1 + 2 * twos:2].set(source_of - moved).at[2:2 + 2 * twos:2].set(taker + moved)
    return sizes[jax.random.permutation(jax.random.fold_in(rng, 2), amount)]


def setup_inputs(seed: int = 0) -> dict:
    streams_of = jax.random.split(jax.random.key(seed), 5)
    coords = place_ends(jax.random.randint(streams_of[0], (FRAMES, 3, RES), -29696, 29697), jax.random.fold_in(streams_of[0], 1), -29696, 29696).astype(jnp.int32)
    frame_scale = draw_frame_scale(jax.random.fold_in(streams_of[4], 71), 0)
    pairs = draw_pairs(jax.random.fold_in(streams_of[4], 71), 0)
    walker_lengths = uneven(streams_of[3], WALKERS, FRAMES, 2 * FR_DEV, 2).astype(jnp.int32)
    return {"coords": coords, "frame_scale": frame_scale, "pairs": pairs, "walker_lengths": walker_lengths}


def contact_block(coords_float, scale_sq, first, second):
    left = jnp.take(coords_float, first, axis=2)
    right = jnp.take(coords_float, second, axis=2)
    diff = left - right
    squares = diff[:, 0] * diff[:, 0] + diff[:, 1] * diff[:, 1] + diff[:, 2] * diff[:, 2]
    dist_sq = scale_sq[:, None] * squares
    return 1.0 / (1.0 + dist_sq * dist_sq * dist_sq)


def reference(coords, frame_scale, pairs, walker_lengths):
    block = min(512, FEATS)
    count = FEATS // block
    coords_float = coords.astype(jnp.float32)
    scale_sq = frame_scale * frame_scale
    grouped = pairs.reshape(2, count, block).transpose(1, 0, 2)
    blocks = lax.map(lambda pair_block: contact_block(coords_float, scale_sq, pair_block[0], pair_block[1]), grouped)
    contact = blocks.transpose(1, 0, 2).reshape(FRAMES, FEATS)
    mean = jnp.sum(contact, axis=0) / jnp.float32(FRAMES)
    centered = (contact - mean).astype(jnp.bfloat16)
    ends = jnp.cumsum(walker_lengths).astype(jnp.int32)
    times = jnp.arange(FRAMES, dtype=jnp.int32)
    later = times + LAG
    own = jnp.sum((times[:, None] >= ends[None, :]).astype(jnp.int32), axis=1)
    ahead = jnp.sum((later[:, None] >= ends[None, :]).astype(jnp.int32), axis=1)
    valid = (own == ahead) & (later < FRAMES)
    npairs = jnp.sum(jnp.maximum(walker_lengths - LAG, 0)).astype(jnp.float32)
    shifted = jnp.concatenate([centered[LAG:], jnp.zeros((LAG, FEATS), jnp.bfloat16)], axis=0)
    lagged = jnp.where(valid[:, None], shifted, jnp.zeros_like(shifted))
    dims = (((0,), (0,)), ((), ()))
    cov_zero = lax.dot_general(centered, centered, dims, preferred_element_type=jnp.float32) / jnp.float32(FRAMES)
    cov_lag = lax.dot_general(centered, lagged, dims, preferred_element_type=jnp.float32) / npairs
    return cov_zero, cov_lag
```

```python
import functools

import jax
import jax.numpy as jnp
from jax import lax
from jax.experimental import pallas as pl
from jax.experimental.pallas import tpu as pltpu
from jax.sharding import PartitionSpec as P

LAG = 384
CHUNK = 128
VMEM_LIMIT = 56 * 1024 * 1024


def contact_values(coords, frame_scale, pairs):
    frames_dev = coords.shape[0]
    residues = coords.shape[2]
    flat = coords.astype(jnp.float32).reshape(frames_dev * 3, residues)
    rows_iota = jnp.arange(residues, dtype=jnp.int32)[:, None]
    selector = (rows_iota == pairs[0][None, :]).astype(jnp.float32) - (
        rows_iota == pairs[1][None, :]
    ).astype(jnp.float32)
    diff = jnp.dot(
        flat, selector, precision=lax.Precision.HIGHEST, preferred_element_type=jnp.float32
    )
    diff = diff.reshape(frames_dev, 3, pairs.shape[1])
    squares = diff[:, 0] * diff[:, 0] + diff[:, 1] * diff[:, 1] + diff[:, 2] * diff[:, 2]
    dist_sq = (frame_scale * frame_scale)[:, None] * squares
    return 1.0 / (1.0 + dist_sq * dist_sq * dist_sq)


def walker_mask(walker_lengths, count, frames_all):
    ends = jnp.cumsum(walker_lengths)
    times = jnp.arange(count, dtype=jnp.int32)
    later = times + LAG
    own = jnp.sum((times[:, None] >= ends[None, :]).astype(jnp.int32), axis=1)
    ahead = jnp.sum((later[:, None] >= ends[None, :]).astype(jnp.int32), axis=1)
    return (own == ahead) & (later < frames_all)


def contract(left, right):
    return lax.dot_general(
        left, right, (((0,), (0,)), ((), ())), preferred_element_type=jnp.float32
    )


def plain_shards(coords, frame_scale, pairs, walker_lengths):
    tm_count = lax.axis_size("tm")
    frames_dev = coords.shape[0]
    local_feats = pairs.shape[1]
    frames_all = frames_dev * tm_count
    contact = contact_values(coords, frame_scale, pairs)
    totals = lax.psum(jnp.sum(contact, axis=0), "tm")
    centered = (contact - totals / jnp.float32(frames_all)).astype(jnp.bfloat16)
    npairs = jnp.sum(jnp.maximum(walker_lengths - LAG, 0)).astype(jnp.float32)
    column_series = lax.all_gather(centered, "tm", axis=0, tiled=True)
    wide = lax.all_gather(centered, "feat", axis=1, tiled=True)
    row_series = lax.all_to_all(wide, "tm", split_axis=1, concat_axis=0, tiled=True)
    valid = walker_mask(walker_lengths, frames_all, frames_all)
    later = jnp.concatenate(
        [column_series[LAG:], jnp.zeros((LAG, local_feats), jnp.bfloat16)], axis=0
    )
    lagged = jnp.where(valid[:, None], later, jnp.zeros_like(later))
    same = contract(row_series, column_series)
    cross = contract(row_series, lagged)
    return (same / jnp.float32(frames_all), cross / npairs)


def split_coords(x):
    high = ((x + 128) >> 8) << 8
    low = x - high
    return (
        high.astype(jnp.float32).astype(jnp.bfloat16),
        low.astype(jnp.float32).astype(jnp.bfloat16),
    )


def selector_rows(pairs_block, depth):
    feats = pairs_block.shape[0]
    lanes = lax.broadcasted_iota(jnp.int32, (feats, depth), 1)
    first = pairs_block[:, 0:1]
    second = pairs_block[:, 1:2]
    one = jnp.float32(1.0)
    zero = jnp.float32(0.0)
    value = jnp.where(lanes == first, one, jnp.where(lanes == second, -one, zero))
    return value.astype(jnp.bfloat16)


def switch(squares, scale):
    dist_sq = (scale * scale) * squares
    return 1.0 / (1.0 + dist_sq * dist_sq * dist_sq)


def contact_kernel(with_sums, slot_ref, coords_ref, scale_ref, pairs_ref, out_ref, *rest):
    if with_sums:
        sums_ref, padded, parts = rest
    else:
        padded, parts = rest
    residues, frames = coords_ref.shape[1:]
    depth = padded.shape[0]

    @pl.when(pl.program_id(0) == 0)
    def _():
        padded[...] = jnp.zeros_like(padded)
        for k in range(3):
            padded[0:residues, :] = coords_ref[k]
            high, low = split_coords(padded[...])
            parts[0:depth, k * frames : (k + 1) * frames] = high
            parts[depth : 2 * depth, k * frames : (k + 1) * frames] = low

    selector = selector_rows(pairs_ref[...], depth)
    both = jnp.concatenate([selector, selector], axis=1)
    diff = jnp.dot(both, parts[...], preferred_element_type=jnp.float32)
    d0 = diff[:, 0:frames]
    d1 = diff[:, frames : 2 * frames]
    d2 = diff[:, 2 * frames : 3 * frames]
    contact = switch(d0 * d0 + d1 * d1 + d2 * d2, scale_ref[...])
    out_ref[...] = contact
    if with_sums:
        part = contact[:, 0:CHUNK]
        for c in range(1, frames // CHUNK):
            part = part + contact[:, c * CHUNK : (c + 1) * CHUNK]
        sums_ref[...] = jnp.sum(part.T, axis=0, keepdims=True)


def contacts(slot, coords_t, scale_row, pairs_t, frames, block, with_sums):
    residues = coords_t.shape[1]
    feats = pairs_t.shape[0]
    depth = -(-residues // 256) * 256
    out_shape = [jax.ShapeDtypeStruct((feats, frames), jnp.float32)]
    out_specs = [pl.BlockSpec((block, frames), lambda n, s: (n, 0))]
    if with_sums:
        out_shape.append(jax.ShapeDtypeStruct((1, feats), jnp.float32))
        out_specs.append(pl.BlockSpec((1, block), lambda n, s: (0, n)))
    flops = 2 * feats * 2 * depth * 3 * frames
    return pl.pallas_call(
        functools.partial(contact_kernel, with_sums),
        out_shape=out_shape,
        grid_spec=pltpu.PrefetchScalarGridSpec(
            num_scalar_prefetch=1,
            grid=(feats // block,),
            in_specs=[
                pl.BlockSpec((3, residues, frames), lambda n, s: (0, 0, s[0])),
                pl.BlockSpec((1, frames), lambda n, s: (0, s[0])),
                pl.BlockSpec((block, 2), lambda n, s: (n, 0)),
            ],
            out_specs=out_specs,
            scratch_shapes=[
                pltpu.VMEM((depth, frames), jnp.int32),
                pltpu.VMEM((2 * depth, 3 * frames), jnp.bfloat16),
            ],
        ),
        compiler_params=pltpu.CompilerParams(vmem_limit_bytes=VMEM_LIMIT),
        cost_estimate=pl.CostEstimate(
            flops=flops, bytes_accessed=12 * residues * frames + 4 * feats * frames, transcendentals=0
        ),
    )(slot, coords_t, scale_row, pairs_t)


def as_column(row):
    return jnp.broadcast_to(row, (CHUNK, row.shape[1])).T


def center_kernel(slot_ref, cols_ref, cols_mean_ref, rows_ref, rows_mean_ref, cols_out, rows_out):
    col = as_column(cols_mean_ref[...])
    for c in range(cols_ref.shape[1] // CHUNK):
        lanes = slice(c * CHUNK, (c + 1) * CHUNK)
        cols_out[:, lanes] = (cols_ref[:, lanes] - col).astype(jnp.bfloat16)
    rows_out[...] = (rows_ref[...] - as_column(rows_mean_ref[...])).astype(jnp.bfloat16)


def center(slot, cols, rows, mean, steps=4):
    feats, frames = cols.shape
    all_feats, chunk = rows.shape
    cols_block = feats // steps
    rows_block = all_feats // steps
    return pl.pallas_call(
        center_kernel,
        out_shape=[
            jax.ShapeDtypeStruct(cols.shape, jnp.bfloat16),
            jax.ShapeDtypeStruct(rows.shape, jnp.bfloat16),
        ],
        grid_spec=pltpu.PrefetchScalarGridSpec(
            num_scalar_prefetch=1,
            grid=(steps,),
            in_specs=[
                pl.BlockSpec((cols_block, frames), lambda n, s: (n, 0)),
                pl.BlockSpec((1, cols_block), lambda n, s: (0, s[0] * steps + n)),
                pl.BlockSpec((rows_block, chunk), lambda n, s: (n, 0)),
                pl.BlockSpec((1, rows_block), lambda n, s: (0, n)),
            ],
            out_specs=[
                pl.BlockSpec((cols_block, frames), lambda n, s: (n, 0)),
                pl.BlockSpec((rows_block, chunk), lambda n, s: (n, 0)),
            ],
        ),
        compiler_params=pltpu.CompilerParams(vmem_limit_bytes=VMEM_LIMIT),
        cost_estimate=pl.CostEstimate(
            flops=2 * (cols.size + rows.size), bytes_accessed=6 * (cols.size + rows.size), transcendentals=0
        ),
    )(slot, cols, mean, rows, mean)


def product_kernel(
    count, parts, me_ref, rows_ref, mask_ref, factors_ref, *rest
):
    cols_refs = rest[:count]
    same_ref, cross_ref, left = rest[count:]
    frames = parts * CHUNK
    behind = LAG // CHUNK

    @pl.when(pl.program_id(0) == 0)
    def _():
        for d in range(count):
            j = me_ref[0] ^ d
            before = jnp.maximum(j - 1, 0)
            mask = mask_ref[j]
            for z in range(parts):
                lanes = slice(d * frames + z * CHUNK, d * frames + (z + 1) * CHUNK)
                left[0, :, lanes] = rows_ref[z, j]
                if z >= behind:
                    shifted = rows_ref[z - behind, j]
                else:
                    shifted = rows_ref[z - behind + parts, before]
                left[1, :, lanes] = shifted * mask[:, z * CHUNK : (z + 1) * CHUNK].astype(jnp.bfloat16)

    right = jnp.concatenate([ref[...] for ref in cols_refs], axis=1)
    dims = (((1,), (1,)), ((), ()))
    same = lax.dot_general(left[0], right, dims, preferred_element_type=jnp.float32)
    same_ref[...] = same * factors_ref[0]
    cross = lax.dot_general(left[1], right, dims, preferred_element_type=jnp.float32)
    cross_ref[...] = cross / factors_ref[1]


def products(me, rows, mask, factors, cols, block=512):
    parts, count, row_feats, _ = rows.shape
    feats, frames = cols[0].shape
    out = jax.ShapeDtypeStruct((row_feats, feats), jnp.float32)
    whole = lambda shape: pl.BlockSpec(shape, lambda n, s: (0,) * len(shape))
    return pl.pallas_call(
        functools.partial(product_kernel, count, parts),
        out_shape=[out, out],
        grid_spec=pltpu.PrefetchScalarGridSpec(
            num_scalar_prefetch=1,
            grid=(feats // block,),
            in_specs=[
                pl.BlockSpec(rows.shape, lambda n, s: (0, 0, 0, 0), pipeline_mode=pl.Buffered(1)),
                whole(mask.shape),
                pl.BlockSpec(memory_space=pltpu.SMEM),
            ]
            + [pl.BlockSpec((block, frames), lambda n, s: (n, 0))] * count,
            out_specs=[pl.BlockSpec((row_feats, block), lambda n, s: (0, n))] * 2,
            scratch_shapes=[pltpu.VMEM((2, row_feats, count * frames), jnp.bfloat16)],
        ),
        compiler_params=pltpu.CompilerParams(vmem_limit_bytes=VMEM_LIMIT),
        cost_estimate=pl.CostEstimate(
            flops=4 * row_feats * feats * count * frames,
            bytes_accessed=2 * rows.size + 2 * count * feats * frames + 8 * row_feats * feats,
            transcendentals=0,
        ),
    )(me, rows, mask, factors, *cols)


def swap(x, bit, count):
    return lax.ppermute(x, "tm", [(i, i ^ bit) for i in range(count)])


def square_gather(x):
    half = x.shape[0] // 2
    core = swap(x, 1, 8)
    along_x = swap(x, 2, 8)
    along_y = swap(x, 4, 8)
    corner_low = swap(along_x[:half], 4, 8)
    corner_high = swap(along_y[half:], 2, 8)
    corner = jnp.concatenate([corner_low, corner_high], axis=0)
    return [
        x,
        core,
        along_x,
        swap(along_x, 1, 8),
        along_y,
        swap(along_y, 1, 8),
        corner,
        swap(corner, 1, 8),
    ]


def shards(coords, frame_scale, pairs, walker_lengths):
    tm_count = lax.axis_size("tm")
    feat_count = lax.axis_size("feat")
    frames_dev = coords.shape[0]
    feats = pairs.shape[1]
    all_feats = feats * feat_count
    frames_all = frames_dev * tm_count
    me = lax.axis_index("tm").astype(jnp.int32).reshape(1)
    slot = lax.axis_index("feat").astype(jnp.int32).reshape(1)
    start = jnp.zeros((1,), jnp.int32)

    coords_t = jnp.transpose(coords, (1, 2, 0))
    scale_row = frame_scale.reshape(1, frames_dev)
    all_pairs = lax.all_gather(pairs, "feat", axis=1, tiled=True)

    raw_cols, sums = contacts(start, coords_t, scale_row, pairs.T, frames_dev, 512, True)
    every = lax.all_gather(sums, ("tm", "feat"), axis=0, tiled=True)
    (raw_rows,) = contacts(slot, coords_t, scale_row, all_pairs.T, CHUNK, 1024, False)
    totals = jnp.sum(every.reshape(tm_count, feat_count * feats), axis=0)
    mean = (totals / jnp.float32(frames_all)).reshape(1, all_feats)

    cols, rows = center(slot, raw_cols, raw_rows, mean)
    rows = rows.reshape(tm_count, all_feats // tm_count, CHUNK)
    rows = lax.all_to_all(rows, "tm", split_axis=0, concat_axis=0, tiled=True)
    rows = lax.all_gather(rows, "feat", axis=0, tiled=False)
    cols = square_gather(cols)

    valid = walker_mask(walker_lengths, frames_all, frames_all)
    mask = jnp.concatenate([jnp.zeros((LAG,), jnp.float32), valid[:-LAG].astype(jnp.float32)])
    npairs = jnp.sum(jnp.maximum(walker_lengths - LAG, 0)).astype(jnp.float32)
    factors = jnp.stack([jnp.float32(1.0 / frames_all), npairs])
    return products(me, rows, mask.reshape(tm_count, 1, frames_dev), factors, cols)


def solution(mesh):
    def run(coords, frame_scale, pairs, walker_lengths):
        tm_count, feat_count = mesh.shape["tm"], mesh.shape["feat"]
        frames_dev = coords.shape[0] // tm_count
        fits = tm_count == 8 and frames_dev == feat_count * CHUNK and frames_dev > LAG
        return jax.shard_map(
            shards if fits else plain_shards,
            mesh=mesh,
            in_specs=(P("tm", None, None), P("tm"), P(None, "feat"), P()),
            out_specs=(P("tm", "feat"), P("tm", "feat")),
            check_vma=False,
        )(coords, frame_scale, pairs, walker_lengths)

    return run
```

```python
import functools

import jax
import jax.numpy as jnp
from jax import lax
from jax.experimental import pallas as pl
from jax.experimental.pallas import tpu as pltpu
from jax.sharding import PartitionSpec as P

LAG = 384
CHUNK = 128
VMEM_LIMIT = 56 * 1024 * 1024


def contact_values(coords, frame_scale, pairs):
    frames_dev = coords.shape[0]
    residues = coords.shape[2]
    flat = coords.astype(jnp.float32).reshape(frames_dev * 3, residues)
    rows_iota = jnp.arange(residues, dtype=jnp.int32)[:, None]
    selector = (rows_iota == pairs[0][None, :]).astype(jnp.float32) - (
        rows_iota == pairs[1][None, :]
    ).astype(jnp.float32)
    diff = jnp.dot(
        flat, selector, precision=lax.Precision.HIGHEST, preferred_element_type=jnp.float32
    )
    diff = diff.reshape(frames_dev, 3, pairs.shape[1])
    squares = diff[:, 0] * diff[:, 0] + diff[:, 1] * diff[:, 1] + diff[:, 2] * diff[:, 2]
    dist_sq = (frame_scale * frame_scale)[:, None] * squares
    return 1.0 / (1.0 + dist_sq * dist_sq * dist_sq)


def walker_mask(walker_lengths, count, frames_all):
    ends = jnp.cumsum(walker_lengths)
    times = jnp.arange(count, dtype=jnp.int32)
    later = times + LAG
    own = jnp.sum((times[:, None] >= ends[None, :]).astype(jnp.int32), axis=1)
    ahead = jnp.sum((later[:, None] >= ends[None, :]).astype(jnp.int32), axis=1)
    return (own == ahead) & (later < frames_all)


def contract(left, right):
    return lax.dot_general(
        left, right, (((0,), (0,)), ((), ())), preferred_element_type=jnp.float32
    )


def plain_shards(coords, frame_scale, pairs, walker_lengths):
    tm_count = lax.axis_size("tm")
    frames_dev = coords.shape[0]
    local_feats = pairs.shape[1]
    frames_all = frames_dev * tm_count
    contact = contact_values(coords, frame_scale, pairs)
    totals = lax.psum(jnp.sum(contact, axis=0), "tm")
    centered = (contact - totals / jnp.float32(frames_all)).astype(jnp.bfloat16)
    npairs = jnp.sum(jnp.maximum(walker_lengths - LAG, 0)).astype(jnp.float32)
    column_series = lax.all_gather(centered, "tm", axis=0, tiled=True)
    wide = lax.all_gather(centered, "feat", axis=1, tiled=True)
    row_series = lax.all_to_all(wide, "tm", split_axis=1, concat_axis=0, tiled=True)
    valid = walker_mask(walker_lengths, frames_all, frames_all)
    later = jnp.concatenate(
        [column_series[LAG:], jnp.zeros((LAG, local_feats), jnp.bfloat16)], axis=0
    )
    lagged = jnp.where(valid[:, None], later, jnp.zeros_like(later))
    same = contract(row_series, column_series)
    cross = contract(row_series, lagged)
    return (same / jnp.float32(frames_all), cross / npairs)


def switch(squares, scale):
    dist_sq = (scale * scale) * squares
    return 1.0 / (1.0 + dist_sq * dist_sq * dist_sq)


def as_column(row):
    return jnp.broadcast_to(row, (CHUNK, row.shape[1])).T


def square_rows(pairs_ref, base, feats, table, stride, squares):
    for f in range(feats):
        first = pl.multiple_of(pairs_ref[0, base + f] * stride, 8)
        second = pl.multiple_of(pairs_ref[1, base + f] * stride, 8)
        diff = table[pl.ds(first, stride), :] - table[pl.ds(second, stride), :]
        diff = diff.astype(jnp.float32)
        squares[pl.ds(f * stride, stride), :] = diff * diff


def add_axes(squares, start, feats, stride, step):
    at = lambda k: squares[pl.ds(start + k * step, feats, stride=stride), :]
    return at(0) + at(1) + at(2)


def own_kernel(centered, pairs_ref, coords_ref, scale_ref, *rest):
    if centered:
        mean_ref, out_ref, table, squares, part = rest
    else:
        out_ref, sums_ref, table, squares, part = rest
    residues, frames = coords_ref.shape[1:]
    chunks = frames // CHUNK
    stride = -(-3 * chunks // 8) * 8
    block = out_ref.shape[0]
    group = squares.shape[0] // stride
    step = pl.program_id(0)

    @pl.when(step == 0)
    def _():
        for k in range(3):
            for c in range(chunks):
                table[pl.ds(k * chunks + c, residues, stride=stride), :] = coords_ref[
                    k, :, c * CHUNK : (c + 1) * CHUNK
                ]

    if centered:
        part[...] = as_column(mean_ref[...])

    @pl.loop(0, block // group)
    def _(g):
        at = pl.multiple_of(g * group, group)
        square_rows(pairs_ref, step * block + at, group, table, stride, squares)
        for h in range(group // 16):
            here = pl.ds(pl.multiple_of(at + h * 16, 16), 16)
            total = jnp.zeros((16, CHUNK), jnp.float32)
            for c in range(chunks):
                lanes = slice(c * CHUNK, (c + 1) * CHUNK)
                added = add_axes(squares, h * 16 * stride + c, 16, stride, chunks)
                contact = switch(added, scale_ref[:, lanes])
                if centered:
                    out_ref[here, lanes] = (contact - part[here, :]).astype(jnp.bfloat16)
                else:
                    out_ref[here, lanes] = contact
                    total = total + contact
            if not centered:
                part[here, :] = total

    if not centered:
        sums_ref[...] = jnp.sum(part[...].T, axis=0, keepdims=True)


def own_contacts(pairs, coords_t, scale_row, mean=None, block=256, group=32):
    residues, frames = coords_t.shape[1:]
    feats = pairs.shape[1]
    stride = -(-3 * (frames // CHUNK) // 8) * 8
    centered = mean is not None
    in_specs = [
        pl.BlockSpec(memory_space=pltpu.SMEM),
        pl.BlockSpec(coords_t.shape, lambda n: (0, 0, 0), pipeline_mode=pl.Buffered(1)),
        pl.BlockSpec((1, frames), lambda n: (0, 0)),
    ]
    out_spec = pl.BlockSpec((block, frames), lambda n: (n, 0))
    row_spec = pl.BlockSpec((1, block), lambda n: (0, n))
    args = [pairs, coords_t, scale_row]
    if centered:
        in_specs.append(row_spec)
        args.append(mean)
        out_shape = jax.ShapeDtypeStruct((feats, frames), jnp.bfloat16)
        out_specs = out_spec
    else:
        out_shape = [
            jax.ShapeDtypeStruct((feats, frames), jnp.float32),
            jax.ShapeDtypeStruct((1, feats), jnp.float32),
        ]
        out_specs = [out_spec, row_spec]
    return pl.pallas_call(
        functools.partial(own_kernel, centered),
        out_shape=out_shape,
        grid=(feats // block,),
        in_specs=in_specs,
        out_specs=out_specs,
        scratch_shapes=[
            pltpu.VMEM((residues * stride, CHUNK), jnp.int32),
            pltpu.VMEM((group * stride, CHUNK), jnp.float32),
            pltpu.VMEM((block, CHUNK), jnp.float32),
        ],
        compiler_params=pltpu.CompilerParams(vmem_limit_bytes=VMEM_LIMIT),
        cost_estimate=pl.CostEstimate(
            flops=40 * feats * frames, bytes_accessed=4 * coords_t.size + 4 * feats * frames, transcendentals=0
        ),
    )(*args)


def sent_kernel(pairs_ref, first_ref, second_ref, scale_ref, mean_ref, out_ref, table, squares, column):
    residues = first_ref.shape[1]
    block = out_ref.shape[1]
    group = squares.shape[0] // 8
    step = pl.program_id(0)

    @pl.when(step == 0)
    def _():
        for s, ref in enumerate((first_ref, second_ref)):
            for k in range(3):
                table[pl.ds(2 * k + s, residues, stride=8), :] = ref[k].astype(jnp.int32)

    column[...] = as_column(mean_ref[...])

    @pl.loop(0, block // group)
    def _(g):
        at = pl.multiple_of(g * group, group)
        square_rows(pairs_ref, step * block + at, group, table, 8, squares)
        for h in range(group // 16):
            here = pl.ds(pl.multiple_of(at + h * 16, 16), 16)
            for s in range(2):
                added = add_axes(squares, h * 128 + s, 16, 8, 2)
                contact = switch(added, scale_ref[s : s + 1, :])
                out_ref[s, here, :] = (contact - column[here, :]).astype(jnp.bfloat16)


def sent_contacts(pairs, first, second, scales, mean, block=512, group=64):
    residues = first.shape[1]
    feats = pairs.shape[1]
    whole = pl.BlockSpec(first.shape, lambda n: (0, 0, 0), pipeline_mode=pl.Buffered(1))
    return pl.pallas_call(
        sent_kernel,
        out_shape=jax.ShapeDtypeStruct((2, feats, CHUNK), jnp.bfloat16),
        grid=(feats // block,),
        in_specs=[
            pl.BlockSpec(memory_space=pltpu.SMEM),
            whole,
            whole,
            pl.BlockSpec((2, CHUNK), lambda n: (0, 0)),
            pl.BlockSpec((1, block), lambda n: (0, n)),
        ],
        out_specs=pl.BlockSpec((2, block, CHUNK), lambda n: (0, n, 0)),
        scratch_shapes=[
            pltpu.VMEM((residues * 8, CHUNK), jnp.int32),
            pltpu.VMEM((group * 8, CHUNK), jnp.float32),
            pltpu.VMEM((block, CHUNK), jnp.float32),
        ],
        compiler_params=pltpu.CompilerParams(vmem_limit_bytes=VMEM_LIMIT),
        cost_estimate=pl.CostEstimate(
            flops=80 * feats * CHUNK, bytes_accessed=4 * first.size + 4 * feats * CHUNK, transcendentals=0
        ),
    )(pairs, first, second, scales, mean)


def center_kernel(raw_ref, mean_ref, out_ref):
    col = as_column(mean_ref[...])
    for c in range(raw_ref.shape[1] // CHUNK):
        lanes = slice(c * CHUNK, (c + 1) * CHUNK)
        out_ref[:, lanes] = (raw_ref[:, lanes] - col).astype(jnp.bfloat16)


def center(raw, mean, block=512):
    feats, frames = raw.shape
    return pl.pallas_call(
        center_kernel,
        out_shape=jax.ShapeDtypeStruct(raw.shape, jnp.bfloat16),
        grid=(feats // block,),
        in_specs=[
            pl.BlockSpec((block, frames), lambda n: (n, 0)),
            pl.BlockSpec((1, block), lambda n: (0, n)),
        ],
        out_specs=pl.BlockSpec((block, frames), lambda n: (n, 0)),
        compiler_params=pltpu.CompilerParams(vmem_limit_bytes=VMEM_LIMIT),
        cost_estimate=pl.CostEstimate(flops=2 * raw.size, bytes_accessed=6 * raw.size, transcendentals=0),
    )(raw, mean)


def product_kernel(first, plan, last, has_sum, me_ref, mask_ref, factors_ref, *rest):
    rows_refs = rest[: len(plan)]
    rest = rest[len(plan) :]
    cols_refs, rest = rest[:8], rest[8:]
    if has_sum:
        same_in, cross_in, same_ref, cross_ref, left, right, ahead = rest
    else:
        same_ref, cross_ref, left, right, ahead = rest
    frames = cols_refs[0].shape[1]
    me = me_ref[0]
    count = left.shape[2] // frames

    @pl.when(pl.program_id(0) == 0)
    def _():
        ahead[...] = jnp.zeros_like(ahead)
        slot = 0
        for form, ref in zip(plan, rows_refs):
            for b in range(1 if form is None else form[1]):
                mask = mask_ref[me ^ (first + slot)]
                for c in range(frames // CHUNK):
                    lanes = slice(slot * frames + c * CHUNK, slot * frames + (c + 1) * CHUNK)
                    inner = slice(c * CHUNK, (c + 1) * CHUNK)
                    value = ref[:, inner] if form is None else ref[c, b]
                    left[0, :, lanes] = value
                    left[1, :, lanes] = value * mask[:, inner].astype(jnp.bfloat16)
                slot += 1

    kept = frames - LAG
    for d in range(8):
        j = me ^ d
        if first <= d < first + count:
            at = (d - first) * frames
            right[:, at : at + frames] = cols_refs[d][...]
            ahead[:, at : at + kept] = cols_refs[d][:, LAG:]
        slot = (me ^ (j - 1)) - first

        @pl.when((j > 0) & (slot >= 0) & (slot < count))
        def _():
            ahead[:, pl.ds(pl.multiple_of(slot * frames + kept, CHUNK), LAG)] = cols_refs[d][:, :LAG]

    dims = (((1,), (1,)), ((), ()))
    same = lax.dot_general(left[0], right[...], dims, preferred_element_type=jnp.float32)
    if has_sum:
        same = same + same_in[...]
    same_ref[...] = same * factors_ref[0] if last else same
    cross = lax.dot_general(left[1], ahead[...], dims, preferred_element_type=jnp.float32)
    if has_sum:
        cross = cross + cross_in[...]
    cross_ref[...] = cross / factors_ref[1] if last else cross


def products(me, mask, factors, first, rows, cols, sums=None, last=False, block=512):
    plan = tuple(None if r.ndim == 2 else (r.shape[0], r.shape[1]) for r in rows)
    count = sum(1 if form is None else form[1] for form in plan)
    feats, frames = cols[0].shape
    row_feats = rows[0].shape[-2]
    out = jax.ShapeDtypeStruct((row_feats, feats), jnp.float32)
    whole = lambda x: pl.BlockSpec(x.shape, lambda n, s: (0,) * x.ndim, pipeline_mode=pl.Buffered(1))
    tile = pl.BlockSpec((row_feats, block), lambda n, s: (0, n))
    sums = () if sums is None else tuple(sums)
    inputs = [mask, factors, *rows, *cols, *sums]
    aliases = {1 + len(inputs) - 2 + i: i for i in range(2)} if sums else {}
    return pl.pallas_call(
        functools.partial(product_kernel, first, plan, last, bool(sums)),
        out_shape=[out, out],
        grid_spec=pltpu.PrefetchScalarGridSpec(
            num_scalar_prefetch=1,
            grid=(feats // block,),
            in_specs=[whole(mask), pl.BlockSpec(memory_space=pltpu.SMEM)]
            + [whole(r) for r in rows]
            + [pl.BlockSpec((block, frames), lambda n, s: (n, 0))] * 8
            + [tile] * len(sums),
            out_specs=[tile] * 2,
            scratch_shapes=[
                pltpu.VMEM((2, row_feats, count * frames), jnp.bfloat16),
                pltpu.VMEM((block, count * frames), jnp.bfloat16),
                pltpu.VMEM((block, count * frames), jnp.bfloat16),
            ],
        ),
        input_output_aliases=aliases,
        compiler_params=pltpu.CompilerParams(vmem_limit_bytes=VMEM_LIMIT),
        cost_estimate=pl.CostEstimate(
            flops=4 * row_feats * feats * count * frames,
            bytes_accessed=2 * count * frames * row_feats
            + 16 * feats * frames
            + (16 if sums else 8) * row_feats * feats,
            transcendentals=0,
        ),
    )(me, *inputs)


def swap(x, bits):
    return lax.ppermute(x, "tm", [(i, i ^ bits) for i in range(8)])


def square_gather(x, axis, half):
    core = swap(x, 1)
    along_x = swap(x, 2)
    along_y = swap(x, 4)
    low = swap(lax.slice_in_dim(along_x, 0, half, axis=axis), 4)
    high = swap(lax.slice_in_dim(along_y, half, x.shape[axis], axis=axis), 2)
    corner = jnp.concatenate([low, high], axis=axis)
    return [x, core, along_x, swap(along_x, 1), along_y, swap(along_y, 1), corner, swap(corner, 1)]


def from_owner(x, feat_count):
    owner = lambda i: i * feat_count // 8
    total = jnp.where(lax.axis_index("feat") == owner(lax.axis_index("tm")), x, jnp.zeros_like(x))
    for s in range(1, feat_count):
        perm = [
            (i * feat_count + owner(i), i * feat_count + (owner(i) + s) % feat_count)
            for i in range(8)
        ]
        total = total + lax.ppermute(x, ("tm", "feat"), perm)
    return total


def shards(coords, frame_scale, pairs, walker_lengths):
    tm_count = lax.axis_size("tm")
    feat_count = lax.axis_size("feat")
    frames_dev = coords.shape[0]
    feats = pairs.shape[1]
    frames_all = frames_dev * tm_count
    row_feats = feats * feat_count // tm_count
    tm = lax.axis_index("tm").astype(jnp.int32)
    z = lax.axis_index("feat").astype(jnp.int32)
    me = tm.reshape(1)
    own_half = (tm % (feats // row_feats)) * row_feats

    coords_t = jnp.transpose(coords, (1, 2, 0))
    scale_row = frame_scale.reshape(1, frames_dev)
    quarter = lax.dynamic_slice_in_dim(coords_t, z * CHUNK, CHUNK, axis=2).astype(jnp.int16)
    quarters = square_gather(quarter, 1, (coords_t.shape[1] // 32) * 16)
    chip_pairs = from_owner(pairs, feat_count)

    raw, sums = own_contacts(pairs, coords_t, scale_row)
    note = jnp.concatenate([sums, scale_row], axis=1)
    notes = [note] + [swap(note, d) for d in range(1, 8)]
    totals = notes[0][:, :feats]
    for other in notes[1:]:
        totals = totals + other[:, :feats]
    mean = totals / jnp.float32(frames_all)
    chip_mean = from_owner(mean, feat_count)
    scales = [lax.dynamic_slice_in_dim(n, feats + z * CHUNK, CHUNK, axis=1) for n in notes]

    cols = square_gather(center(raw, mean), 0, feats // 2)

    row_pairs = lax.dynamic_slice_in_dim(chip_pairs, own_half, row_feats, axis=1)
    row_mean = lax.dynamic_slice_in_dim(chip_mean, own_half, row_feats, axis=1)
    pieces = []
    for d in (2, 4, 6):
        piece = sent_contacts(
            row_pairs,
            quarters[d],
            quarters[d + 1],
            jnp.concatenate([scales[d], scales[d + 1]], axis=0),
            row_mean,
        )
        pieces.append(lax.all_gather(piece, "feat", axis=0, tiled=False))

    chip = own_contacts(chip_pairs, coords_t, scale_row, chip_mean)
    mine = lax.dynamic_slice_in_dim(chip, own_half, row_feats, axis=0)
    others = lax.dynamic_slice_in_dim(chip, row_feats - own_half, row_feats, axis=0)
    partner = swap(others, 1)

    valid = walker_mask(walker_lengths, frames_all, frames_all)
    mask = valid.astype(jnp.float32).reshape(tm_count, 1, frames_dev)
    npairs = jnp.sum(jnp.maximum(walker_lengths - LAG, 0)).astype(jnp.float32)
    factors = jnp.stack([jnp.float32(1.0 / frames_all), npairs])
    partial = products(me, mask, factors, 0, [mine, partner, pieces[0], pieces[1]], cols)
    return products(me, mask, factors, 6, [pieces[2]], cols, sums=partial, last=True)


def solution(mesh):
    def run(coords, frame_scale, pairs, walker_lengths):
        tm_count, feat_count = mesh.shape["tm"], mesh.shape["feat"]
        frames_dev = coords.shape[0] // tm_count
        square = tm_count == 8 and feat_count == 4
        fits = square and frames_dev == feat_count * CHUNK and pairs.shape[1] % (tm_count * 512) == 0
        return jax.shard_map(
            shards if fits else plain_shards,
            mesh=mesh,
            in_specs=(P("tm", None, None), P("tm"), P(None, "feat"), P()),
            out_specs=(P("tm", "feat"), P("tm", "feat")),
            check_vma=False,
        )(coords, frame_scale, pairs, walker_lengths)

    return run
```

```python
import functools

import jax
import jax.numpy as jnp
from jax import lax
from jax.experimental import pallas as pl
from jax.experimental.pallas import tpu as pltpu
from jax.sharding import PartitionSpec as P

LAG = 384
CHUNK = 128
VMEM_LIMIT = 56 * 1024 * 1024


def contact_values(coords, frame_scale, pairs):
    frames_dev = coords.shape[0]
    residues = coords.shape[2]
    flat = coords.astype(jnp.float32).reshape(frames_dev * 3, residues)
    rows_iota = jnp.arange(residues, dtype=jnp.int32)[:, None]
    selector = (rows_iota == pairs[0][None, :]).astype(jnp.float32) - (
        rows_iota == pairs[1][None, :]
    ).astype(jnp.float32)
    diff = jnp.dot(
        flat, selector, precision=lax.Precision.HIGHEST, preferred_element_type=jnp.float32
    )
    diff = diff.reshape(frames_dev, 3, pairs.shape[1])
    squares = diff[:, 0] * diff[:, 0] + diff[:, 1] * diff[:, 1] + diff[:, 2] * diff[:, 2]
    dist_sq = (frame_scale * frame_scale)[:, None] * squares
    return 1.0 / (1.0 + dist_sq * dist_sq * dist_sq)


def walker_mask(walker_lengths, count, frames_all):
    ends = jnp.cumsum(walker_lengths)
    times = jnp.arange(count, dtype=jnp.int32)
    later = times + LAG
    own = jnp.sum((times[:, None] >= ends[None, :]).astype(jnp.int32), axis=1)
    ahead = jnp.sum((later[:, None] >= ends[None, :]).astype(jnp.int32), axis=1)
    return (own == ahead) & (later < frames_all)


def contract(left, right):
    return lax.dot_general(
        left, right, (((0,), (0,)), ((), ())), preferred_element_type=jnp.float32
    )


def plain_shards(coords, frame_scale, pairs, walker_lengths):
    tm_count = lax.axis_size("tm")
    frames_dev = coords.shape[0]
    local_feats = pairs.shape[1]
    frames_all = frames_dev * tm_count
    contact = contact_values(coords, frame_scale, pairs)
    totals = lax.psum(jnp.sum(contact, axis=0), "tm")
    centered = (contact - totals / jnp.float32(frames_all)).astype(jnp.bfloat16)
    npairs = jnp.sum(jnp.maximum(walker_lengths - LAG, 0)).astype(jnp.float32)
    column_series = lax.all_gather(centered, "tm", axis=0, tiled=True)
    wide = lax.all_gather(centered, "feat", axis=1, tiled=True)
    row_series = lax.all_to_all(wide, "tm", split_axis=1, concat_axis=0, tiled=True)
    valid = walker_mask(walker_lengths, frames_all, frames_all)
    later = jnp.concatenate(
        [column_series[LAG:], jnp.zeros((LAG, local_feats), jnp.bfloat16)], axis=0
    )
    lagged = jnp.where(valid[:, None], later, jnp.zeros_like(later))
    same = contract(row_series, column_series)
    cross = contract(row_series, lagged)
    return (same / jnp.float32(frames_all), cross / npairs)


def switch(squares, scale):
    dist_sq = (scale * scale) * squares
    return 1.0 / (1.0 + dist_sq * dist_sq * dist_sq)


def as_column(row):
    return jnp.broadcast_to(row, (CHUNK, row.shape[1])).T


def gather_kernel(centered, coords_count, pairs_ref, scale_ref, *rest):
    coords_refs, rest = rest[:coords_count], rest[coords_count:]
    if centered:
        mean_ref, out_ref, table, dense, part = rest
    else:
        out_ref, sums_ref, table, dense, part = rest
    residues = coords_refs[0].shape[1]
    chunks = 4 if coords_count == 1 else coords_count
    stride = table.shape[0] // residues
    block = part.shape[0]
    group = dense.shape[0] // chunks
    step = pl.program_id(0)

    @pl.when(step == 0)
    def _():
        for k in range(3):
            for c in range(chunks):
                if coords_count == 1:
                    plane = coords_refs[0][k, :, c * CHUNK : (c + 1) * CHUNK]
                else:
                    plane = coords_refs[c][k].astype(jnp.int32)
                table[pl.ds(k * chunks + c, residues, stride=stride), :] = plane

    if centered:
        part[...] = as_column(mean_ref[...])
    sublane = lax.broadcasted_iota(jnp.int32, (8, CHUNK), 0)
    scale = scale_ref[...]

    def squares(f):
        first = pl.multiple_of(pairs_ref[0, f], 8)
        second = pl.multiple_of(pairs_ref[1, f], 8)
        diff = (table[pl.ds(first, stride), :] - table[pl.ds(second, stride), :]).astype(jnp.float32)
        diff = diff * diff
        if chunks == 4:
            total = diff[0:8] + jnp.where(sublane < 4, diff[8:16], 0.0)
            return total + pltpu.roll(total, 4, 0)
        diff = jnp.where(sublane < 6, diff, 0.0)
        total = diff + pltpu.roll(diff, 4, 0)
        return total + pltpu.roll(total, 2, 0)

    @pl.loop(0, block // group)
    def _(g):
        at = pl.multiple_of(g * group, group)
        packed = 8 // chunks
        for f in range(0, group, packed):
            base = step * block + at + f
            value = squares(base)
            for i in range(1, packed):
                value = jnp.where(sublane < i * chunks, value, squares(base + i))
            dense[pl.ds(f * chunks, 8), :] = switch(value, scale)
        for h in range(group // 16):
            here = pl.ds(pl.multiple_of(at + h * 16, 16), 16)
            total = jnp.zeros((16, CHUNK), jnp.float32)
            for c in range(chunks):
                contact = dense[pl.ds(h * 16 * chunks + c, 16, stride=chunks), :]
                if not centered:
                    out_ref[here, c * CHUNK : (c + 1) * CHUNK] = contact
                    total = total + contact
                elif coords_count == 1:
                    out_ref[here, c * CHUNK : (c + 1) * CHUNK] = (contact - part[here, :]).astype(
                        jnp.bfloat16
                    )
                else:
                    out_ref[c, here, :] = (contact - part[here, :]).astype(jnp.bfloat16)
            if not centered:
                part[here, :] = total

    if not centered:
        sums_ref[...] = jnp.sum(part[...].T, axis=0, keepdims=True)


def contacts(pairs, coords, scale, mean=None, block=512, group=32):
    residues = coords[0].shape[1]
    feats = pairs.shape[1]
    chunks = scale.shape[0]
    stride = -(-3 * chunks // 8) * 8
    centered = mean is not None
    row_spec = pl.BlockSpec((1, block), lambda n: (0, n))
    in_specs = [pl.BlockSpec(memory_space=pltpu.SMEM), pl.BlockSpec((8, CHUNK), lambda n: (0, 0))]
    in_specs += [pl.BlockSpec(x.shape, lambda n: (0, 0, 0), pipeline_mode=pl.Buffered(1)) for x in coords]
    args = [pairs * stride, jnp.concatenate([scale] * (8 // chunks), axis=0), *coords]
    if len(coords) == 1:
        out_shape = jax.ShapeDtypeStruct((feats, chunks * CHUNK), jnp.bfloat16 if centered else jnp.float32)
        out_specs = pl.BlockSpec((block, chunks * CHUNK), lambda n: (n, 0))
    else:
        out_shape = jax.ShapeDtypeStruct((chunks, feats, CHUNK), jnp.bfloat16)
        out_specs = pl.BlockSpec((chunks, block, CHUNK), lambda n: (0, n, 0))
    if centered:
        in_specs.append(row_spec)
        args.append(mean)
    else:
        out_shape = [out_shape, jax.ShapeDtypeStruct((1, feats), jnp.float32)]
        out_specs = [out_specs, row_spec]
    return pl.pallas_call(
        functools.partial(gather_kernel, centered, len(coords)),
        out_shape=out_shape,
        grid=(feats // block,),
        in_specs=in_specs,
        out_specs=out_specs,
        scratch_shapes=[
            pltpu.VMEM((residues * stride, CHUNK), jnp.int32),
            pltpu.VMEM((group * chunks, CHUNK), jnp.float32),
            pltpu.VMEM((block, CHUNK), jnp.float32),
        ],
        compiler_params=pltpu.CompilerParams(vmem_limit_bytes=VMEM_LIMIT),
        cost_estimate=pl.CostEstimate(
            flops=40 * feats * chunks * CHUNK,
            bytes_accessed=12 * residues * chunks * CHUNK + 4 * feats * chunks * CHUNK,
            transcendentals=0,
        ),
    )(*args)


def center_kernel(raw_ref, mean_ref, out_ref):
    col = as_column(mean_ref[...])
    for c in range(raw_ref.shape[1] // CHUNK):
        lanes = slice(c * CHUNK, (c + 1) * CHUNK)
        out_ref[:, lanes] = (raw_ref[:, lanes] - col).astype(jnp.bfloat16)


def center(raw, mean, block=512):
    feats, frames = raw.shape
    return pl.pallas_call(
        center_kernel,
        out_shape=jax.ShapeDtypeStruct(raw.shape, jnp.bfloat16),
        grid=(feats // block,),
        in_specs=[
            pl.BlockSpec((block, frames), lambda n: (n, 0)),
            pl.BlockSpec((1, block), lambda n: (0, n)),
        ],
        out_specs=pl.BlockSpec((block, frames), lambda n: (n, 0)),
        compiler_params=pltpu.CompilerParams(vmem_limit_bytes=VMEM_LIMIT),
        cost_estimate=pl.CostEstimate(flops=2 * raw.size, bytes_accessed=6 * raw.size, transcendentals=0),
    )(raw, mean)


def product_kernel(sources, me_ref, mask_ref, factors_ref, *rest):
    rows_refs, rest = rest[:5], rest[5:]
    cols_refs, rest = rest[:8], rest[8:]
    same_ref, cross_ref, left = rest[-3:]
    feats = same_ref.shape[0]
    frames = cols_refs[0].shape[1]
    parts = frames // CHUNK
    me = me_ref[0]

    @pl.when(pl.program_id(0) == 0)
    def _():
        for d, (operand, block) in enumerate(sources):
            j = me ^ d
            after = me ^ lax.rem(j + 1, 8)
            mask = mask_ref[j].astype(jnp.bfloat16)
            ref = rows_refs[operand]
            for c in range(parts):
                inner = slice(c * CHUNK, (c + 1) * CHUNK)
                value = ref[:, inner] if block is None else ref[c, block]
                left[0:feats, d * frames + c * CHUNK : d * frames + (c + 1) * CHUNK] = value
                to = c + LAG // CHUNK
                start = (d if to < parts else after) * frames + (to % parts) * CHUNK
                if to >= parts:
                    start = pl.multiple_of(start, CHUNK)
                left[feats : 2 * feats, pl.ds(start, CHUNK)] = value * mask[:, inner]

    right = jnp.concatenate([ref[...] for ref in cols_refs], axis=1)
    both = lax.dot_general(
        left[...], right, (((1,), (1,)), ((), ())), preferred_element_type=jnp.float32
    )
    same_ref[...] = both[0:feats] * factors_ref[0]
    cross_ref[...] = both[feats : 2 * feats] / factors_ref[1]


def products(me, mask, factors, piece, pieces, near, gathered, cols, outs=(), block=512):
    sources = ((0, None), (1, None), (2, None), (4, 0), (3, None), (4, 1), (4, 2), (4, 3))
    feats, frames = cols[0].shape
    row_feats = near[0].shape[0]
    rows = row_feats // pieces
    out = jax.ShapeDtypeStruct((row_feats, feats), jnp.float32)
    whole = lambda x: pl.BlockSpec(x.shape, lambda n, s: (0,) * x.ndim, pipeline_mode=pl.Buffered(1))
    inputs = [mask, factors, *near, gathered, *cols, *outs]
    return pl.pallas_call(
        functools.partial(product_kernel, sources),
        out_shape=[out, out],
        grid_spec=pltpu.PrefetchScalarGridSpec(
            num_scalar_prefetch=1,
            grid=(feats // block,),
            in_specs=[whole(mask), pl.BlockSpec(memory_space=pltpu.SMEM)]
            + [pl.BlockSpec((rows, frames), lambda n, s: (piece, 0), pipeline_mode=pl.Buffered(1))] * 4
            + [whole(gathered)]
            + [pl.BlockSpec((block, frames), lambda n, s: (n, 0))] * 8
            + [pl.BlockSpec(memory_space=pl.ANY)] * len(outs),
            out_specs=[pl.BlockSpec((rows, block), lambda n, s: (piece, n))] * 2,
            scratch_shapes=[pltpu.VMEM((2 * rows, 8 * frames), jnp.bfloat16)],
        ),
        input_output_aliases={1 + len(inputs) - 2 + i: i for i in range(len(outs))},
        compiler_params=pltpu.CompilerParams(vmem_limit_bytes=VMEM_LIMIT),
        cost_estimate=pl.CostEstimate(
            flops=4 * rows * feats * 8 * frames,
            bytes_accessed=16 * frames * (rows + feats) + 8 * rows * feats,
            transcendentals=0,
        ),
    )(me, *inputs)


def swap(x, bits):
    return lax.ppermute(x, "tm", [(i, i ^ bits) for i in range(8)])


def corner(along_x, along_y, axis, half):
    low = swap(lax.slice_in_dim(along_x, 0, half, axis=axis), 4)
    high = swap(lax.slice_in_dim(along_y, half, along_y.shape[axis], axis=axis), 2)
    return jnp.concatenate([low, high], axis=axis)


def from_owner(x, feat_count, *after):
    owner = lambda i: i * feat_count // 8
    held = [jnp.where(lax.axis_index("feat") == owner(lax.axis_index("tm")), x, jnp.zeros_like(x))]
    for s in range(1, feat_count):
        perm = [
            (i * feat_count + owner(i), i * feat_count + (owner(i) + s) % feat_count)
            for i in range(8)
        ]
        held.append(lax.ppermute(x, ("tm", "feat"), perm))
    if after:
        held = tie(held, *after)
    return sum(held[1:], held[0])


def tie(x, *after):
    return lax.optimization_barrier((x, after))[0]


def shards(coords, frame_scale, pairs, walker_lengths):
    tm_count = lax.axis_size("tm")
    feat_count = lax.axis_size("feat")
    frames_dev = coords.shape[0]
    feats = pairs.shape[1]
    frames_all = frames_dev * tm_count
    row_feats = feats * feat_count // tm_count
    parts = frames_dev // CHUNK
    pieces = 2
    tm = lax.axis_index("tm").astype(jnp.int32)
    z = lax.axis_index("feat").astype(jnp.int32)
    me = tm.reshape(1)
    own_half = (tm % (feats // row_feats)) * row_feats

    coords_t = jnp.transpose(coords, (1, 2, 0))
    scale_own = frame_scale.reshape(parts, CHUNK)
    quarter = lax.dynamic_slice_in_dim(coords_t, z * CHUNK, CHUNK, axis=2).astype(jnp.int16)
    quarters = {3: swap(quarter, 3), 5: swap(quarter, 5)}

    raw, sums = contacts(pairs, [coords_t], scale_own)
    note = jnp.concatenate([sums, frame_scale.reshape(1, frames_dev)], axis=1)
    notes = [note] + [swap(note, d) for d in range(1, 8)]

    quarters = tie(quarters, sums)
    quarters[7] = corner(quarters[3], quarters[5], 1, (coords_t.shape[1] // 32) * 16)
    chip_pairs = from_owner(pairs, feat_count, sums)
    row_pairs = lax.dynamic_slice_in_dim(chip_pairs, own_half, row_feats, axis=1)
    near_pairs = jnp.concatenate([swap(row_pairs, 2), swap(row_pairs, 4)], axis=1)

    totals = notes[0][:, :feats]
    for other in notes[1:]:
        totals = totals + other[:, :feats]
    mean = totals / jnp.float32(frames_all)
    chip_mean = from_owner(mean, feat_count)
    row_mean = lax.dynamic_slice_in_dim(chip_mean, own_half, row_feats, axis=1)
    scales = [lax.dynamic_slice_in_dim(n, feats + z * CHUNK, CHUNK, axis=1) for n in notes]
    scale_of = lambda *d: jnp.concatenate([scales[i] for i in d], axis=0)

    sent_near = contacts(row_pairs, [quarters[3], quarters[5]], scale_of(3, 5), row_mean)
    raw = tie(raw, sent_near, quarters[7])
    mine = center(raw, mean)
    quarters[6] = swap(quarters[7], 1)
    cols = {0: mine, 1: swap(mine, 1), 2: swap(mine, 2), 4: swap(mine, 4)}

    far = tie([quarters[6], quarters[7]], mine)
    sent_far = contacts(row_pairs, far, scale_of(6, 7), row_mean)
    joined = []
    for p in range(pieces):
        cut = slice(p * row_feats // pieces, (p + 1) * row_feats // pieces)
        joined.append(jnp.concatenate([sent_near[:, cut], sent_far[:, cut]], axis=0))
    gathered = [lax.all_gather(x, "feat", axis=0, tiled=False) for x in joined]

    near_mean = jnp.concatenate([swap(row_mean, 2), swap(row_mean, 4)], axis=1)
    out_pairs = jnp.concatenate([near_pairs, chip_pairs], axis=1)
    out_mean = jnp.concatenate([near_mean, chip_mean], axis=1)
    out_pairs = tie(out_pairs, *joined)
    sent = contacts(out_pairs, [coords_t], scale_own, out_mean)
    rows_cut = lambda start: lax.dynamic_slice_in_dim(sent, start, row_feats, axis=0)
    own = rows_cut(2 * row_feats + own_half)
    partner = swap(rows_cut(3 * row_feats - own_half), 1)

    cols = tie(cols, sent)
    cols[6] = corner(cols[2], cols[4], 0, feats // 2)
    from_x = swap(rows_cut(0), 2)
    from_y = swap(rows_cut(row_feats), 4)
    for d in (2, 4, 6):
        cols[d + 1] = swap(cols[d], 1)
    cols = [cols[d] for d in range(8)]

    valid = walker_mask(walker_lengths, frames_all, frames_all)
    mask = valid.astype(jnp.float32).reshape(tm_count, 1, frames_dev)
    npairs = jnp.sum(jnp.maximum(walker_lengths - LAG, 0)).astype(jnp.float32)
    factors = jnp.stack([jnp.float32(1.0 / frames_all), npairs])
    outs = ()
    for p in range(pieces):
        outs = products(me, mask, factors, p, pieces, [own, partner, from_x, from_y], gathered[p], cols, outs)
    return outs


def solution(mesh):
    def run(coords, frame_scale, pairs, walker_lengths):
        tm_count, feat_count = mesh.shape["tm"], mesh.shape["feat"]
        frames_dev = coords.shape[0] // tm_count
        square = tm_count == 8 and feat_count == 4
        fits = square and frames_dev == 4 * CHUNK and pairs.shape[1] == 16 * 512
        return jax.shard_map(
            shards if fits else plain_shards,
            mesh=mesh,
            in_specs=(P("tm", None, None), P("tm"), P(None, "feat"), P()),
            out_specs=(P("tm", "feat"), P("tm", "feat")),
            check_vma=False,
        )(coords, frame_scale, pairs, walker_lengths)

    return run
```

```python
import functools

import jax
import jax.numpy as jnp
from jax import lax
from jax.experimental import pallas as pl
from jax.experimental.pallas import tpu as pltpu
from jax.sharding import PartitionSpec as P

LAG = 384
CHUNK = 128
VMEM_LIMIT = 56 * 1024 * 1024
NEAR = (0, 1, 2, 4)
FAR = (3, 5, 6, 7)


def contact_values(coords, frame_scale, pairs):
    frames_dev = coords.shape[0]
    residues = coords.shape[2]
    flat = coords.astype(jnp.float32).reshape(frames_dev * 3, residues)
    rows_iota = jnp.arange(residues, dtype=jnp.int32)[:, None]
    selector = (rows_iota == pairs[0][None, :]).astype(jnp.float32) - (
        rows_iota == pairs[1][None, :]
    ).astype(jnp.float32)
    diff = jnp.dot(
        flat, selector, precision=lax.Precision.HIGHEST, preferred_element_type=jnp.float32
    )
    diff = diff.reshape(frames_dev, 3, pairs.shape[1])
    squares = diff[:, 0] * diff[:, 0] + diff[:, 1] * diff[:, 1] + diff[:, 2] * diff[:, 2]
    dist_sq = (frame_scale * frame_scale)[:, None] * squares
    return 1.0 / (1.0 + dist_sq * dist_sq * dist_sq)


def walker_mask(walker_lengths, count, frames_all):
    ends = jnp.cumsum(walker_lengths)
    times = jnp.arange(count, dtype=jnp.int32)
    later = times + LAG
    own = jnp.sum((times[:, None] >= ends[None, :]).astype(jnp.int32), axis=1)
    ahead = jnp.sum((later[:, None] >= ends[None, :]).astype(jnp.int32), axis=1)
    return (own == ahead) & (later < frames_all)


def estimate(micros):
    return pl.CostEstimate(
        flops=int(micros * 1_000_000_000), bytes_accessed=int(micros * 3_690_000), transcendentals=0
    )


def contract(left, right):
    return lax.dot_general(
        left, right, (((0,), (0,)), ((), ())), preferred_element_type=jnp.float32
    )


def plain_shards(coords, frame_scale, pairs, walker_lengths):
    tm_count = lax.axis_size("tm")
    frames_dev = coords.shape[0]
    local_feats = pairs.shape[1]
    frames_all = frames_dev * tm_count
    contact = contact_values(coords, frame_scale, pairs)
    totals = lax.psum(jnp.sum(contact, axis=0), "tm")
    centered = (contact - totals / jnp.float32(frames_all)).astype(jnp.bfloat16)
    npairs = jnp.sum(jnp.maximum(walker_lengths - LAG, 0)).astype(jnp.float32)
    column_series = lax.all_gather(centered, "tm", axis=0, tiled=True)
    wide = lax.all_gather(centered, "feat", axis=1, tiled=True)
    row_series = lax.all_to_all(wide, "tm", split_axis=1, concat_axis=0, tiled=True)
    valid = walker_mask(walker_lengths, frames_all, frames_all)
    later = jnp.concatenate(
        [column_series[LAG:], jnp.zeros((LAG, local_feats), jnp.bfloat16)], axis=0
    )
    lagged = jnp.where(valid[:, None], later, jnp.zeros_like(later))
    same = contract(row_series, column_series)
    cross = contract(row_series, lagged)
    return (same / jnp.float32(frames_all), cross / npairs)


def switch(squares, scale):
    dist_sq = (scale * scale) * squares
    return 1.0 / (1.0 + dist_sq * dist_sq * dist_sq)


def as_column(row):
    return jnp.broadcast_to(row, (CHUNK, row.shape[1])).T


def gather_kernel(centered, coords_count, pairs_ref, scale_ref, *rest):
    coords_refs, rest = rest[:coords_count], rest[coords_count:]
    if centered:
        mean_ref, out_ref, table, dense, part, held, arrived = rest
    else:
        out_ref, sums_ref, table, dense, part, held, arrived = rest
    residues = coords_refs[0].shape[1]
    chunks = 4 if coords_count == 1 else coords_count
    stride = table.shape[0] // residues
    block = part.shape[0]
    group = dense.shape[0] // chunks
    step = pl.program_id(0)

    @pl.when(step == 0)
    def _():
        copies = [
            pltpu.make_async_copy(ref.at[k], held.at[n, k], arrived.at[n, k])
            for k in range(3)
            for n, ref in enumerate(coords_refs)
        ]
        for copy in copies:
            copy.start()
        for k in range(3):
            for n in range(coords_count):
                copies[k * coords_count + n].wait()
            for c in range(chunks):
                if coords_count == 1:
                    plane = held[0, k, :, c * CHUNK : (c + 1) * CHUNK]
                else:
                    plane = held[c, k].astype(jnp.int32)
                table[pl.ds(k * chunks + c, residues, stride=stride), :] = plane

    if centered:
        part[...] = as_column(mean_ref[...])
    sublane = lax.broadcasted_iota(jnp.int32, (8, CHUNK), 0)
    scale = scale_ref[...]

    def squares(f):
        first = pl.multiple_of(pairs_ref[0, f], 8)
        second = pl.multiple_of(pairs_ref[1, f], 8)
        diff = (table[pl.ds(first, stride), :] - table[pl.ds(second, stride), :]).astype(jnp.float32)
        diff = diff * diff
        if chunks == 4:
            total = diff[0:8] + jnp.where(sublane < 4, diff[8:16], 0.0)
            return total + pltpu.roll(total, 4, 0)
        diff = jnp.where(sublane < 6, diff, 0.0)
        total = diff + pltpu.roll(diff, 4, 0)
        return total + pltpu.roll(total, 2, 0)

    @pl.loop(0, block // group)
    def _(g):
        at = pl.multiple_of(g * group, group)
        packed = 8 // chunks
        for f in range(0, group, packed):
            base = step * block + at + f
            value = squares(base)
            for i in range(1, packed):
                value = jnp.where(sublane < i * chunks, value, squares(base + i))
            dense[pl.ds(f * chunks, 8), :] = switch(value, scale)
        for h in range(group // 16):
            here = pl.ds(pl.multiple_of(at + h * 16, 16), 16)
            total = jnp.zeros((16, CHUNK), jnp.float32)
            for c in range(chunks):
                contact = dense[pl.ds(h * 16 * chunks + c, 16, stride=chunks), :]
                if not centered:
                    out_ref[here, c * CHUNK : (c + 1) * CHUNK] = contact
                    total = total + contact
                elif coords_count == 1:
                    out_ref[here, c * CHUNK : (c + 1) * CHUNK] = (contact - part[here, :]).astype(
                        jnp.bfloat16
                    )
                else:
                    out_ref[c, here, :] = (contact - part[here, :]).astype(jnp.bfloat16)
            if not centered:
                part[here, :] = total

    if not centered:
        sums_ref[...] = jnp.sum(part[...].T, axis=0, keepdims=True)


def contacts(pairs, coords, scale, mean=None, block=512, group=32):
    residues = coords[0].shape[1]
    feats = pairs.shape[1]
    chunks = scale.shape[0]
    stride = -(-3 * chunks // 8) * 8
    centered = mean is not None
    row_spec = pl.BlockSpec((1, block), lambda n: (0, n))
    in_specs = [pl.BlockSpec(memory_space=pltpu.SMEM), pl.BlockSpec((8, CHUNK), lambda n: (0, 0))]
    in_specs += [pl.BlockSpec(memory_space=pl.ANY) for x in coords]
    args = [pairs * stride, jnp.concatenate([scale] * (8 // chunks), axis=0), *coords]
    if len(coords) == 1:
        out_shape = jax.ShapeDtypeStruct((feats, chunks * CHUNK), jnp.bfloat16 if centered else jnp.float32)
        out_specs = pl.BlockSpec((block, chunks * CHUNK), lambda n: (n, 0))
    else:
        out_shape = jax.ShapeDtypeStruct((chunks, feats, CHUNK), jnp.bfloat16)
        out_specs = pl.BlockSpec((chunks, block, CHUNK), lambda n: (0, n, 0))
    if centered:
        in_specs.append(row_spec)
        args.append(mean)
    else:
        out_shape = [out_shape, jax.ShapeDtypeStruct((1, feats), jnp.float32)]
        out_specs = [out_specs, row_spec]
    return pl.pallas_call(
        functools.partial(gather_kernel, centered, len(coords)),
        out_shape=out_shape,
        grid=(feats // block,),
        in_specs=in_specs,
        out_specs=out_specs,
        scratch_shapes=[
            pltpu.VMEM((residues * stride, CHUNK), jnp.int32),
            pltpu.VMEM((group * chunks, CHUNK), jnp.float32),
            pltpu.VMEM((block, CHUNK), jnp.float32),
            pltpu.VMEM((len(coords),) + coords[0].shape, coords[0].dtype),
            pltpu.SemaphoreType.DMA((len(coords), 3)),
        ],
        compiler_params=pltpu.CompilerParams(vmem_limit_bytes=VMEM_LIMIT),
        cost_estimate=estimate(1),
    )(*args)


def center_kernel(raw_ref, mean_ref, out_ref):
    for c in range(raw_ref.shape[1] // CHUNK):
        frames = slice(c * CHUNK, (c + 1) * CHUNK)
        out_ref[frames, :] = (raw_ref[:, frames].T - mean_ref[...]).astype(jnp.bfloat16)


def center(raw, mean, block=512):
    feats, frames = raw.shape
    return pl.pallas_call(
        center_kernel,
        out_shape=jax.ShapeDtypeStruct((frames, feats), jnp.bfloat16),
        grid=(feats // block,),
        in_specs=[
            pl.BlockSpec((block, frames), lambda n: (n, 0)),
            pl.BlockSpec((1, block), lambda n: (0, n)),
        ],
        out_specs=pl.BlockSpec((frames, block), lambda n: (0, n)),
        compiler_params=pltpu.CompilerParams(vmem_limit_bytes=VMEM_LIMIT),
        cost_estimate=estimate(1),
    )(raw, mean)


def product_kernel(place_ref, mask_ref, factors_ref, *rest):
    near_refs, rest = rest[: len(NEAR)], rest[len(NEAR) :]
    far_refs, rest = rest[:7], rest[7:]
    cols_refs, rest = rest[:8], rest[8:]
    same_ref, cross_ref, left = rest[-3:]
    feats = same_ref.shape[0]
    frames = cols_refs[0].shape[0]
    parts = frames // CHUNK
    me, z = place_ref[0], place_ref[1]

    def put(d, c, value):
        j = me ^ d
        after = me ^ lax.rem(j + 1, 8)
        mask = mask_ref[j, c].astype(jnp.bfloat16)
        at = pl.multiple_of(d * frames + c * CHUNK, CHUNK)
        left[0:feats, pl.ds(at, CHUNK)] = value
        to = c + LAG // CHUNK
        at = jnp.where(to < parts, d * frames + to * CHUNK, after * frames + (to - parts) * CHUNK)
        left[feats : 2 * feats, pl.ds(pl.multiple_of(at, CHUNK), CHUNK)] = value * mask

    @pl.when(pl.program_id(0) == 0)
    def _():
        for d, ref in zip(NEAR, near_refs):
            for c in range(parts):
                put(d, c, ref[:, c * CHUNK : (c + 1) * CHUNK])
        for n, ref in enumerate(far_refs):
            hop = (n + 1) // 2
            c = z - hop if n % 2 else z + hop

            @pl.when((c >= 0) & (c < parts))
            def _():
                for i, d in enumerate(FAR):
                    put(d, c, ref[0, i])

    right = jnp.concatenate([ref[...] for ref in cols_refs], axis=0)
    both = jnp.dot(left[...], right, preferred_element_type=jnp.float32)
    same_ref[...] = both[0:feats] * factors_ref[0]
    cross_ref[...] = both[feats : 2 * feats] / factors_ref[1]


def products(place, mask, factors, piece, pieces, near, far, cols, outs=(), block=256):
    frames, feats = cols[0][0].shape
    rows = near[0].shape[0]
    row_feats = rows * pieces
    out = jax.ShapeDtypeStruct((row_feats, feats), jnp.float32)
    whole = lambda x: pl.BlockSpec(x.shape, lambda n, s: (0,) * x.ndim, pipeline_mode=pl.Buffered(1))
    part = lambda x: pl.BlockSpec(
        (1,) + x.shape[1:],
        lambda n, s: (piece if x.shape[0] == pieces else 0, 0, 0, 0),
        pipeline_mode=pl.Buffered(1),
    )
    inputs = [mask, factors, *near, *far, *[x for x, _ in cols], *outs]
    return pl.pallas_call(
        product_kernel,
        out_shape=[out, out],
        grid_spec=pltpu.PrefetchScalarGridSpec(
            num_scalar_prefetch=1,
            grid=(feats // block,),
            in_specs=[whole(mask), pl.BlockSpec(memory_space=pltpu.SMEM)]
            + [whole(x) for x in near]
            + [part(x) for x in far]
            + [pl.BlockSpec((frames, block), lambda n, s, i=i: (i, n)) for _, i in cols]
            + [pl.BlockSpec(memory_space=pl.ANY)] * len(outs),
            out_specs=[pl.BlockSpec((rows, block), lambda n, s: (piece, n))] * 2,
            scratch_shapes=[pltpu.VMEM((2 * rows, 8 * frames), jnp.bfloat16)],
        ),
        input_output_aliases={1 + len(inputs) - 2 + i: i for i in range(len(outs))},
        compiler_params=pltpu.CompilerParams(vmem_limit_bytes=VMEM_LIMIT),
        cost_estimate=estimate(24),
    )(place, *inputs)


def swap(x, bits):
    return lax.ppermute(x, "tm", [(i, i ^ bits) for i in range(8)])


def corner(along_x, along_y, axis, half):
    low = swap(lax.slice_in_dim(along_x, 0, half, axis=axis), 4)
    high = swap(lax.slice_in_dim(along_y, half, along_y.shape[axis], axis=axis), 2)
    return low, high


def line_gather(x, count):
    shift = lambda s: [(i, (i + s) % count) for i in range(count)]
    return jnp.stack([x] + [lax.ppermute(x, "feat", shift(s)) for s in range(1, count)])


def line_hop(up, down, hop, count):
    up = lax.ppermute(up, "feat", [(i, i + 1) for i in range(hop - 1, count - 1)])
    down = lax.ppermute(down, "feat", [(i + 1, i) for i in range(count - hop)])
    return up, down


def together(*values):
    return lax.optimization_barrier(values)


def shards(coords, frame_scale, pairs, walker_lengths):
    tm_count = lax.axis_size("tm")
    feat_count = lax.axis_size("feat")
    frames_dev = coords.shape[0]
    feats = pairs.shape[1]
    frames_all = frames_dev * tm_count
    row_feats = feats * feat_count // tm_count
    parts = frames_dev // CHUNK
    pieces = 1
    tm = lax.axis_index("tm").astype(jnp.int32)
    z = lax.axis_index("feat").astype(jnp.int32)
    place = jnp.stack([tm, z])
    own_half = (tm % (feats // row_feats)) * row_feats

    coords_t = jnp.transpose(coords, (1, 2, 0))
    scale_own = frame_scale.reshape(parts, CHUNK)
    quarter = lax.dynamic_slice_in_dim(coords_t, z * CHUNK, CHUNK, axis=2).astype(jnp.int16)
    quarters = {3: swap(quarter, 3), 5: swap(quarter, 5)}

    raw, sums = contacts(pairs, [coords_t], scale_own)
    raw, sums, quarters = together(raw, sums, quarters)
    halves = corner(quarters[3], quarters[5], 1, (coords_t.shape[1] // 32) * 16)
    note = jnp.concatenate([sums, frame_scale.reshape(1, frames_dev)], axis=1)
    notes = [note] + [swap(note, d) for d in range(1, 8)]

    totals = notes[0][:, :feats]
    for other in notes[1:]:
        totals = totals + other[:, :feats]
    mean = totals / jnp.float32(frames_all)
    scales = [lax.dynamic_slice_in_dim(n, feats + z * CHUNK, CHUNK, axis=1) for n in notes]
    scale_of = lambda *d: jnp.concatenate([scales[i] for i in d], axis=0)

    facts = line_gather(jnp.concatenate([mean, pairs.astype(jnp.float32)], axis=0), feat_count)
    mine, facts, halves = together(center(raw, mean), facts, halves)
    quarters[7] = jnp.concatenate(halves, axis=1)
    cols = {0: mine, 2: swap(mine, 2), 4: swap(mine, 4)}
    quarters[6] = swap(quarters[7], 1)

    def facts_of(i, start, count):
        back = (z - i * feat_count // tm_count) % feat_count
        return lax.dynamic_slice(facts, (back, 0, start), (1, 3, count))[0]

    row_facts = facts_of(tm, own_half, row_feats)
    out_facts = jnp.concatenate(
        [facts_of(tm ^ 2, own_half, row_feats), facts_of(tm ^ 4, own_half, row_feats), facts_of(tm, 0, feats)],
        axis=1,
    )
    row_facts, out_facts, scales = together(row_facts, out_facts, scales)
    row_mean, row_pairs = row_facts[0:1], row_facts[1:3].astype(jnp.int32)
    out_mean, out_pairs = out_facts[0:1], out_facts[1:3].astype(jnp.int32)

    sent_near = contacts(row_pairs, [quarters[3], quarters[5]], scale_of(3, 5), row_mean)
    sent_near, quarters, mine = together(sent_near, quarters, mine)
    cols[1] = swap(mine, 1)
    sent_far = contacts(row_pairs, [quarters[6], quarters[7]], scale_of(6, 7), row_mean)

    valid = walker_mask(walker_lengths, frames_all, frames_all)
    mask = valid.astype(jnp.float32).reshape(tm_count, parts, 1, CHUNK)
    npairs = jnp.sum(jnp.maximum(walker_lengths - LAG, 0)).astype(jnp.float32)
    factors = jnp.stack([jnp.float32(1.0 / frames_all), npairs])

    rows = row_feats // pieces
    joined = jnp.concatenate([sent_near, sent_far], axis=0).reshape(len(FAR), pieces, rows, CHUNK)
    joined = jnp.transpose(joined, (1, 0, 2, 3))
    out_pairs, mask, factors, joined = together(out_pairs, mask, factors, joined)
    up, down = line_hop(joined, joined, 1, feat_count)
    sent = contacts(out_pairs, [coords_t], scale_own, out_mean)
    sent, up, down = together(sent, up, down)
    far = [joined, up, down]
    up, down = line_hop(up, down, 2, feat_count)
    cut = lambda start: lax.dynamic_slice_in_dim(sent, start, row_feats, axis=0)
    own = cut(2 * row_feats + own_half)
    partner = swap(cut(3 * row_feats - own_half), 1)
    cols, sent = together(cols, sent)
    low, high = corner(cols[2], cols[4], 0, frames_dev // 2)
    low, high, up, down, sent = together(low, high, up, down, sent)
    far_cols = jnp.concatenate([cols[2], cols[4], low, high], axis=0)
    their_cols = swap(far_cols, 1)
    far += [up, down, *line_hop(up, down, 3, feat_count)]
    near = [own, partner, swap(cut(0), 2), swap(cut(row_feats), 4)]
    cols = [(cols[0], 0), (cols[1], 0)]
    for i in range(3):
        cols += [(far_cols, i), (their_cols, i)]
    return products(place, mask, factors, 0, pieces, near, far, cols)


def solution(mesh):
    def run(coords, frame_scale, pairs, walker_lengths):
        tm_count, feat_count = mesh.shape["tm"], mesh.shape["feat"]
        frames_dev = coords.shape[0] // tm_count
        square = tm_count == 8 and feat_count == 4
        fits = square and frames_dev == 4 * CHUNK and pairs.shape[1] == 16 * 512
        return jax.shard_map(
            shards if fits else plain_shards,
            mesh=mesh,
            in_specs=(P("tm", None, None), P("tm"), P(None, "feat"), P()),
            out_specs=(P("tm", "feat"), P("tm", "feat")),
            check_vma=False,
        )(coords, frame_scale, pairs, walker_lengths)

    return run
```

```python
import functools

import jax
import jax.numpy as jnp
from jax import lax
from jax.experimental import pallas as pl
from jax.experimental.pallas import tpu as pltpu
from jax.sharding import PartitionSpec as P

LAG = 384
CHUNK = 128
VMEM_LIMIT = 56 * 1024 * 1024
NEAR = (0, 1, 2, 4)
FAR = (3, 5, 6, 7)


def contact_values(coords, frame_scale, pairs):
    frames_dev = coords.shape[0]
    residues = coords.shape[2]
    flat = coords.astype(jnp.float32).reshape(frames_dev * 3, residues)
    rows_iota = jnp.arange(residues, dtype=jnp.int32)[:, None]
    selector = (rows_iota == pairs[0][None, :]).astype(jnp.float32) - (
        rows_iota == pairs[1][None, :]
    ).astype(jnp.float32)
    diff = jnp.dot(
        flat, selector, precision=lax.Precision.HIGHEST, preferred_element_type=jnp.float32
    )
    diff = diff.reshape(frames_dev, 3, pairs.shape[1])
    squares = diff[:, 0] * diff[:, 0] + diff[:, 1] * diff[:, 1] + diff[:, 2] * diff[:, 2]
    dist_sq = (frame_scale * frame_scale)[:, None] * squares
    return 1.0 / (1.0 + dist_sq * dist_sq * dist_sq)


def walker_mask(walker_lengths, count, frames_all):
    ends = jnp.cumsum(walker_lengths)
    times = jnp.arange(count, dtype=jnp.int32)
    later = times + LAG
    own = jnp.sum((times[:, None] >= ends[None, :]).astype(jnp.int32), axis=1)
    ahead = jnp.sum((later[:, None] >= ends[None, :]).astype(jnp.int32), axis=1)
    return (own == ahead) & (later < frames_all)


def estimate(micros):
    return pl.CostEstimate(
        flops=int(micros * 1_000_000_000), bytes_accessed=int(micros * 3_690_000), transcendentals=0
    )


def contract(left, right):
    return lax.dot_general(
        left, right, (((0,), (0,)), ((), ())), preferred_element_type=jnp.float32
    )


def plain_shards(coords, frame_scale, pairs, walker_lengths):
    tm_count = lax.axis_size("tm")
    frames_dev = coords.shape[0]
    local_feats = pairs.shape[1]
    frames_all = frames_dev * tm_count
    contact = contact_values(coords, frame_scale, pairs)
    totals = lax.psum(jnp.sum(contact, axis=0), "tm")
    centered = (contact - totals / jnp.float32(frames_all)).astype(jnp.bfloat16)
    npairs = jnp.sum(jnp.maximum(walker_lengths - LAG, 0)).astype(jnp.float32)
    column_series = lax.all_gather(centered, "tm", axis=0, tiled=True)
    wide = lax.all_gather(centered, "feat", axis=1, tiled=True)
    row_series = lax.all_to_all(wide, "tm", split_axis=1, concat_axis=0, tiled=True)
    valid = walker_mask(walker_lengths, frames_all, frames_all)
    later = jnp.concatenate(
        [column_series[LAG:], jnp.zeros((LAG, local_feats), jnp.bfloat16)], axis=0
    )
    lagged = jnp.where(valid[:, None], later, jnp.zeros_like(later))
    same = contract(row_series, column_series)
    cross = contract(row_series, lagged)
    return (same / jnp.float32(frames_all), cross / npairs)


def switch(squares, scale):
    dist_sq = (scale * scale) * squares
    return 1.0 / (1.0 + dist_sq * dist_sq * dist_sq)


def as_column(row):
    return jnp.broadcast_to(row, (CHUNK, row.shape[1])).T


def gather_kernel(form, chunks, count, pairs_ref, scale_ref, *rest):
    sources, rest = rest[:count], rest[count:]
    if form == "first":
        out_ref, sums_ref, table_out, table, dense, part, held, arrived, left = rest
    elif form == "own":
        mean_ref, out_ref, table, dense, part, arrived = rest
    else:
        mean_ref, out_ref, table, dense, part, held, arrived = rest
    block = part.shape[0]
    stride = -(-3 * chunks // 8) * 8
    residues = table.shape[0] // stride
    group = dense.shape[0] // chunks
    step = pl.program_id(0)

    @pl.when(step == 0)
    def _():
        if form == "own":
            copy = pltpu.make_async_copy(sources[0], table, arrived)
            copy.start()
            copy.wait()
            return
        copies = [
            pltpu.make_async_copy(ref.at[k], held.at[n, k], arrived.at[n, k])
            for k in range(3)
            for n, ref in enumerate(sources)
        ]
        for copy in copies:
            copy.start()
        for k in range(3):
            for n in range(count):
                copies[k * count + n].wait()
            for c in range(chunks):
                if form == "first":
                    plane = held[0, k, :, c * CHUNK : (c + 1) * CHUNK]
                else:
                    plane = held[c, k].astype(jnp.int32)
                table[pl.ds(k * chunks + c, residues, stride=stride), :] = plane
        if form == "first":
            pltpu.make_async_copy(table, table_out, left).start()

    if form != "first":
        part[...] = as_column(mean_ref[...])
    sublane = lax.broadcasted_iota(jnp.int32, (8, CHUNK), 0)
    scale = jnp.concatenate([scale_ref[...]] * (8 // chunks), axis=0)

    def squares(f):
        first = pl.multiple_of(pairs_ref[0, f], 8)
        second = pl.multiple_of(pairs_ref[1, f], 8)
        diff = (table[pl.ds(first, stride), :] - table[pl.ds(second, stride), :]).astype(jnp.float32)
        diff = diff * diff
        total = diff[0:8] + jnp.where(sublane < 4, diff[8:16], 0.0)
        return total + pltpu.roll(total, 4, 0)

    @pl.loop(0, block // group)
    def _(g):
        at = pl.multiple_of(g * group, group)
        for f in range(0, group, 2):
            base = step * block + at + f
            value = jnp.where(sublane < 4, squares(base), squares(base + 1))
            dense[pl.ds(f * chunks, 8), :] = switch(value, scale)
        for h in range(group // 16):
            here = pl.ds(pl.multiple_of(at + h * 16, 16), 16)
            total = jnp.zeros((16, CHUNK), jnp.float32)
            for c in range(chunks):
                contact = dense[pl.ds(h * 16 * chunks + c, 16, stride=chunks), :]
                lanes = slice(c * CHUNK, (c + 1) * CHUNK)
                if form == "first":
                    out_ref[here, lanes] = contact
                    total = total + contact
                elif form == "own":
                    out_ref[here, lanes] = (contact - part[here, :]).astype(jnp.bfloat16)
                else:
                    out_ref[c, here, :] = (contact - part[here, :]).astype(jnp.bfloat16)
            if form == "first":
                part[here, :] = total

    if form == "first":
        sums_ref[...] = jnp.sum(part[...].T, axis=0, keepdims=True)

        @pl.when(step == pl.num_programs(0) - 1)
        def _():
            pltpu.make_async_copy(table, table_out, left).wait()


def contacts(form, pairs, sources, scale, mean=None, block=512, group=32):
    feats = pairs.shape[1]
    chunks = scale.shape[0]
    stride = -(-3 * chunks // 8) * 8
    rows = sources[0].shape[0] if form == "own" else sources[0].shape[1] * stride
    row_spec = pl.BlockSpec((1, block), lambda n: (0, n))
    any_spec = pl.BlockSpec(memory_space=pl.ANY)
    in_specs = [pl.BlockSpec(memory_space=pltpu.SMEM), pl.BlockSpec((chunks, CHUNK), lambda n: (0, 0))]
    in_specs += [any_spec] * len(sources)
    args = [pairs * stride, scale, *sources]
    scratch = [
        pltpu.VMEM((rows, CHUNK), jnp.int32),
        pltpu.VMEM((group * chunks, CHUNK), jnp.float32),
        pltpu.VMEM((block, CHUNK), jnp.float32),
    ]
    if form == "sent":
        out_shape = jax.ShapeDtypeStruct((chunks, feats, CHUNK), jnp.bfloat16)
        out_specs = pl.BlockSpec((chunks, block, CHUNK), lambda n: (0, n, 0))
    else:
        dtype = jnp.bfloat16 if form == "own" else jnp.float32
        out_shape = jax.ShapeDtypeStruct((feats, chunks * CHUNK), dtype)
        out_specs = pl.BlockSpec((block, chunks * CHUNK), lambda n: (n, 0))
    if form == "own":
        scratch.append(pltpu.SemaphoreType.DMA)
    else:
        scratch.append(pltpu.VMEM((len(sources),) + sources[0].shape, sources[0].dtype))
        scratch.append(pltpu.SemaphoreType.DMA((len(sources), 3)))
    if form == "first":
        out_shape = [
            out_shape,
            jax.ShapeDtypeStruct((1, feats), jnp.float32),
            jax.ShapeDtypeStruct((rows, CHUNK), jnp.int32),
        ]
        out_specs = [out_specs, row_spec, any_spec]
        scratch.append(pltpu.SemaphoreType.DMA)
    else:
        in_specs.append(row_spec)
        args.append(mean)
    return pl.pallas_call(
        functools.partial(gather_kernel, form, chunks, len(sources)),
        out_shape=out_shape,
        grid=(feats // block,),
        in_specs=in_specs,
        out_specs=out_specs,
        scratch_shapes=scratch,
        compiler_params=pltpu.CompilerParams(vmem_limit_bytes=VMEM_LIMIT),
        cost_estimate=estimate(1),
    )(*args)


def center_kernel(raw_ref, mean_ref, out_ref):
    for c in range(raw_ref.shape[1] // CHUNK):
        frames = slice(c * CHUNK, (c + 1) * CHUNK)
        out_ref[frames, :] = (raw_ref[:, frames].T - mean_ref[...]).astype(jnp.bfloat16)


def center(raw, mean, block=512):
    feats, frames = raw.shape
    return pl.pallas_call(
        center_kernel,
        out_shape=jax.ShapeDtypeStruct((frames, feats), jnp.bfloat16),
        grid=(feats // block,),
        in_specs=[
            pl.BlockSpec((block, frames), lambda n: (n, 0)),
            pl.BlockSpec((1, block), lambda n: (0, n)),
        ],
        out_specs=pl.BlockSpec((frames, block), lambda n: (0, n)),
        compiler_params=pltpu.CompilerParams(vmem_limit_bytes=VMEM_LIMIT),
        cost_estimate=estimate(1),
    )(raw, mean)


def product_kernel(place_ref, mask_ref, factors_ref, *rest):
    near_refs, rest = rest[: len(NEAR)], rest[len(NEAR) :]
    far_refs, rest = rest[:7], rest[7:]
    cols_refs, rest = rest[:8], rest[8:]
    same_ref, cross_ref, left = rest[-3:]
    feats = same_ref.shape[0]
    frames = cols_refs[0].shape[0]
    parts = frames // CHUNK
    me, z = place_ref[0], place_ref[1]

    def put(d, c, value):
        j = me ^ d
        after = me ^ lax.rem(j + 1, 8)
        mask = mask_ref[j, c].astype(jnp.bfloat16)
        at = pl.multiple_of(d * frames + c * CHUNK, CHUNK)
        left[0:feats, pl.ds(at, CHUNK)] = value
        to = c + LAG // CHUNK
        at = jnp.where(to < parts, d * frames + to * CHUNK, after * frames + (to - parts) * CHUNK)
        left[feats : 2 * feats, pl.ds(pl.multiple_of(at, CHUNK), CHUNK)] = value * mask

    @pl.when(pl.program_id(0) == 0)
    def _():
        for d, ref in zip(NEAR, near_refs):
            for c in range(parts):
                put(d, c, ref[:, c * CHUNK : (c + 1) * CHUNK])
        for n, ref in enumerate(far_refs):
            hop = (n + 1) // 2
            c = z - hop if n % 2 else z + hop

            @pl.when((c >= 0) & (c < parts))
            def _():
                for i, d in enumerate(FAR):
                    put(d, c, ref[i])

    right = jnp.concatenate([ref[...] for ref in cols_refs], axis=0)
    both = jnp.dot(left[...], right, preferred_element_type=jnp.float32)
    same_ref[...] = both[0:feats] * factors_ref[0]
    cross_ref[...] = both[feats : 2 * feats] / factors_ref[1]


def products(place, mask, factors, near, far, cols, block=256):
    frames, feats = cols[0][0].shape
    rows = near[0].shape[0]
    out = jax.ShapeDtypeStruct((rows, feats), jnp.float32)
    whole = lambda x: pl.BlockSpec(x.shape, lambda n, s: (0,) * x.ndim, pipeline_mode=pl.Buffered(1))
    inputs = [mask, factors, *near, *far, *[x for x, _ in cols]]
    return pl.pallas_call(
        product_kernel,
        out_shape=[out, out],
        grid_spec=pltpu.PrefetchScalarGridSpec(
            num_scalar_prefetch=1,
            grid=(feats // block,),
            in_specs=[whole(mask), pl.BlockSpec(memory_space=pltpu.SMEM)]
            + [whole(x) for x in (*near, *far)]
            + [pl.BlockSpec((frames, block), lambda n, s, i=i: (i, n)) for _, i in cols],
            out_specs=[pl.BlockSpec((rows, block), lambda n, s: (0, n))] * 2,
            scratch_shapes=[pltpu.VMEM((2 * rows, 8 * frames), jnp.bfloat16)],
        ),
        compiler_params=pltpu.CompilerParams(vmem_limit_bytes=VMEM_LIMIT),
        cost_estimate=estimate(24),
    )(place, *inputs)


def swap(x, bits):
    return lax.ppermute(x, "tm", [(i, i ^ bits) for i in range(8)])


def corner(along_x, along_y):
    over_y = lax.ppermute(along_x, "tm", [(i, i ^ 4) for i in range(0, 8, 2)])
    over_x = lax.ppermute(along_y, "tm", [(i, i ^ 2) for i in range(1, 8, 2)])
    return over_y, over_x


def line_gather(x, count):
    shift = lambda s: [(i, (i + s) % count) for i in range(count)]
    return jnp.stack([x] + [lax.ppermute(x, "feat", shift(s)) for s in range(1, count)])


def line_hop(up, down, hop, count):
    up = lax.ppermute(up, "feat", [(i, i + 1) for i in range(hop - 1, count - 1)])
    down = lax.ppermute(down, "feat", [(i + 1, i) for i in range(count - hop)])
    return up, down


def together(*values):
    return lax.optimization_barrier(values)


def shards(coords, frame_scale, pairs, walker_lengths):
    tm_count = lax.axis_size("tm")
    feat_count = lax.axis_size("feat")
    frames_dev = coords.shape[0]
    feats = pairs.shape[1]
    frames_all = frames_dev * tm_count
    row_feats = feats * feat_count // tm_count
    parts = frames_dev // CHUNK
    tm = lax.axis_index("tm").astype(jnp.int32)
    z = lax.axis_index("feat").astype(jnp.int32)
    place = jnp.stack([tm, z])
    own_half = (tm % (feats // row_feats)) * row_feats

    coords_t = jnp.transpose(coords, (1, 2, 0))
    scale_own = frame_scale.reshape(parts, CHUNK)
    quarter = lax.dynamic_slice_in_dim(coords_t, z * CHUNK, CHUNK, axis=2).astype(jnp.int16)
    quarters = {3: swap(quarter, 3), 5: swap(quarter, 5)}

    raw, sums, table = contacts("first", pairs, [coords_t], scale_own)
    raw, sums, quarters = together(raw, sums, quarters)
    across = corner(quarters[3], quarters[5])
    note = jnp.concatenate([sums, frame_scale.reshape(1, frames_dev)], axis=1)
    notes = [note] + [swap(note, d) for d in range(1, 8)]

    totals = notes[0][:, :feats]
    for other in notes[1:]:
        totals = totals + other[:, :feats]
    mean = totals / jnp.float32(frames_all)
    scales = [lax.dynamic_slice_in_dim(n, feats + z * CHUNK, CHUNK, axis=1) for n in notes]
    scale_of = lambda *d: jnp.concatenate([scales[i] for i in d], axis=0)

    facts = line_gather(jnp.concatenate([mean, pairs.astype(jnp.float32)], axis=0), feat_count)
    mine, facts, across = together(center(raw, mean), facts, across)
    quarters[7] = across[0] + across[1]
    cols = {0: mine, 2: swap(mine, 2), 4: swap(mine, 4)}
    quarters[6] = swap(quarters[7], 1)

    def facts_of(i, start, count):
        back = (z - i * feat_count // tm_count) % feat_count
        return lax.dynamic_slice(facts, (back, 0, start), (1, 3, count))[0]

    row_facts = facts_of(tm, own_half, row_feats)
    out_facts = jnp.concatenate(
        [facts_of(tm ^ 2, own_half, row_feats), facts_of(tm ^ 4, own_half, row_feats), facts_of(tm, 0, feats)],
        axis=1,
    )
    row_facts, out_facts, scales = together(row_facts, out_facts, scales)
    row_mean, row_pairs = row_facts[0:1], row_facts[1:3].astype(jnp.int32)
    out_mean, out_pairs = out_facts[0:1], out_facts[1:3].astype(jnp.int32)

    row_pairs, mine, quarters = together(row_pairs, mine, quarters)
    cols[1] = swap(mine, 1)
    mixed = contacts("sent", row_pairs, [quarters[d] for d in FAR], scale_of(*FAR), row_mean)

    out_pairs, mixed, walker_lengths = together(out_pairs, mixed, walker_lengths)
    up, down = line_hop(mixed, mixed, 1, feat_count)
    valid = walker_mask(walker_lengths, frames_all, frames_all)
    mask = valid.astype(jnp.float32).reshape(tm_count, parts, 1, CHUNK)
    npairs = jnp.sum(jnp.maximum(walker_lengths - LAG, 0)).astype(jnp.float32)
    factors = jnp.stack([jnp.float32(1.0 / frames_all), npairs])
    near_rows = contacts("own", out_pairs[:, :feats], [table], scale_own, out_mean[:, :feats])
    near_rows, mask, factors, up, down, cols = together(near_rows, mask, factors, up, down, cols)
    far = [mixed, up, down]

    up, down = line_hop(up, down, 2, feat_count)
    across = corner(cols[2], cols[4])
    side_cols = jnp.concatenate([cols[2], cols[4]], axis=0)
    their_side_cols = swap(side_cols, 1)
    chip_pairs, side_cols = together(out_pairs[:, feats:], side_cols)
    chip_rows = contacts("own", chip_pairs, [table], scale_own, out_mean[:, feats:])
    chip_rows, across, up, down, their_side_cols = together(chip_rows, across, up, down, their_side_cols)

    far += [up, down, *line_hop(up, down, 3, feat_count)]
    far_cols = across[0] + across[1]
    their_far_cols = swap(far_cols, 1)
    near_rows, far_cols = together(near_rows, far_cols)
    cut = lambda x, start: lax.dynamic_slice_in_dim(x, start, row_feats, axis=0)
    own = cut(chip_rows, own_half)
    partner = swap(cut(chip_rows, row_feats - own_half), 1)
    near = [own, partner, swap(near_rows[:row_feats], 2), swap(near_rows[row_feats:], 4)]
    cols = [(cols[0], 0), (cols[1], 0)]
    cols += [(side_cols, 0), (their_side_cols, 0), (side_cols, 1), (their_side_cols, 1)]
    cols += [(far_cols, 0), (their_far_cols, 0)]
    return products(place, mask, factors, near, far, cols)


def solution(mesh):
    def run(coords, frame_scale, pairs, walker_lengths):
        tm_count, feat_count = mesh.shape["tm"], mesh.shape["feat"]
        frames_dev = coords.shape[0] // tm_count
        square = tm_count == 8 and feat_count == 4
        fits = square and frames_dev == 4 * CHUNK and pairs.shape[1] == 16 * 512
        return jax.shard_map(
            shards if fits else plain_shards,
            mesh=mesh,
            in_specs=(P("tm", None, None), P("tm"), P(None, "feat"), P()),
            out_specs=(P("tm", "feat"), P("tm", "feat")),
            check_vma=False,
        )(coords, frame_scale, pairs, walker_lengths)

    return run
```

```python
import functools

import jax
import jax.numpy as jnp
from jax import lax
from jax.experimental import pallas as pl
from jax.experimental.pallas import tpu as pltpu
from jax.sharding import PartitionSpec as P

LAG = 384
CHUNK = 128
VMEM_LIMIT = 56 * 1024 * 1024
NEAR = (0, 1, 2, 4)
FAR = (3, 5, 6, 7)


def contact_values(coords, frame_scale, pairs):
    frames_dev = coords.shape[0]
    residues = coords.shape[2]
    flat = coords.astype(jnp.float32).reshape(frames_dev * 3, residues)
    rows_iota = jnp.arange(residues, dtype=jnp.int32)[:, None]
    selector = (rows_iota == pairs[0][None, :]).astype(jnp.float32) - (
        rows_iota == pairs[1][None, :]
    ).astype(jnp.float32)
    diff = jnp.dot(
        flat, selector, precision=lax.Precision.HIGHEST, preferred_element_type=jnp.float32
    )
    diff = diff.reshape(frames_dev, 3, pairs.shape[1])
    squares = diff[:, 0] * diff[:, 0] + diff[:, 1] * diff[:, 1] + diff[:, 2] * diff[:, 2]
    dist_sq = (frame_scale * frame_scale)[:, None] * squares
    return 1.0 / (1.0 + dist_sq * dist_sq * dist_sq)


def walker_mask(walker_lengths, count, frames_all):
    ends = jnp.cumsum(walker_lengths)
    times = jnp.arange(count, dtype=jnp.int32)
    later = times + LAG
    own = jnp.sum((times[:, None] >= ends[None, :]).astype(jnp.int32), axis=1)
    ahead = jnp.sum((later[:, None] >= ends[None, :]).astype(jnp.int32), axis=1)
    return (own == ahead) & (later < frames_all)


def estimate(micros):
    return pl.CostEstimate(
        flops=int(micros * 1_000_000_000), bytes_accessed=int(micros * 3_690_000), transcendentals=0
    )


def contract(left, right):
    return lax.dot_general(
        left, right, (((0,), (0,)), ((), ())), preferred_element_type=jnp.float32
    )


def plain_shards(coords, frame_scale, pairs, walker_lengths):
    tm_count = lax.axis_size("tm")
    frames_dev = coords.shape[0]
    local_feats = pairs.shape[1]
    frames_all = frames_dev * tm_count
    contact = contact_values(coords, frame_scale, pairs)
    totals = lax.psum(jnp.sum(contact, axis=0), "tm")
    centered = (contact - totals / jnp.float32(frames_all)).astype(jnp.bfloat16)
    npairs = jnp.sum(jnp.maximum(walker_lengths - LAG, 0)).astype(jnp.float32)
    column_series = lax.all_gather(centered, "tm", axis=0, tiled=True)
    wide = lax.all_gather(centered, "feat", axis=1, tiled=True)
    row_series = lax.all_to_all(wide, "tm", split_axis=1, concat_axis=0, tiled=True)
    valid = walker_mask(walker_lengths, frames_all, frames_all)
    later = jnp.concatenate(
        [column_series[LAG:], jnp.zeros((LAG, local_feats), jnp.bfloat16)], axis=0
    )
    lagged = jnp.where(valid[:, None], later, jnp.zeros_like(later))
    same = contract(row_series, column_series)
    cross = contract(row_series, lagged)
    return (same / jnp.float32(frames_all), cross / npairs)


def switch(squares, scale):
    dist_sq = (scale * scale) * squares
    return 1.0 / (1.0 + dist_sq * dist_sq * dist_sq)


def as_column(row):
    return jnp.broadcast_to(row, (CHUNK, row.shape[1])).T


def gather_kernel(form, chunks, count, pairs_ref, scale_ref, *rest):
    sources, rest = rest[:count], rest[count:]
    if form == "first":
        out_ref, sums_ref, table_out, table, dense, part, held, arrived, left = rest
    elif form == "own":
        mean_ref, out_ref, table, dense, part, arrived = rest
    else:
        mean_ref, out_ref, table, dense, part, held, arrived = rest
    block = part.shape[0]
    stride = -(-3 * chunks // 8) * 8
    residues = table.shape[0] // stride
    group = dense.shape[0] // chunks
    step = pl.program_id(0)

    @pl.when(step == 0)
    def _():
        if form == "own":
            copy = pltpu.make_async_copy(sources[0], table, arrived)
            copy.start()
            copy.wait()
            return
        copies = [
            pltpu.make_async_copy(ref.at[k], held.at[n, k], arrived.at[n, k])
            for k in range(3)
            for n, ref in enumerate(sources)
        ]
        for copy in copies:
            copy.start()
        for k in range(3):
            for n in range(count):
                copies[k * count + n].wait()
            for c in range(chunks):
                if form == "first":
                    plane = held[0, k, :, c * CHUNK : (c + 1) * CHUNK]
                else:
                    plane = held[c, k].astype(jnp.int32)
                table[pl.ds(k * chunks + c, residues, stride=stride), :] = plane
        if form == "first":
            pltpu.make_async_copy(table, table_out, left).start()

    if form != "first":
        part[...] = as_column(mean_ref[...])
    sublane = lax.broadcasted_iota(jnp.int32, (8, CHUNK), 0)
    scale = jnp.concatenate([scale_ref[...]] * (8 // chunks), axis=0)

    def squares(f):
        first = pl.multiple_of(pairs_ref[0, f], 8)
        second = pl.multiple_of(pairs_ref[1, f], 8)
        diff = (table[pl.ds(first, stride), :] - table[pl.ds(second, stride), :]).astype(jnp.float32)
        diff = diff * diff
        total = diff[0:8] + jnp.where(sublane < 4, diff[8:16], 0.0)
        return total + pltpu.roll(total, 4, 0)

    @pl.loop(0, block // group)
    def _(g):
        at = pl.multiple_of(g * group, group)
        for f in range(0, group, 2):
            base = step * block + at + f
            value = jnp.where(sublane < 4, squares(base), squares(base + 1))
            dense[pl.ds(f * chunks, 8), :] = switch(value, scale)
        for h in range(group // 16):
            here = pl.ds(pl.multiple_of(at + h * 16, 16), 16)
            total = jnp.zeros((16, CHUNK), jnp.float32)
            for c in range(chunks):
                contact = dense[pl.ds(h * 16 * chunks + c, 16, stride=chunks), :]
                lanes = slice(c * CHUNK, (c + 1) * CHUNK)
                if form == "first":
                    out_ref[here, lanes] = contact
                    total = total + contact
                elif form == "own":
                    out_ref[here, lanes] = (contact - part[here, :]).astype(jnp.bfloat16)
                else:
                    out_ref[c, here, :] = (contact - part[here, :]).astype(jnp.bfloat16)
            if form == "first":
                part[here, :] = total

    if form == "first":
        sums_ref[...] = jnp.sum(part[...].T, axis=0, keepdims=True)

        @pl.when(step == pl.num_programs(0) - 1)
        def _():
            pltpu.make_async_copy(table, table_out, left).wait()


def contacts(form, pairs, sources, scale, mean=None, block=512, group=32):
    feats = pairs.shape[1]
    chunks = scale.shape[0]
    stride = -(-3 * chunks // 8) * 8
    rows = sources[0].shape[0] if form == "own" else sources[0].shape[1] * stride
    row_spec = pl.BlockSpec((1, block), lambda n: (0, n))
    any_spec = pl.BlockSpec(memory_space=pl.ANY)
    in_specs = [pl.BlockSpec(memory_space=pltpu.SMEM), pl.BlockSpec((chunks, CHUNK), lambda n: (0, 0))]
    in_specs += [any_spec] * len(sources)
    args = [pairs * stride, scale, *sources]
    scratch = [
        pltpu.VMEM((rows, CHUNK), jnp.int32),
        pltpu.VMEM((group * chunks, CHUNK), jnp.float32),
        pltpu.VMEM((block, CHUNK), jnp.float32),
    ]
    if form == "sent":
        out_shape = jax.ShapeDtypeStruct((chunks, feats, CHUNK), jnp.bfloat16)
        out_specs = pl.BlockSpec((chunks, block, CHUNK), lambda n: (0, n, 0))
    else:
        dtype = jnp.bfloat16 if form == "own" else jnp.float32
        out_shape = jax.ShapeDtypeStruct((feats, chunks * CHUNK), dtype)
        out_specs = pl.BlockSpec((block, chunks * CHUNK), lambda n: (n, 0))
    if form == "own":
        scratch.append(pltpu.SemaphoreType.DMA)
    else:
        scratch.append(pltpu.VMEM((len(sources),) + sources[0].shape, sources[0].dtype))
        scratch.append(pltpu.SemaphoreType.DMA((len(sources), 3)))
    if form == "first":
        out_shape = [
            out_shape,
            jax.ShapeDtypeStruct((1, feats), jnp.float32),
            jax.ShapeDtypeStruct((rows, CHUNK), jnp.int32),
        ]
        out_specs = [out_specs, row_spec, any_spec]
        scratch.append(pltpu.SemaphoreType.DMA)
    else:
        in_specs.append(row_spec)
        args.append(mean)
    return pl.pallas_call(
        functools.partial(gather_kernel, form, chunks, len(sources)),
        out_shape=out_shape,
        grid=(feats // block,),
        in_specs=in_specs,
        out_specs=out_specs,
        scratch_shapes=scratch,
        compiler_params=pltpu.CompilerParams(vmem_limit_bytes=VMEM_LIMIT),
        cost_estimate=estimate(1),
    )(*args)


def center_kernel(raw_ref, mean_ref, out_ref):
    for c in range(raw_ref.shape[1] // CHUNK):
        frames = slice(c * CHUNK, (c + 1) * CHUNK)
        out_ref[frames, :] = (raw_ref[:, frames].T - mean_ref[...]).astype(jnp.bfloat16)


def center(raw, mean, block=512):
    feats, frames = raw.shape
    return pl.pallas_call(
        center_kernel,
        out_shape=jax.ShapeDtypeStruct((frames, feats), jnp.bfloat16),
        grid=(feats // block,),
        in_specs=[
            pl.BlockSpec((block, frames), lambda n: (n, 0)),
            pl.BlockSpec((1, block), lambda n: (0, n)),
        ],
        out_specs=pl.BlockSpec((frames, block), lambda n: (0, n)),
        compiler_params=pltpu.CompilerParams(vmem_limit_bytes=VMEM_LIMIT),
        cost_estimate=estimate(1),
    )(raw, mean)


def product_kernel(place_ref, mask_ref, factors_ref, *rest):
    near_refs, rest = rest[: len(NEAR)], rest[len(NEAR) :]
    far_refs, rest = rest[:7], rest[7:]
    cols_refs, rest = rest[:8], rest[8:]
    same_ref, cross_ref, left, near_held, far_held, arrived = rest
    feats = same_ref.shape[0]
    frames = cols_refs[0].shape[0]
    parts = frames // CHUNK
    me, z = place_ref[0], place_ref[1]

    def put(d, c, value):
        j = me ^ d
        after = me ^ lax.rem(j + 1, 8)
        mask = mask_ref[j, c].astype(jnp.bfloat16)
        at = pl.multiple_of(d * frames + c * CHUNK, CHUNK)
        left[0:feats, pl.ds(at, CHUNK)] = value
        to = c + LAG // CHUNK
        at = jnp.where(to < parts, d * frames + to * CHUNK, after * frames + (to - parts) * CHUNK)
        left[feats : 2 * feats, pl.ds(pl.multiple_of(at, CHUNK), CHUNK)] = value * mask

    @pl.when(pl.program_id(0) == 0)
    def _():
        copies = [
            pltpu.make_async_copy(ref, near_held.at[n], arrived.at[n]) for n, ref in enumerate(near_refs)
        ]
        copies += [
            pltpu.make_async_copy(ref, far_held.at[n], arrived.at[len(NEAR) + n])
            for n, ref in enumerate(far_refs)
        ]
        for copy in copies:
            copy.start()
        for n, d in enumerate(NEAR):
            copies[n].wait()
            for c in range(parts):
                put(d, c, near_held[n, :, c * CHUNK : (c + 1) * CHUNK])
        for n in range(len(far_refs)):
            copies[len(NEAR) + n].wait()
            hop = (n + 1) // 2
            c = z - hop if n % 2 else z + hop

            @pl.when((c >= 0) & (c < parts))
            def _():
                for i, d in enumerate(FAR):
                    put(d, c, far_held[n, i])

    right = jnp.concatenate([ref[...] for ref in cols_refs], axis=0)
    for m in range(0, feats, 512):
        here = slice(m, m + 512)
        same = jnp.dot(left[here, :], right, preferred_element_type=jnp.float32)
        same_ref[here, :] = same * factors_ref[0]
    for m in range(0, feats, 512):
        here = slice(m, m + 512)
        cross = jnp.dot(left[feats + m : feats + m + 512, :], right, preferred_element_type=jnp.float32)
        cross_ref[here, :] = cross / factors_ref[1]


def products(place, mask, factors, near, far, cols, block=256):
    frames, feats = cols[0].shape
    rows = near[0].shape[0]
    out = jax.ShapeDtypeStruct((rows, feats), jnp.float32)
    inputs = [mask, factors, *near, *far, *cols]
    return pl.pallas_call(
        product_kernel,
        out_shape=[out, out],
        grid_spec=pltpu.PrefetchScalarGridSpec(
            num_scalar_prefetch=1,
            grid=(feats // block,),
            in_specs=[
                pl.BlockSpec(mask.shape, lambda n, s: (0,) * mask.ndim),
                pl.BlockSpec(memory_space=pltpu.SMEM),
            ]
            + [pl.BlockSpec(memory_space=pl.ANY)] * (len(near) + len(far))
            + [pl.BlockSpec((frames, block), lambda n, s: (0, n))] * 8,
            out_specs=[pl.BlockSpec((rows, block), lambda n, s: (0, n))] * 2,
            scratch_shapes=[
                pltpu.VMEM((2 * rows, 8 * frames), jnp.bfloat16),
                pltpu.VMEM((len(near),) + near[0].shape, jnp.bfloat16),
                pltpu.VMEM((len(far),) + far[0].shape, jnp.bfloat16),
                pltpu.SemaphoreType.DMA((len(near) + len(far),)),
            ],
        ),
        compiler_params=pltpu.CompilerParams(vmem_limit_bytes=VMEM_LIMIT),
        cost_estimate=estimate(24),
    )(place, *inputs)


def swap(x, bits):
    return lax.ppermute(x, "tm", [(i, i ^ bits) for i in range(8)])


def corner(along_x, along_y):
    even = lax.axis_index("tm") % 2 == 0
    forwarded = jnp.where(even, along_x, along_y)
    return lax.ppermute(forwarded, "tm", [(i, i ^ (2 if i % 2 else 4)) for i in range(8)])


def line_gather(x, count):
    shift = lambda s: [(i, (i + s) % count) for i in range(count)]
    return jnp.stack([x] + [lax.ppermute(x, "feat", shift(s)) for s in range(1, count)])


def line_hop(up, down, hop, count):
    up = lax.ppermute(up, "feat", [(i, i + 1) for i in range(hop - 1, count - 1)])
    down = lax.ppermute(down, "feat", [(i + 1, i) for i in range(count - hop)])
    return up, down


def together(*values):
    return lax.optimization_barrier(values)


def shards(coords, frame_scale, pairs, walker_lengths):
    tm_count = lax.axis_size("tm")
    feat_count = lax.axis_size("feat")
    frames_dev = coords.shape[0]
    feats = pairs.shape[1]
    frames_all = frames_dev * tm_count
    row_feats = feats * feat_count // tm_count
    parts = frames_dev // CHUNK
    tm = lax.axis_index("tm").astype(jnp.int32)
    z = lax.axis_index("feat").astype(jnp.int32)
    place = jnp.stack([tm, z])
    own_half = (tm % (feats // row_feats)) * row_feats

    coords_t = jnp.transpose(coords, (1, 2, 0))
    scale_own = frame_scale.reshape(parts, CHUNK)
    quarter = lax.dynamic_slice_in_dim(coords_t, z * CHUNK, CHUNK, axis=2).astype(jnp.int16)
    quarters = {3: swap(quarter, 3), 5: swap(quarter, 5)}

    raw, sums, table = contacts("first", pairs, [coords_t], scale_own)
    quarters, _ = together(quarters, sums)
    quarters[7] = corner(quarters[3], quarters[5])
    note = jnp.concatenate([sums, frame_scale.reshape(1, frames_dev)], axis=1)
    notes = [note] + [swap(note, d) for d in range(1, 8)]

    totals = notes[0][:, :feats]
    for other in notes[1:]:
        totals = totals + other[:, :feats]
    mean = totals / jnp.float32(frames_all)
    scales = [lax.dynamic_slice_in_dim(n, feats + z * CHUNK, CHUNK, axis=1) for n in notes]
    scale_of = lambda *d: jnp.concatenate([scales[i] for i in d], axis=0)

    facts = line_gather(jnp.concatenate([mean, pairs.astype(jnp.float32)], axis=0), feat_count)
    mine, facts, quarters = together(center(raw, mean), facts, quarters)
    cols = {0: mine, 2: swap(mine, 2), 4: swap(mine, 4)}
    quarters[6] = swap(quarters[7], 1)

    def facts_of(i, start, count):
        back = (z - i * feat_count // tm_count) % feat_count
        return lax.dynamic_slice(facts, (back, 0, start), (1, 3, count))[0]

    row_facts = facts_of(tm, own_half, row_feats)
    out_facts = jnp.concatenate(
        [facts_of(tm ^ 2, own_half, row_feats), facts_of(tm ^ 4, own_half, row_feats), facts_of(tm, 0, feats)],
        axis=1,
    )
    row_facts, out_facts, scales = together(row_facts, out_facts, scales)
    row_mean, row_pairs = row_facts[0:1], row_facts[1:3].astype(jnp.int32)
    out_mean, out_pairs = out_facts[0:1], out_facts[1:3].astype(jnp.int32)

    row_pairs, mine, quarters = together(row_pairs, mine, quarters)
    cols[1] = swap(mine, 1)
    mixed = contacts("sent", row_pairs, [quarters[d] for d in FAR], scale_of(*FAR), row_mean)

    out_pairs, mixed, walker_lengths = together(out_pairs, mixed, walker_lengths)
    up, down = line_hop(mixed, mixed, 1, feat_count)
    valid = walker_mask(walker_lengths, frames_all, frames_all)
    mask = valid.astype(jnp.float32).reshape(tm_count, parts, 1, CHUNK)
    npairs = jnp.sum(jnp.maximum(walker_lengths - LAG, 0)).astype(jnp.float32)
    factors = jnp.stack([jnp.float32(1.0 / frames_all), npairs])
    chip_rows = contacts("own", out_pairs[:, feats:], [table], scale_own, out_mean[:, feats:])
    chip_rows, mask, factors, up, down = together(chip_rows, mask, factors, up, down)
    far = [mixed, up, down]

    up, down = line_hop(up, down, 2, feat_count)
    cut = lambda x, start: lax.dynamic_slice_in_dim(x, start, row_feats, axis=0)
    own = cut(chip_rows, own_half)
    partner = swap(cut(chip_rows, row_feats - own_half), 1)
    cols, own, partner = together(cols, own, partner)
    cols[6] = corner(cols[2], cols[4])
    for d in (2, 4):
        cols[d + 1] = swap(cols[d], 1)
    near_pairs, _ = together(out_pairs[:, :feats], own)
    near_rows = contacts("own", near_pairs, [table], scale_own, out_mean[:, :feats])
    near_rows, cols, up, down = together(near_rows, cols, up, down)

    far += [up, down, *line_hop(up, down, 3, feat_count)]
    cols[7] = swap(cols[6], 1)
    near = [own, partner, swap(near_rows[:row_feats], 2), swap(near_rows[row_feats:], 4)]
    cols = [cols[d] for d in range(8)]
    return products(place, mask, factors, near, far, cols)


def solution(mesh):
    def run(coords, frame_scale, pairs, walker_lengths):
        tm_count, feat_count = mesh.shape["tm"], mesh.shape["feat"]
        frames_dev = coords.shape[0] // tm_count
        square = tm_count == 8 and feat_count == 4
        fits = square and frames_dev == 4 * CHUNK and pairs.shape[1] == 16 * 512
        return jax.shard_map(
            shards if fits else plain_shards,
            mesh=mesh,
            in_specs=(P("tm", None, None), P("tm"), P(None, "feat"), P()),
            out_specs=(P("tm", "feat"), P("tm", "feat")),
            check_vma=False,
        )(coords, frame_scale, pairs, walker_lengths)

    return run
```

```python
import functools

import jax
import jax.numpy as jnp
from jax import lax
from jax.experimental import pallas as pl
from jax.experimental.pallas import tpu as pltpu
from jax.sharding import PartitionSpec as P

LAG = 384
CHUNK = 128
VMEM_LIMIT = 56 * 1024 * 1024
LATE = (2, 4)
FAR = (3, 5, 6, 7)
EARLY = (0, 1) + FAR


def contact_values(coords, frame_scale, pairs):
    frames_dev = coords.shape[0]
    residues = coords.shape[2]
    flat = coords.astype(jnp.float32).reshape(frames_dev * 3, residues)
    rows_iota = jnp.arange(residues, dtype=jnp.int32)[:, None]
    selector = (rows_iota == pairs[0][None, :]).astype(jnp.float32) - (
        rows_iota == pairs[1][None, :]
    ).astype(jnp.float32)
    diff = jnp.dot(
        flat, selector, precision=lax.Precision.HIGHEST, preferred_element_type=jnp.float32
    )
    diff = diff.reshape(frames_dev, 3, pairs.shape[1])
    squares = diff[:, 0] * diff[:, 0] + diff[:, 1] * diff[:, 1] + diff[:, 2] * diff[:, 2]
    dist_sq = (frame_scale * frame_scale)[:, None] * squares
    return 1.0 / (1.0 + dist_sq * dist_sq * dist_sq)


def walker_mask(walker_lengths, count, frames_all):
    ends = jnp.cumsum(walker_lengths)
    times = jnp.arange(count, dtype=jnp.int32)
    later = times + LAG
    own = jnp.sum((times[:, None] >= ends[None, :]).astype(jnp.int32), axis=1)
    ahead = jnp.sum((later[:, None] >= ends[None, :]).astype(jnp.int32), axis=1)
    return (own == ahead) & (later < frames_all)


def estimate(micros):
    return pl.CostEstimate(
        flops=int(micros * 1_000_000_000), bytes_accessed=int(micros * 3_690_000), transcendentals=0
    )


def contract(left, right):
    return lax.dot_general(
        left, right, (((0,), (0,)), ((), ())), preferred_element_type=jnp.float32
    )


def plain_shards(coords, frame_scale, pairs, walker_lengths):
    tm_count = lax.axis_size("tm")
    frames_dev = coords.shape[0]
    local_feats = pairs.shape[1]
    frames_all = frames_dev * tm_count
    contact = contact_values(coords, frame_scale, pairs)
    totals = lax.psum(jnp.sum(contact, axis=0), "tm")
    centered = (contact - totals / jnp.float32(frames_all)).astype(jnp.bfloat16)
    npairs = jnp.sum(jnp.maximum(walker_lengths - LAG, 0)).astype(jnp.float32)
    column_series = lax.all_gather(centered, "tm", axis=0, tiled=True)
    wide = lax.all_gather(centered, "feat", axis=1, tiled=True)
    row_series = lax.all_to_all(wide, "tm", split_axis=1, concat_axis=0, tiled=True)
    valid = walker_mask(walker_lengths, frames_all, frames_all)
    later = jnp.concatenate(
        [column_series[LAG:], jnp.zeros((LAG, local_feats), jnp.bfloat16)], axis=0
    )
    lagged = jnp.where(valid[:, None], later, jnp.zeros_like(later))
    same = contract(row_series, column_series)
    cross = contract(row_series, lagged)
    return (same / jnp.float32(frames_all), cross / npairs)


def switch(squares, scale):
    dist_sq = (scale * scale) * squares
    return 1.0 / (1.0 + dist_sq * dist_sq * dist_sq)


def as_column(row):
    return jnp.broadcast_to(row, (CHUNK, row.shape[1])).T


def gather_kernel(form, chunks, count, pairs_ref, scale_ref, *rest):
    sources, rest = rest[:count], rest[count:]
    if form == "first":
        out_ref, sums_ref, table_out, table, dense, part, held, arrived, left = rest
    elif form == "own":
        mean_ref, out_ref, table, dense, part, arrived = rest
    else:
        mean_ref, out_ref, table, dense, part, held, arrived = rest
    block = part.shape[0]
    stride = -(-3 * chunks // 8) * 8
    residues = table.shape[0] // stride
    group = dense.shape[0] // chunks
    step = pl.program_id(0)

    @pl.when(step == 0)
    def _():
        if form == "own":
            copy = pltpu.make_async_copy(sources[0], table, arrived)
            copy.start()
            copy.wait()
            return
        copies = [
            pltpu.make_async_copy(ref.at[k], held.at[n, k], arrived.at[n, k])
            for k in range(3)
            for n, ref in enumerate(sources)
        ]
        for copy in copies:
            copy.start()
        for k in range(3):
            for n in range(count):
                copies[k * count + n].wait()
            for c in range(chunks):
                if form == "first":
                    plane = held[0, k, :, c * CHUNK : (c + 1) * CHUNK]
                else:
                    plane = held[c, k].astype(jnp.int32)
                table[pl.ds(k * chunks + c, residues, stride=stride), :] = plane
        if form == "first":
            pltpu.make_async_copy(table, table_out, left).start()

    if form != "first":
        part[...] = as_column(mean_ref[...])
    sublane = lax.broadcasted_iota(jnp.int32, (8, CHUNK), 0)
    scale = jnp.concatenate([scale_ref[...]] * (8 // chunks), axis=0)

    def squares(f):
        first = pl.multiple_of(pairs_ref[0, f], 8)
        second = pl.multiple_of(pairs_ref[1, f], 8)
        diff = (table[pl.ds(first, stride), :] - table[pl.ds(second, stride), :]).astype(jnp.float32)
        diff = diff * diff
        total = diff[0:8] + jnp.where(sublane < 4, diff[8:16], 0.0)
        return total + pltpu.roll(total, 4, 0)

    @pl.loop(0, block // group)
    def _(g):
        at = pl.multiple_of(g * group, group)
        for f in range(0, group, 2):
            base = step * block + at + f
            value = jnp.where(sublane < 4, squares(base), squares(base + 1))
            dense[pl.ds(f * chunks, 8), :] = switch(value, scale)
        for h in range(group // 16):
            here = pl.ds(pl.multiple_of(at + h * 16, 16), 16)
            total = jnp.zeros((16, CHUNK), jnp.float32)
            for c in range(chunks):
                contact = dense[pl.ds(h * 16 * chunks + c, 16, stride=chunks), :]
                lanes = slice(c * CHUNK, (c + 1) * CHUNK)
                if form == "first":
                    out_ref[here, lanes] = contact
                    total = total + contact
                elif form == "own":
                    out_ref[here, lanes] = (contact - part[here, :]).astype(jnp.bfloat16)
                else:
                    out_ref[c, here, :] = (contact - part[here, :]).astype(jnp.bfloat16)
            if form == "first":
                part[here, :] = total

    if form == "first":
        sums_ref[...] = jnp.sum(part[...].T, axis=0, keepdims=True)

        @pl.when(step == pl.num_programs(0) - 1)
        def _():
            pltpu.make_async_copy(table, table_out, left).wait()


def contacts(form, pairs, sources, scale, mean=None, block=512, group=32):
    feats = pairs.shape[1]
    chunks = scale.shape[0]
    stride = -(-3 * chunks // 8) * 8
    rows = sources[0].shape[0] if form == "own" else sources[0].shape[1] * stride
    row_spec = pl.BlockSpec((1, block), lambda n: (0, n))
    any_spec = pl.BlockSpec(memory_space=pl.ANY)
    in_specs = [pl.BlockSpec(memory_space=pltpu.SMEM), pl.BlockSpec((chunks, CHUNK), lambda n: (0, 0))]
    in_specs += [any_spec] * len(sources)
    args = [pairs * stride, scale, *sources]
    scratch = [
        pltpu.VMEM((rows, CHUNK), jnp.int32),
        pltpu.VMEM((group * chunks, CHUNK), jnp.float32),
        pltpu.VMEM((block, CHUNK), jnp.float32),
    ]
    if form == "sent":
        out_shape = jax.ShapeDtypeStruct((chunks, feats, CHUNK), jnp.bfloat16)
        out_specs = pl.BlockSpec((chunks, block, CHUNK), lambda n: (0, n, 0))
    else:
        dtype = jnp.bfloat16 if form == "own" else jnp.float32
        out_shape = jax.ShapeDtypeStruct((feats, chunks * CHUNK), dtype)
        out_specs = pl.BlockSpec((block, chunks * CHUNK), lambda n: (n, 0))
    if form == "own":
        scratch.append(pltpu.SemaphoreType.DMA)
    else:
        scratch.append(pltpu.VMEM((len(sources),) + sources[0].shape, sources[0].dtype))
        scratch.append(pltpu.SemaphoreType.DMA((len(sources), 3)))
    if form == "first":
        out_shape = [
            out_shape,
            jax.ShapeDtypeStruct((1, feats), jnp.float32),
            jax.ShapeDtypeStruct((rows, CHUNK), jnp.int32),
        ]
        out_specs = [out_specs, row_spec, any_spec]
        scratch.append(pltpu.SemaphoreType.DMA)
    else:
        in_specs.append(row_spec)
        args.append(mean)
    return pl.pallas_call(
        functools.partial(gather_kernel, form, chunks, len(sources)),
        out_shape=out_shape,
        grid=(feats // block,),
        in_specs=in_specs,
        out_specs=out_specs,
        scratch_shapes=scratch,
        compiler_params=pltpu.CompilerParams(vmem_limit_bytes=VMEM_LIMIT),
        cost_estimate=estimate(1),
    )(*args)


def center_kernel(raw_ref, mean_ref, out_ref):
    for c in range(raw_ref.shape[1] // CHUNK):
        frames = slice(c * CHUNK, (c + 1) * CHUNK)
        out_ref[frames, :] = (raw_ref[:, frames].T - mean_ref[...]).astype(jnp.bfloat16)


def center(raw, mean, block=512):
    feats, frames = raw.shape
    return pl.pallas_call(
        center_kernel,
        out_shape=jax.ShapeDtypeStruct((frames, feats), jnp.bfloat16),
        grid=(feats // block,),
        in_specs=[
            pl.BlockSpec((block, frames), lambda n: (n, 0)),
            pl.BlockSpec((1, block), lambda n: (0, n)),
        ],
        out_specs=pl.BlockSpec((frames, block), lambda n: (0, n)),
        compiler_params=pltpu.CompilerParams(vmem_limit_bytes=VMEM_LIMIT),
        cost_estimate=estimate(1),
    )(raw, mean)


def fetch(sources, held, arrived):
    copies = [pltpu.make_async_copy(ref, held.at[n], arrived.at[n]) for n, ref in enumerate(sources)]
    for copy in copies:
        copy.start()
    return copies


def multiply(left, right, ahead, rows=512):
    feats = left.shape[1]
    for m in range(0, feats, rows):
        here = slice(m, m + rows)
        same = jnp.dot(left[0, here, :], right, preferred_element_type=jnp.float32)
        cross = jnp.dot(left[1, here, :], ahead, preferred_element_type=jnp.float32)
        yield here, same, cross


def first_product_kernel(place_ref, mask_ref, *rest):
    rows_refs, cols_refs = rest[:7], rest[7:15]
    same_ref, cross_ref, left, right, ahead, near_held, far_held, near_arrived, far_arrived = rest[15:]
    frames = cols_refs[0].shape[0]
    parts = frames // CHUNK
    kept = frames - LAG
    me, z = place_ref[0], place_ref[1]

    def put(d, c, value):
        at = pl.multiple_of(EARLY.index(d) * frames + c * CHUNK, CHUNK)
        left[0, :, pl.ds(at, CHUNK)] = value
        left[1, :, pl.ds(at, CHUNK)] = value * mask_ref[me ^ d, c].astype(jnp.bfloat16)

    @pl.when(pl.program_id(0) == 0)
    def _():
        near = fetch(rows_refs[:2], near_held, near_arrived)
        far = fetch(rows_refs[2:], far_held, far_arrived)
        ahead[...] = jnp.zeros_like(ahead)

        @pl.when((z == 0) | (z == parts - 1))
        def _():
            for d in FAR:
                put(d, parts - 1 - z, jnp.zeros((left.shape[1], CHUNK), jnp.bfloat16))

        for d in range(2):
            near[d].wait()
            for c in range(parts):
                put(d, c, near_held[d, :, c * CHUNK : (c + 1) * CHUNK])
        for n, copy in enumerate(far):
            copy.wait()
            hop = (n + 1) // 2
            c = z - hop if n % 2 else z + hop

            @pl.when((c >= 0) & (c < parts))
            def _():
                for i, d in enumerate(FAR):
                    put(d, c, far_held[n, i])

    for s, d in enumerate(EARLY):
        right[s * frames : (s + 1) * frames, :] = cols_refs[d][...]
        ahead[s * frames : s * frames + kept, :] = cols_refs[d][LAG:, :]
    for d in range(8):
        j = me ^ d
        before = me ^ (j - 1)
        for s, e in enumerate(EARLY):

            @pl.when((j > 0) & (before == e))
            def _():
                ahead[s * frames + kept : (s + 1) * frames, :] = cols_refs[d][:LAG, :]

    for here, same, cross in multiply(left, right[...], ahead[...]):
        same_ref[here, :] = same
        cross_ref[here, :] = cross


def second_product_kernel(place_ref, mask_ref, factors_ref, *rest):
    rows_refs, cols_refs, sums_refs = rest[:4], rest[4:12], rest[12:14]
    same_ref, cross_ref, left, right, ahead, near_held, far_held, near_arrived, far_arrived = rest[14:]
    frames = cols_refs[0].shape[0]
    parts = frames // CHUNK
    kept = frames - LAG
    me, z = place_ref[0], place_ref[1]
    quarter = jnp.where(z == 0, parts - 1, 0)
    base = len(LATE) * frames

    def put(at, d, c, value):
        left[0, :, at : at + CHUNK] = value
        left[1, :, at : at + CHUNK] = value * mask_ref[me ^ d, c].astype(jnp.bfloat16)

    @pl.when(pl.program_id(0) == 0)
    def _():
        near = fetch(rows_refs[:2], near_held, near_arrived)
        far = fetch(rows_refs[2:], far_held, far_arrived)
        ahead[...] = jnp.zeros_like(ahead)
        for s, d in enumerate(LATE):
            near[s].wait()
            for c in range(parts):
                put(s * frames + c * CHUNK, d, c, near_held[s, :, c * CHUNK : (c + 1) * CHUNK])
        for copy in far:
            copy.wait()
        for i, d in enumerate(FAR):
            put(base + i * CHUNK, d, quarter, far_held[0, i] + far_held[1, i])

    for s, d in enumerate(LATE):
        right[s * frames : (s + 1) * frames, :] = cols_refs[d][...]
        ahead[s * frames : s * frames + kept, :] = cols_refs[d][LAG:, :]
    for i, d in enumerate(FAR):
        at = slice(base + i * CHUNK, base + (i + 1) * CHUNK)
        right[at, :] = cols_refs[d][pl.ds(pl.multiple_of(quarter * CHUNK, CHUNK), CHUNK), :]

        @pl.when(quarter == 0)
        def _():
            ahead[at, :] = cols_refs[d][LAG:, :]

    for d in range(8):
        j = me ^ d
        before = me ^ (j - 1)
        for s, e in enumerate(LATE):

            @pl.when((j > 0) & (before == e))
            def _():
                ahead[s * frames + kept : (s + 1) * frames, :] = cols_refs[d][:LAG, :]

        for i, e in enumerate(FAR):

            @pl.when((j > 0) & (before == e) & (quarter > 0))
            def _():
                at = slice(base + i * CHUNK, base + (i + 1) * CHUNK)
                ahead[at, :] = cols_refs[d][LAG - CHUNK : LAG, :]

    for here, same, cross in multiply(left, right[...], ahead[...]):
        same_ref[here, :] = (same + sums_refs[0][here, :]) * factors_ref[0]
        cross_ref[here, :] = (cross + sums_refs[1][here, :]) / factors_ref[1]


def products(place, mask, near, far, cols, factors=None, sums=(), block=256):
    frames, feats = cols[0].shape
    rows = near[0].shape[0]
    depth = len(EARLY if factors is None else LATE) * frames + (0 if factors is None else len(FAR) * CHUNK)
    out = jax.ShapeDtypeStruct((rows, feats), jnp.float32)
    tile = pl.BlockSpec((rows, block), lambda n, s: (0, n))
    any_spec = pl.BlockSpec(memory_space=pl.ANY)
    last = factors is not None
    inputs = [mask] + [factors] * last + [*near, *far, *cols, *sums]
    return pl.pallas_call(
        second_product_kernel if last else first_product_kernel,
        out_shape=[out, out],
        grid_spec=pltpu.PrefetchScalarGridSpec(
            num_scalar_prefetch=1,
            grid=(feats // block,),
            in_specs=[pl.BlockSpec(mask.shape, lambda n, s: (0,) * mask.ndim)]
            + [pl.BlockSpec(memory_space=pltpu.SMEM)] * last
            + [any_spec] * (len(near) + len(far))
            + [pl.BlockSpec((frames, block), lambda n, s: (0, n))] * 8
            + [tile] * len(sums),
            out_specs=[tile] * 2,
            scratch_shapes=[
                pltpu.VMEM((2, rows, depth), jnp.bfloat16),
                pltpu.VMEM((depth, block), jnp.bfloat16),
                pltpu.VMEM((depth, block), jnp.bfloat16),
                pltpu.VMEM((len(near),) + near[0].shape, jnp.bfloat16),
                pltpu.VMEM((len(far),) + far[0].shape, jnp.bfloat16),
                pltpu.SemaphoreType.DMA((len(near),)),
                pltpu.SemaphoreType.DMA((len(far),)),
            ],
        ),
        input_output_aliases={len(inputs) - 1 + i: i for i in range(2)} if sums else {},
        compiler_params=pltpu.CompilerParams(vmem_limit_bytes=VMEM_LIMIT),
        cost_estimate=estimate(24),
    )(place, *inputs)


def swap(x, bits):
    return lax.ppermute(x, "tm", [(i, i ^ bits) for i in range(8)])


def corner(along_x, along_y):
    even = lax.axis_index("tm") % 2 == 0
    forwarded = jnp.where(even, along_x, along_y)
    return lax.ppermute(forwarded, "tm", [(i, i ^ (2 if i % 2 else 4)) for i in range(8)])


def line_gather(x, count):
    shift = lambda s: [(i, (i + s) % count) for i in range(count)]
    return jnp.stack([x] + [lax.ppermute(x, "feat", shift(s)) for s in range(1, count)])


def line_hop(up, down, hop, count):
    up = lax.ppermute(up, "feat", [(i, i + 1) for i in range(hop - 1, count - 1)])
    down = lax.ppermute(down, "feat", [(i + 1, i) for i in range(count - hop)])
    return up, down


def together(*values):
    return lax.optimization_barrier(values)


def shards(coords, frame_scale, pairs, walker_lengths):
    tm_count = lax.axis_size("tm")
    feat_count = lax.axis_size("feat")
    frames_dev = coords.shape[0]
    feats = pairs.shape[1]
    frames_all = frames_dev * tm_count
    row_feats = feats * feat_count // tm_count
    parts = frames_dev // CHUNK
    tm = lax.axis_index("tm").astype(jnp.int32)
    z = lax.axis_index("feat").astype(jnp.int32)
    place = jnp.stack([tm, z])
    own_half = (tm % (feats // row_feats)) * row_feats

    coords_t = jnp.transpose(coords, (1, 2, 0))
    scale_own = frame_scale.reshape(parts, CHUNK)
    quarter = lax.dynamic_slice_in_dim(coords_t, z * CHUNK, CHUNK, axis=2).astype(jnp.int16)
    quarters = {3: swap(quarter, 3), 5: swap(quarter, 5)}

    raw, sums, table = contacts("first", pairs, [coords_t], scale_own)
    quarters, _ = together(quarters, sums)
    quarters[7] = corner(quarters[3], quarters[5])
    note = jnp.concatenate([sums, frame_scale.reshape(1, frames_dev)], axis=1)
    notes = [note] + [swap(note, d) for d in range(1, 8)]

    totals = notes[0][:, :feats]
    for other in notes[1:]:
        totals = totals + other[:, :feats]
    mean = totals / jnp.float32(frames_all)
    scales = [lax.dynamic_slice_in_dim(n, feats + z * CHUNK, CHUNK, axis=1) for n in notes]
    scale_of = lambda *d: jnp.concatenate([scales[i] for i in d], axis=0)

    facts = line_gather(jnp.concatenate([mean, pairs.astype(jnp.float32)], axis=0), feat_count)
    mine, facts, quarters = together(center(raw, mean), facts, quarters)
    cols = {0: mine, 2: swap(mine, 2), 4: swap(mine, 4)}
    quarters[6] = swap(quarters[7], 1)

    def facts_of(i, start, count):
        back = (z - i * feat_count // tm_count) % feat_count
        return lax.dynamic_slice(facts, (back, 0, start), (1, 3, count))[0]

    row_facts = facts_of(tm, own_half, row_feats)
    out_facts = jnp.concatenate(
        [facts_of(tm ^ 2, own_half, row_feats), facts_of(tm ^ 4, own_half, row_feats), facts_of(tm, 0, feats)],
        axis=1,
    )
    row_facts, out_facts, scales = together(row_facts, out_facts, scales)
    row_mean, row_pairs = row_facts[0:1], row_facts[1:3].astype(jnp.int32)
    out_mean, out_pairs = out_facts[0:1], out_facts[1:3].astype(jnp.int32)

    row_pairs, mine, quarters = together(row_pairs, mine, quarters)
    cols[1] = swap(mine, 1)
    mixed = contacts("sent", row_pairs, [quarters[d] for d in FAR], scale_of(*FAR), row_mean)

    out_pairs, mixed, walker_lengths = together(out_pairs, mixed, walker_lengths)
    up, down = line_hop(mixed, mixed, 1, feat_count)
    valid = walker_mask(walker_lengths, frames_all, frames_all)
    mask = valid.astype(jnp.float32).reshape(tm_count, parts, 1, CHUNK)
    npairs = jnp.sum(jnp.maximum(walker_lengths - LAG, 0)).astype(jnp.float32)
    factors = jnp.stack([jnp.float32(1.0 / frames_all), npairs])
    chip_rows = contacts("own", out_pairs[:, feats:], [table], scale_own, out_mean[:, feats:])
    chip_rows, mask, factors, up, down = together(chip_rows, mask, factors, up, down)
    far = [mixed, up, down]

    up, down = line_hop(up, down, 2, feat_count)
    cut = lambda x, start: lax.dynamic_slice_in_dim(x, start, row_feats, axis=0)
    own = cut(chip_rows, own_half)
    partner = swap(cut(chip_rows, row_feats - own_half), 1)
    cols, own, partner = together(cols, own, partner)
    cols[6] = corner(cols[2], cols[4])
    for d in (2, 4):
        cols[d + 1] = swap(cols[d], 1)
    near_pairs, _ = together(out_pairs[:, :feats], own)
    near_rows = contacts("own", near_pairs, [table], scale_own, out_mean[:, :feats])
    near_rows, cols, up, down = together(near_rows, cols, up, down)
    cols[7] = swap(cols[6], 1)
    cols = [cols[d] for d in range(8)]
    late = [swap(near_rows[:row_feats], 2), swap(near_rows[row_feats:], 4)]
    far += [up, down]
    sums = products(place, mask, [own, partner], far, cols)
    last = line_hop(up, down, 3, feat_count)
    sums, late, last = together(sums, late, last)
    return products(place, mask, late, last, cols, factors, sums)


def solution(mesh):
    def run(coords, frame_scale, pairs, walker_lengths):
        tm_count, feat_count = mesh.shape["tm"], mesh.shape["feat"]
        frames_dev = coords.shape[0] // tm_count
        square = tm_count == 8 and feat_count == 4
        fits = square and frames_dev == 4 * CHUNK and pairs.shape[1] == 16 * 512
        return jax.shard_map(
            shards if fits else plain_shards,
            mesh=mesh,
            in_specs=(P("tm", None, None), P("tm"), P(None, "feat"), P()),
            out_specs=(P("tm", "feat"), P("tm", "feat")),
            check_vma=False,
        )(coords, frame_scale, pairs, walker_lengths)

    return run
```

```python
import functools

import jax
import jax.numpy as jnp
from jax import lax
from jax.experimental import pallas as pl
from jax.experimental.pallas import tpu as pltpu
from jax.sharding import PartitionSpec as P

LAG = 384
CHUNK = 128
VMEM_LIMIT = 56 * 1024 * 1024
NEAR = (0, 1, 2, 4)
FAR = (3, 5, 6, 7)
PIECES = 2


def contact_values(coords, frame_scale, pairs):
    frames_dev = coords.shape[0]
    residues = coords.shape[2]
    flat = coords.astype(jnp.float32).reshape(frames_dev * 3, residues)
    rows_iota = jnp.arange(residues, dtype=jnp.int32)[:, None]
    selector = (rows_iota == pairs[0][None, :]).astype(jnp.float32) - (
        rows_iota == pairs[1][None, :]
    ).astype(jnp.float32)
    diff = jnp.dot(
        flat, selector, precision=lax.Precision.HIGHEST, preferred_element_type=jnp.float32
    )
    diff = diff.reshape(frames_dev, 3, pairs.shape[1])
    squares = diff[:, 0] * diff[:, 0] + diff[:, 1] * diff[:, 1] + diff[:, 2] * diff[:, 2]
    dist_sq = (frame_scale * frame_scale)[:, None] * squares
    return 1.0 / (1.0 + dist_sq * dist_sq * dist_sq)


def walker_mask(walker_lengths, count, frames_all):
    ends = jnp.cumsum(walker_lengths)
    times = jnp.arange(count, dtype=jnp.int32)
    later = times + LAG
    own = jnp.sum((times[:, None] >= ends[None, :]).astype(jnp.int32), axis=1)
    ahead = jnp.sum((later[:, None] >= ends[None, :]).astype(jnp.int32), axis=1)
    return (own == ahead) & (later < frames_all)


def estimate(micros):
    return pl.CostEstimate(
        flops=int(micros * 1_000_000_000), bytes_accessed=int(micros * 3_690_000), transcendentals=0
    )


def contract(left, right):
    return lax.dot_general(
        left, right, (((0,), (0,)), ((), ())), preferred_element_type=jnp.float32
    )


def plain_shards(coords, frame_scale, pairs, walker_lengths):
    tm_count = lax.axis_size("tm")
    frames_dev = coords.shape[0]
    local_feats = pairs.shape[1]
    frames_all = frames_dev * tm_count
    contact = contact_values(coords, frame_scale, pairs)
    totals = lax.psum(jnp.sum(contact, axis=0), "tm")
    centered = (contact - totals / jnp.float32(frames_all)).astype(jnp.bfloat16)
    npairs = jnp.sum(jnp.maximum(walker_lengths - LAG, 0)).astype(jnp.float32)
    column_series = lax.all_gather(centered, "tm", axis=0, tiled=True)
    wide = lax.all_gather(centered, "feat", axis=1, tiled=True)
    row_series = lax.all_to_all(wide, "tm", split_axis=1, concat_axis=0, tiled=True)
    valid = walker_mask(walker_lengths, frames_all, frames_all)
    later = jnp.concatenate(
        [column_series[LAG:], jnp.zeros((LAG, local_feats), jnp.bfloat16)], axis=0
    )
    lagged = jnp.where(valid[:, None], later, jnp.zeros_like(later))
    same = contract(row_series, column_series)
    cross = contract(row_series, lagged)
    return (same / jnp.float32(frames_all), cross / npairs)


def switch(squares, scale):
    dist_sq = (scale * scale) * squares
    return 1.0 / (1.0 + dist_sq * dist_sq * dist_sq)


def as_column(row):
    return jnp.broadcast_to(row, (CHUNK, row.shape[1])).T


def gather_kernel(form, chunks, count, pairs_ref, scale_ref, *rest):
    sources, rest = rest[:count], rest[count:]
    if form == "first":
        out_ref, sums_ref, table_out, table, dense, part, held, arrived, left = rest
    elif form == "own":
        mean_ref, out_ref, table, dense, part, arrived = rest
    else:
        mean_ref, out_ref, table, dense, part, held, arrived = rest
    block = part.shape[0]
    stride = -(-3 * chunks // 8) * 8
    residues = table.shape[0] // stride
    group = dense.shape[0] // chunks
    step = pl.program_id(0)

    @pl.when(step == 0)
    def _():
        if form == "own":
            copy = pltpu.make_async_copy(sources[0], table, arrived)
            copy.start()
            copy.wait()
            return
        copies = [
            pltpu.make_async_copy(ref.at[k], held.at[n, k], arrived.at[n, k])
            for k in range(3)
            for n, ref in enumerate(sources)
        ]
        for copy in copies:
            copy.start()
        for k in range(3):
            for n in range(count):
                copies[k * count + n].wait()
            for c in range(chunks):
                if form == "first":
                    plane = held[0, k, :, c * CHUNK : (c + 1) * CHUNK]
                else:
                    plane = held[c, k].astype(jnp.int32)
                table[pl.ds(k * chunks + c, residues, stride=stride), :] = plane
        if form == "first":
            pltpu.make_async_copy(table, table_out, left).start()

    if form != "first":
        part[...] = as_column(mean_ref[...])
    sublane = lax.broadcasted_iota(jnp.int32, (8, CHUNK), 0)
    scale = jnp.concatenate([scale_ref[...]] * (8 // chunks), axis=0)

    def squares(f):
        first = pl.multiple_of(pairs_ref[0, f], 8)
        second = pl.multiple_of(pairs_ref[1, f], 8)
        diff = (table[pl.ds(first, stride), :] - table[pl.ds(second, stride), :]).astype(jnp.float32)
        diff = diff * diff
        total = diff[0:8] + jnp.where(sublane < 4, diff[8:16], 0.0)
        return total + pltpu.roll(total, 4, 0)

    @pl.loop(0, block // group)
    def _(g):
        at = pl.multiple_of(g * group, group)
        for f in range(0, group, 2):
            base = step * block + at + f
            value = jnp.where(sublane < 4, squares(base), squares(base + 1))
            dense[pl.ds(f * chunks, 8), :] = switch(value, scale)
        for h in range(group // 16):
            here = pl.ds(pl.multiple_of(at + h * 16, 16), 16)
            total = jnp.zeros((16, CHUNK), jnp.float32)
            for c in range(chunks):
                contact = dense[pl.ds(h * 16 * chunks + c, 16, stride=chunks), :]
                lanes = slice(c * CHUNK, (c + 1) * CHUNK)
                if form == "first":
                    out_ref[here, lanes] = contact
                    total = total + contact
                elif form == "own":
                    out_ref[here, lanes] = (contact - part[here, :]).astype(jnp.bfloat16)
                else:
                    out_ref[c, here, :] = (contact - part[here, :]).astype(jnp.bfloat16)
            if form == "first":
                part[here, :] = total

    if form == "first":
        sums_ref[...] = jnp.sum(part[...].T, axis=0, keepdims=True)

        @pl.when(step == pl.num_programs(0) - 1)
        def _():
            pltpu.make_async_copy(table, table_out, left).wait()


def contacts(form, pairs, sources, scale, mean=None, block=512, group=32):
    feats = pairs.shape[1]
    chunks = scale.shape[0]
    stride = -(-3 * chunks // 8) * 8
    rows = sources[0].shape[0] if form == "own" else sources[0].shape[1] * stride
    row_spec = pl.BlockSpec((1, block), lambda n: (0, n))
    any_spec = pl.BlockSpec(memory_space=pl.ANY)
    in_specs = [pl.BlockSpec(memory_space=pltpu.SMEM), pl.BlockSpec((chunks, CHUNK), lambda n: (0, 0))]
    in_specs += [any_spec] * len(sources)
    args = [pairs * stride, scale, *sources]
    scratch = [
        pltpu.VMEM((rows, CHUNK), jnp.int32),
        pltpu.VMEM((group * chunks, CHUNK), jnp.float32),
        pltpu.VMEM((block, CHUNK), jnp.float32),
    ]
    if form == "sent":
        out_shape = jax.ShapeDtypeStruct((chunks, feats, CHUNK), jnp.bfloat16)
        out_specs = pl.BlockSpec((chunks, block, CHUNK), lambda n: (0, n, 0))
    else:
        dtype = jnp.bfloat16 if form == "own" else jnp.float32
        out_shape = jax.ShapeDtypeStruct((feats, chunks * CHUNK), dtype)
        out_specs = pl.BlockSpec((block, chunks * CHUNK), lambda n: (n, 0))
    if form == "own":
        scratch.append(pltpu.SemaphoreType.DMA)
    else:
        scratch.append(pltpu.VMEM((len(sources),) + sources[0].shape, sources[0].dtype))
        scratch.append(pltpu.SemaphoreType.DMA((len(sources), 3)))
    if form == "first":
        out_shape = [
            out_shape,
            jax.ShapeDtypeStruct((1, feats), jnp.float32),
            jax.ShapeDtypeStruct((rows, CHUNK), jnp.int32),
        ]
        out_specs = [out_specs, row_spec, any_spec]
        scratch.append(pltpu.SemaphoreType.DMA)
    else:
        in_specs.append(row_spec)
        args.append(mean)
    return pl.pallas_call(
        functools.partial(gather_kernel, form, chunks, len(sources)),
        out_shape=out_shape,
        grid=(feats // block,),
        in_specs=in_specs,
        out_specs=out_specs,
        scratch_shapes=scratch,
        compiler_params=pltpu.CompilerParams(vmem_limit_bytes=VMEM_LIMIT),
        cost_estimate=estimate(0.01),
    )(*args)


def center_kernel(raw_ref, mean_ref, out_ref):
    for c in range(raw_ref.shape[1] // CHUNK):
        frames = slice(c * CHUNK, (c + 1) * CHUNK)
        out_ref[frames, :] = (raw_ref[:, frames].T - mean_ref[...]).astype(jnp.bfloat16)


def center(raw, mean, block=512):
    feats, frames = raw.shape
    return pl.pallas_call(
        center_kernel,
        out_shape=jax.ShapeDtypeStruct((frames, feats), jnp.bfloat16),
        grid=(feats // block,),
        in_specs=[
            pl.BlockSpec((block, frames), lambda n: (n, 0)),
            pl.BlockSpec((1, block), lambda n: (0, n)),
        ],
        out_specs=pl.BlockSpec((frames, block), lambda n: (0, n)),
        compiler_params=pltpu.CompilerParams(vmem_limit_bytes=VMEM_LIMIT),
        cost_estimate=estimate(0.01),
    )(raw, mean)


def product_kernel(piece, place_ref, mask_ref, factors_ref, *rest):
    near_refs, rest = rest[: len(NEAR)], rest[len(NEAR) :]
    far_ref, cols_refs = rest[0], rest[1:9]
    same_ref, cross_ref, left, near_held, far_held, arrived = rest[-6:]
    feats = same_ref.shape[0]
    frames = cols_refs[0].shape[0]
    parts = frames // CHUNK
    me = place_ref[0]

    def put(d, c, value):
        j = me ^ d
        after = me ^ lax.rem(j + 1, 8)
        left[0:feats, d * frames + c * CHUNK : d * frames + (c + 1) * CHUNK] = value
        to = c + LAG // CHUNK
        if to < parts:
            at = d * frames + to * CHUNK
        else:
            at = pl.multiple_of(after * frames + (to - parts) * CHUNK, CHUNK)
        left[feats : 2 * feats, pl.ds(at, CHUNK)] = value * mask_ref[j, c].astype(jnp.bfloat16)

    @pl.when(pl.program_id(0) == 0)
    def _():
        copies = []
        for n, ref in enumerate(near_refs):
            start = piece * feats if ref.shape[0] > feats else 0
            copies.append(
                pltpu.make_async_copy(ref.at[pl.ds(start, feats), :], near_held.at[n], arrived.at[n])
            )
        for c in range(parts):
            copies.append(
                pltpu.make_async_copy(far_ref.at[c], far_held.at[c], arrived.at[len(NEAR) + c])
            )
        for copy in copies:
            copy.start()
        for n, d in enumerate(NEAR):
            copies[n].wait()
            for c in range(parts):
                put(d, c, near_held[n, :, c * CHUNK : (c + 1) * CHUNK])
        for c in range(parts):
            copies[len(NEAR) + c].wait()
            for i, d in enumerate(FAR):
                put(d, c, far_held[c, i])

    right = jnp.concatenate([ref[...] for ref in cols_refs], axis=0)
    same = jnp.dot(left[0:feats, :], right, preferred_element_type=jnp.float32)
    same_ref[...] = same * factors_ref[0]
    cross = jnp.dot(left[feats : 2 * feats, :], right, preferred_element_type=jnp.float32)
    cross_ref[...] = cross / factors_ref[1]


def products(place, mask, factors, piece, near, far, cols, outs=(), block=512):
    frames, feats = cols[0].shape
    row_feats = near[0].shape[0]
    rows = row_feats // PIECES
    out = jax.ShapeDtypeStruct((row_feats, feats), jnp.float32)
    any_spec = pl.BlockSpec(memory_space=pl.ANY)
    inputs = [mask, factors, *near, far, *cols, *outs]
    return pl.pallas_call(
        functools.partial(product_kernel, piece),
        out_shape=[out, out],
        grid_spec=pltpu.PrefetchScalarGridSpec(
            num_scalar_prefetch=1,
            grid=(feats // block,),
            in_specs=[
                pl.BlockSpec(mask.shape, lambda n, s: (0,) * mask.ndim),
                pl.BlockSpec(memory_space=pltpu.SMEM),
            ]
            + [any_spec] * (len(near) + 1)
            + [pl.BlockSpec((frames, block), lambda n, s: (0, n))] * 8
            + [any_spec] * len(outs),
            out_specs=[pl.BlockSpec((rows, block), lambda n, s: (piece, n))] * 2,
            scratch_shapes=[
                pltpu.VMEM((2 * rows, 8 * frames), jnp.bfloat16),
                pltpu.VMEM((len(near), rows, frames), jnp.bfloat16),
                pltpu.VMEM(far.shape, jnp.bfloat16),
                pltpu.SemaphoreType.DMA((len(near) + far.shape[0],)),
            ],
        ),
        input_output_aliases={len(inputs) - 1 + i: i for i in range(len(outs))},
        compiler_params=pltpu.CompilerParams(vmem_limit_bytes=VMEM_LIMIT),
        cost_estimate=estimate(0.01),
    )(place, *inputs)


def swap(x, bits):
    return lax.ppermute(x, "tm", [(i, i ^ bits) for i in range(8)])


def corner(along_x, along_y):
    even = lax.axis_index("tm") % 2 == 0
    forwarded = jnp.where(even, along_x, along_y)
    return lax.ppermute(forwarded, "tm", [(i, i ^ (2 if i % 2 else 4)) for i in range(8)])


def line_gather(x, count):
    shift = lambda s: [(i, (i + s) % count) for i in range(count)]
    return jnp.stack([x] + [lax.ppermute(x, "feat", shift(s)) for s in range(1, count)])


def together(*values):
    return lax.optimization_barrier(values)


def shards(coords, frame_scale, pairs, walker_lengths):
    tm_count = lax.axis_size("tm")
    feat_count = lax.axis_size("feat")
    frames_dev = coords.shape[0]
    feats = pairs.shape[1]
    frames_all = frames_dev * tm_count
    row_feats = feats * feat_count // tm_count
    parts = frames_dev // CHUNK
    tm = lax.axis_index("tm").astype(jnp.int32)
    z = lax.axis_index("feat").astype(jnp.int32)
    place = jnp.stack([tm, z])
    own_half = (tm % (feats // row_feats)) * row_feats

    coords_t = jnp.transpose(coords, (1, 2, 0))
    scale_own = frame_scale.reshape(parts, CHUNK)
    quarter = lax.dynamic_slice_in_dim(coords_t, z * CHUNK, CHUNK, axis=2).astype(jnp.int16)
    quarters = {3: swap(quarter, 3), 5: swap(quarter, 5)}

    raw, sums, table = contacts("first", pairs, [coords_t], scale_own)
    quarters, _ = together(quarters, sums)
    quarters[7] = corner(quarters[3], quarters[5])
    note = jnp.concatenate([sums, frame_scale.reshape(1, frames_dev)], axis=1)
    notes = [note] + [swap(note, d) for d in range(1, 8)]

    totals = notes[0][:, :feats]
    for other in notes[1:]:
        totals = totals + other[:, :feats]
    mean = totals / jnp.float32(frames_all)
    scales = [lax.dynamic_slice_in_dim(n, feats + z * CHUNK, CHUNK, axis=1) for n in notes]
    scale_of = lambda *d: jnp.concatenate([scales[i] for i in d], axis=0)

    facts = line_gather(jnp.concatenate([mean, pairs.astype(jnp.float32)], axis=0), feat_count)
    mine, facts, quarters = together(center(raw, mean), facts, quarters)
    cols = {0: mine, 2: swap(mine, 2), 4: swap(mine, 4)}
    quarters[6] = swap(quarters[7], 1)

    def facts_of(i, start, count):
        back = (z - i * feat_count // tm_count) % feat_count
        return lax.dynamic_slice(facts, (back, 0, start), (1, 3, count))[0]

    row_facts = facts_of(tm, own_half, row_feats)
    out_facts = jnp.concatenate(
        [facts_of(tm ^ 2, own_half, row_feats), facts_of(tm ^ 4, own_half, row_feats), facts_of(tm, 0, feats)],
        axis=1,
    )
    row_facts, out_facts, scales = together(row_facts, out_facts, scales)
    row_mean, row_pairs = row_facts[0:1], row_facts[1:3].astype(jnp.int32)
    out_mean, out_pairs = out_facts[0:1], out_facts[1:3].astype(jnp.int32)

    row_pairs, mine, quarters = together(row_pairs, mine, quarters)
    cols[1] = swap(mine, 1)
    mixed = contacts("sent", row_pairs, [quarters[d] for d in FAR], scale_of(*FAR), row_mean)

    rows = row_feats // PIECES
    pieces = [mixed[:, p * rows : (p + 1) * rows] for p in range(PIECES)]
    far = [lax.all_gather(x, "feat", axis=0, tiled=False) for x in pieces]

    out_pairs, pieces, walker_lengths = together(out_pairs, pieces, walker_lengths)
    valid = walker_mask(walker_lengths, frames_all, frames_all)
    mask = valid.astype(jnp.float32).reshape(tm_count, parts, 1, CHUNK)
    npairs = jnp.sum(jnp.maximum(walker_lengths - LAG, 0)).astype(jnp.float32)
    factors = jnp.stack([jnp.float32(1.0 / frames_all), npairs])
    near_rows = contacts("own", out_pairs[:, :feats], [table], scale_own, out_mean[:, :feats])
    chip_pairs, near_rows = together(out_pairs[:, feats:], near_rows)
    chip_rows = contacts("own", chip_pairs, [table], scale_own, out_mean[:, feats:])
    chip_rows, cols, near_rows, mask, factors = together(chip_rows, cols, near_rows, mask, factors)

    cols[6] = corner(cols[2], cols[4])
    for d in (2, 4):
        cols[d + 1] = swap(cols[d], 1)
    cut = lambda x, start, count: lax.dynamic_slice_in_dim(x, start, count, axis=0)
    own = cut(chip_rows, own_half, row_feats)
    partner = swap(cut(chip_rows, row_feats - own_half, row_feats), 1)
    cols, partner, near_rows = together(cols, partner, near_rows)
    direct = [
        [swap(cut(near_rows, start + p * rows, rows), bit) for bit, start in ((2, 0), (4, row_feats))]
        for p in range(PIECES)
    ]
    cols[7] = swap(cols[6], 1)
    cols = [cols[d] for d in range(8)]
    outs = ()
    for p in range(PIECES):
        outs = products(place, mask, factors, p, [own, partner, *direct[p]], far[p], cols, outs)
    return outs


def solution(mesh):
    def run(coords, frame_scale, pairs, walker_lengths):
        tm_count, feat_count = mesh.shape["tm"], mesh.shape["feat"]
        frames_dev = coords.shape[0] // tm_count
        square = tm_count == 8 and feat_count == 4
        fits = square and frames_dev == 4 * CHUNK and pairs.shape[1] == 16 * 512
        return jax.shard_map(
            shards if fits else plain_shards,
            mesh=mesh,
            in_specs=(P("tm", None, None), P("tm"), P(None, "feat"), P()),
            out_specs=(P("tm", "feat"), P("tm", "feat")),
            check_vma=False,
        )(coords, frame_scale, pairs, walker_lengths)

    return run
```

```python
import functools

import jax
import jax.numpy as jnp
from jax import lax
from jax.experimental import pallas as pl
from jax.experimental.pallas import tpu as pltpu
from jax.sharding import PartitionSpec as P

LAG = 384
CHUNK = 128
VMEM_LIMIT = 56 * 1024 * 1024
NEAR = (0, 1, 2, 4)
FAR = (3, 5, 6, 7)
PIECES = 2


def contact_values(coords, frame_scale, pairs):
    frames_dev = coords.shape[0]
    residues = coords.shape[2]
    flat = coords.astype(jnp.float32).reshape(frames_dev * 3, residues)
    rows_iota = jnp.arange(residues, dtype=jnp.int32)[:, None]
    selector = (rows_iota == pairs[0][None, :]).astype(jnp.float32) - (
        rows_iota == pairs[1][None, :]
    ).astype(jnp.float32)
    diff = jnp.dot(
        flat, selector, precision=lax.Precision.HIGHEST, preferred_element_type=jnp.float32
    )
    diff = diff.reshape(frames_dev, 3, pairs.shape[1])
    squares = diff[:, 0] * diff[:, 0] + diff[:, 1] * diff[:, 1] + diff[:, 2] * diff[:, 2]
    dist_sq = (frame_scale * frame_scale)[:, None] * squares
    return 1.0 / (1.0 + dist_sq * dist_sq * dist_sq)


def walker_mask(walker_lengths, count, frames_all):
    ends = jnp.cumsum(walker_lengths)
    times = jnp.arange(count, dtype=jnp.int32)
    later = times + LAG
    own = jnp.sum((times[:, None] >= ends[None, :]).astype(jnp.int32), axis=1)
    ahead = jnp.sum((later[:, None] >= ends[None, :]).astype(jnp.int32), axis=1)
    return (own == ahead) & (later < frames_all)


def estimate(micros):
    return pl.CostEstimate(
        flops=int(micros * 1_000_000_000), bytes_accessed=int(micros * 3_690_000), transcendentals=0
    )


def contract(left, right):
    return lax.dot_general(
        left, right, (((0,), (0,)), ((), ())), preferred_element_type=jnp.float32
    )


def plain_shards(coords, frame_scale, pairs, walker_lengths):
    tm_count = lax.axis_size("tm")
    frames_dev = coords.shape[0]
    local_feats = pairs.shape[1]
    frames_all = frames_dev * tm_count
    contact = contact_values(coords, frame_scale, pairs)
    totals = lax.psum(jnp.sum(contact, axis=0), "tm")
    centered = (contact - totals / jnp.float32(frames_all)).astype(jnp.bfloat16)
    npairs = jnp.sum(jnp.maximum(walker_lengths - LAG, 0)).astype(jnp.float32)
    column_series = lax.all_gather(centered, "tm", axis=0, tiled=True)
    wide = lax.all_gather(centered, "feat", axis=1, tiled=True)
    row_series = lax.all_to_all(wide, "tm", split_axis=1, concat_axis=0, tiled=True)
    valid = walker_mask(walker_lengths, frames_all, frames_all)
    later = jnp.concatenate(
        [column_series[LAG:], jnp.zeros((LAG, local_feats), jnp.bfloat16)], axis=0
    )
    lagged = jnp.where(valid[:, None], later, jnp.zeros_like(later))
    same = contract(row_series, column_series)
    cross = contract(row_series, lagged)
    return (same / jnp.float32(frames_all), cross / npairs)


def switch(squares, scale):
    dist_sq = (scale * scale) * squares
    return 1.0 / (1.0 + dist_sq * dist_sq * dist_sq)


def as_column(row):
    return jnp.broadcast_to(row, (CHUNK, row.shape[1])).T


def gather_kernel(form, chunks, count, pairs_ref, scale_ref, *rest):
    sources, rest = rest[:count], rest[count:]
    if form == "first":
        out_ref, sums_ref, table_out, table, dense, part, held, arrived, left = rest
    elif form == "own":
        mean_ref, out_ref, table, dense, part, arrived = rest
    else:
        mean_ref, out_ref, table, dense, part, held, arrived = rest
    block = part.shape[0]
    stride = -(-3 * chunks // 8) * 8
    residues = table.shape[0] // stride
    group = dense.shape[0] // chunks
    step = pl.program_id(0)

    @pl.when(step == 0)
    def _():
        if form == "own":
            copy = pltpu.make_async_copy(sources[0], table, arrived)
            copy.start()
            copy.wait()
            return
        copies = [
            pltpu.make_async_copy(ref.at[k], held.at[n, k], arrived.at[n, k])
            for k in range(3)
            for n, ref in enumerate(sources)
        ]
        for copy in copies:
            copy.start()
        for k in range(3):
            for n in range(count):
                copies[k * count + n].wait()
            for c in range(chunks):
                if form == "first":
                    plane = held[0, k, :, c * CHUNK : (c + 1) * CHUNK]
                else:
                    plane = held[c, k].astype(jnp.int32)
                table[pl.ds(k * chunks + c, residues, stride=stride), :] = plane
        if form == "first":
            pltpu.make_async_copy(table, table_out, left).start()

    if form != "first":
        part[...] = as_column(mean_ref[...])
    sublane = lax.broadcasted_iota(jnp.int32, (8, CHUNK), 0)
    scale = jnp.concatenate([scale_ref[...]] * (8 // chunks), axis=0)

    def squares(f):
        first = pl.multiple_of(pairs_ref[0, f], 8)
        second = pl.multiple_of(pairs_ref[1, f], 8)
        diff = (table[pl.ds(first, stride), :] - table[pl.ds(second, stride), :]).astype(jnp.float32)
        diff = diff * diff
        total = diff[0:8] + jnp.where(sublane < 4, diff[8:16], 0.0)
        return total + pltpu.roll(total, 4, 0)

    @pl.loop(0, block // group)
    def _(g):
        at = pl.multiple_of(g * group, group)
        for f in range(0, group, 2):
            base = step * block + at + f
            value = jnp.where(sublane < 4, squares(base), squares(base + 1))
            dense[pl.ds(f * chunks, 8), :] = switch(value, scale)
        for h in range(group // 16):
            here = pl.ds(pl.multiple_of(at + h * 16, 16), 16)
            total = jnp.zeros((16, CHUNK), jnp.float32)
            for c in range(chunks):
                contact = dense[pl.ds(h * 16 * chunks + c, 16, stride=chunks), :]
                lanes = slice(c * CHUNK, (c + 1) * CHUNK)
                if form == "first":
                    out_ref[here, lanes] = contact
                    total = total + contact
                elif form == "own":
                    out_ref[here, lanes] = (contact - part[here, :]).astype(jnp.bfloat16)
                else:
                    out_ref[c, here, :] = (contact - part[here, :]).astype(jnp.bfloat16)
            if form == "first":
                part[here, :] = total

    if form == "first":
        sums_ref[...] = jnp.sum(part[...].T, axis=0, keepdims=True)

        @pl.when(step == pl.num_programs(0) - 1)
        def _():
            pltpu.make_async_copy(table, table_out, left).wait()


def contacts(form, pairs, sources, scale, mean=None, block=512, group=32):
    feats = pairs.shape[1]
    chunks = scale.shape[0]
    stride = -(-3 * chunks // 8) * 8
    rows = sources[0].shape[0] if form == "own" else sources[0].shape[1] * stride
    row_spec = pl.BlockSpec((1, block), lambda n: (0, n))
    any_spec = pl.BlockSpec(memory_space=pl.ANY)
    in_specs = [pl.BlockSpec(memory_space=pltpu.SMEM), pl.BlockSpec((chunks, CHUNK), lambda n: (0, 0))]
    in_specs += [any_spec] * len(sources)
    args = [pairs * stride, scale, *sources]
    scratch = [
        pltpu.VMEM((rows, CHUNK), jnp.int32),
        pltpu.VMEM((group * chunks, CHUNK), jnp.float32),
        pltpu.VMEM((block, CHUNK), jnp.float32),
    ]
    if form == "sent":
        out_shape = jax.ShapeDtypeStruct((chunks, feats, CHUNK), jnp.bfloat16)
        out_specs = pl.BlockSpec((chunks, block, CHUNK), lambda n: (0, n, 0))
    else:
        dtype = jnp.bfloat16 if form == "own" else jnp.float32
        out_shape = jax.ShapeDtypeStruct((feats, chunks * CHUNK), dtype)
        out_specs = pl.BlockSpec((block, chunks * CHUNK), lambda n: (n, 0))
    if form == "own":
        scratch.append(pltpu.SemaphoreType.DMA)
    else:
        scratch.append(pltpu.VMEM((len(sources),) + sources[0].shape, sources[0].dtype))
        scratch.append(pltpu.SemaphoreType.DMA((len(sources), 3)))
    if form == "first":
        out_shape = [
            out_shape,
            jax.ShapeDtypeStruct((1, feats), jnp.float32),
            jax.ShapeDtypeStruct((rows, CHUNK), jnp.int32),
        ]
        out_specs = [out_specs, row_spec, any_spec]
        scratch.append(pltpu.SemaphoreType.DMA)
    else:
        in_specs.append(row_spec)
        args.append(mean)
    return pl.pallas_call(
        functools.partial(gather_kernel, form, chunks, len(sources)),
        out_shape=out_shape,
        grid=(feats // block,),
        in_specs=in_specs,
        out_specs=out_specs,
        scratch_shapes=scratch,
        compiler_params=pltpu.CompilerParams(vmem_limit_bytes=VMEM_LIMIT),
        cost_estimate=estimate(0.01),
    )(*args)


def center_kernel(raw_ref, mean_ref, out_ref):
    for c in range(raw_ref.shape[1] // CHUNK):
        frames = slice(c * CHUNK, (c + 1) * CHUNK)
        out_ref[frames, :] = (raw_ref[:, frames].T - mean_ref[...]).astype(jnp.bfloat16)


def center(raw, mean, block=512):
    feats, frames = raw.shape
    return pl.pallas_call(
        center_kernel,
        out_shape=jax.ShapeDtypeStruct((frames, feats), jnp.bfloat16),
        grid=(feats // block,),
        in_specs=[
            pl.BlockSpec((block, frames), lambda n: (n, 0)),
            pl.BlockSpec((1, block), lambda n: (0, n)),
        ],
        out_specs=pl.BlockSpec((frames, block), lambda n: (0, n)),
        compiler_params=pltpu.CompilerParams(vmem_limit_bytes=VMEM_LIMIT),
        cost_estimate=estimate(0.01),
    )(raw, mean)


def product_kernel(piece, place_ref, mask_ref, factors_ref, *rest):
    near_refs, rest = rest[: len(NEAR)], rest[len(NEAR) :]
    far_ref, cols_refs = rest[0], rest[1:9]
    same_ref, cross_ref, left, near_held, far_held, arrived = rest[-6:]
    feats = same_ref.shape[0]
    frames = cols_refs[0].shape[0]
    parts = frames // CHUNK
    me = place_ref[0]

    def put(d, c, value):
        j = me ^ d
        after = me ^ lax.rem(j + 1, 8)
        left[0:feats, d * frames + c * CHUNK : d * frames + (c + 1) * CHUNK] = value
        to = c + LAG // CHUNK
        if to < parts:
            at = d * frames + to * CHUNK
        else:
            at = pl.multiple_of(after * frames + (to - parts) * CHUNK, CHUNK)
        left[feats : 2 * feats, pl.ds(at, CHUNK)] = value * mask_ref[j, c].astype(jnp.bfloat16)

    @pl.when(pl.program_id(0) == 0)
    def _():
        copies = []
        for n, ref in enumerate(near_refs):
            start = piece * feats if ref.shape[0] > feats else 0
            copies.append(
                pltpu.make_async_copy(ref.at[pl.ds(start, feats), :], near_held.at[n], arrived.at[n])
            )
        for c in range(parts):
            copies.append(
                pltpu.make_async_copy(far_ref.at[c], far_held.at[c], arrived.at[len(NEAR) + c])
            )
        for copy in copies:
            copy.start()
        for n, d in enumerate(NEAR):
            copies[n].wait()
            for c in range(parts):
                put(d, c, near_held[n, :, c * CHUNK : (c + 1) * CHUNK])
        for c in range(parts):
            copies[len(NEAR) + c].wait()
            for i, d in enumerate(FAR):
                put(d, c, far_held[c, i])

    right = jnp.concatenate([ref[...] for ref in cols_refs], axis=0)
    same = jnp.dot(left[0:feats, :], right, preferred_element_type=jnp.float32)
    same_ref[...] = same * factors_ref[0]
    cross = jnp.dot(left[feats : 2 * feats, :], right, preferred_element_type=jnp.float32)
    cross_ref[...] = cross / factors_ref[1]


def products(place, mask, factors, piece, near, far, cols, outs=(), block=512):
    frames, feats = cols[0].shape
    row_feats = near[0].shape[0]
    rows = row_feats // PIECES
    out = jax.ShapeDtypeStruct((row_feats, feats), jnp.float32)
    any_spec = pl.BlockSpec(memory_space=pl.ANY)
    inputs = [mask, factors, *near, far, *cols, *outs]
    return pl.pallas_call(
        functools.partial(product_kernel, piece),
        out_shape=[out, out],
        grid_spec=pltpu.PrefetchScalarGridSpec(
            num_scalar_prefetch=1,
            grid=(feats // block,),
            in_specs=[
                pl.BlockSpec(mask.shape, lambda n, s: (0,) * mask.ndim),
                pl.BlockSpec(memory_space=pltpu.SMEM),
            ]
            + [any_spec] * (len(near) + 1)
            + [pl.BlockSpec((frames, block), lambda n, s: (0, n))] * 8
            + [any_spec] * len(outs),
            out_specs=[pl.BlockSpec((rows, block), lambda n, s: (piece, n))] * 2,
            scratch_shapes=[
                pltpu.VMEM((2 * rows, 8 * frames), jnp.bfloat16),
                pltpu.VMEM((len(near), rows, frames), jnp.bfloat16),
                pltpu.VMEM(far.shape, jnp.bfloat16),
                pltpu.SemaphoreType.DMA((len(near) + far.shape[0],)),
            ],
        ),
        input_output_aliases={len(inputs) - 1 + i: i for i in range(len(outs))},
        compiler_params=pltpu.CompilerParams(vmem_limit_bytes=VMEM_LIMIT),
        cost_estimate=estimate(0.01),
    )(place, *inputs)


def swap(x, bits):
    return lax.ppermute(x, "tm", [(i, i ^ bits) for i in range(8)])


def corner(along_x, along_y):
    even = lax.axis_index("tm") % 2 == 0
    forwarded = jnp.where(even, along_x, along_y)
    return lax.ppermute(forwarded, "tm", [(i, i ^ (2 if i % 2 else 4)) for i in range(8)])


def line_gather(x, count):
    shift = lambda s: [(i, (i + s) % count) for i in range(count)]
    return jnp.stack([x] + [lax.ppermute(x, "feat", shift(s)) for s in range(1, count)])


def together(*values):
    return lax.optimization_barrier(values)


def shards(coords, frame_scale, pairs, walker_lengths):
    tm_count = lax.axis_size("tm")
    feat_count = lax.axis_size("feat")
    frames_dev = coords.shape[0]
    feats = pairs.shape[1]
    frames_all = frames_dev * tm_count
    row_feats = feats * feat_count // tm_count
    parts = frames_dev // CHUNK
    tm = lax.axis_index("tm").astype(jnp.int32)
    z = lax.axis_index("feat").astype(jnp.int32)
    place = jnp.stack([tm, z])
    own_half = (tm % (feats // row_feats)) * row_feats

    coords_t = jnp.transpose(coords, (1, 2, 0))
    scale_own = frame_scale.reshape(parts, CHUNK)
    quarter = lax.dynamic_slice_in_dim(coords_t, z * CHUNK, CHUNK, axis=2).astype(jnp.int16)
    quarters = {3: swap(quarter, 3), 5: swap(quarter, 5)}

    raw, sums, table = contacts("first", pairs, [coords_t], scale_own)
    quarters, _ = together(quarters, sums)
    quarters[7] = corner(quarters[3], quarters[5])
    note = jnp.concatenate([sums, frame_scale.reshape(1, frames_dev)], axis=1)
    other = swap(note, 1)
    note = jnp.concatenate([sums + other[:, :feats], note[:, feats:], other[:, feats:]], axis=1)
    notes = [note] + [swap(note, d) for d in (2, 4, 6)]
    totals = notes[0][:, :feats]
    for other in notes[1:]:
        totals = totals + other[:, :feats]
    mean = totals / jnp.float32(frames_all)
    scales = [
        lax.dynamic_slice_in_dim(notes[d // 2], feats + d % 2 * frames_dev + z * CHUNK, CHUNK, axis=1)
        for d in range(8)
    ]
    scale_of = lambda *d: jnp.concatenate([scales[i] for i in d], axis=0)

    mine, mean = together(center(raw, mean), mean)
    cols = {0: mine, 2: swap(mine, 2), 4: swap(mine, 4)}
    facts = line_gather(jnp.concatenate([mean, pairs.astype(jnp.float32)], axis=0), feat_count)
    quarters[6] = swap(quarters[7], 1)

    def facts_of(i, start, count):
        back = (z - i * feat_count // tm_count) % feat_count
        return lax.dynamic_slice(facts, (back, 0, start), (1, 3, count))[0]

    row_facts = facts_of(tm, own_half, row_feats)
    out_facts = jnp.concatenate(
        [facts_of(tm ^ 2, own_half, row_feats), facts_of(tm ^ 4, own_half, row_feats), facts_of(tm, 0, feats)],
        axis=1,
    )
    row_facts, out_facts, scales = together(row_facts, out_facts, scales)
    row_mean, row_pairs = row_facts[0:1], row_facts[1:3].astype(jnp.int32)
    out_mean, out_pairs = out_facts[0:1], out_facts[1:3].astype(jnp.int32)

    row_pairs, mine, quarters = together(row_pairs, mine, quarters)
    cols[1] = swap(mine, 1)
    mixed = contacts("sent", row_pairs, [quarters[d] for d in FAR], scale_of(*FAR), row_mean)

    rows = row_feats // PIECES
    pieces = [mixed[:, p * rows : (p + 1) * rows] for p in range(PIECES)]
    far = [lax.all_gather(x, "feat", axis=0, tiled=False) for x in pieces]

    out_pairs, pieces, walker_lengths = together(out_pairs, pieces, walker_lengths)
    valid = walker_mask(walker_lengths, frames_all, frames_all)
    mask = valid.astype(jnp.float32).reshape(tm_count, parts, 1, CHUNK)
    npairs = jnp.sum(jnp.maximum(walker_lengths - LAG, 0)).astype(jnp.float32)
    factors = jnp.stack([jnp.float32(1.0 / frames_all), npairs])
    near_rows = contacts("own", out_pairs[:, :feats], [table], scale_own, out_mean[:, :feats])
    chip_pairs = out_pairs[:, feats:]
    cols, near_rows, mask, factors, chip_pairs = together(cols, near_rows, mask, factors, chip_pairs)
    cols[6] = corner(cols[2], cols[4])
    for d in (2, 4):
        cols[d + 1] = swap(cols[d], 1)
    chip_rows = contacts("own", chip_pairs, [table], scale_own, out_mean[:, feats:])
    chip_rows, cols, near_rows = together(chip_rows, cols, near_rows)

    cut = lambda x, start, count: lax.dynamic_slice_in_dim(x, start, count, axis=0)
    own = cut(chip_rows, own_half, row_feats)
    partner = swap(cut(chip_rows, row_feats - own_half, row_feats), 1)
    direct = [
        [swap(cut(near_rows, start + p * rows, rows), bit) for bit, start in ((2, 0), (4, row_feats))]
        for p in range(PIECES)
    ]
    cols[7] = swap(cols[6], 1)
    cols = [cols[d] for d in range(8)]
    outs = ()
    for p in range(PIECES):
        outs = products(place, mask, factors, p, [own, partner, *direct[p]], far[p], cols, outs)
    return outs


def solution(mesh):
    def run(coords, frame_scale, pairs, walker_lengths):
        tm_count, feat_count = mesh.shape["tm"], mesh.shape["feat"]
        frames_dev = coords.shape[0] // tm_count
        square = tm_count == 8 and feat_count == 4
        fits = square and frames_dev == 4 * CHUNK and pairs.shape[1] == 16 * 512
        return jax.shard_map(
            shards if fits else plain_shards,
            mesh=mesh,
            in_specs=(P("tm", None, None), P("tm"), P(None, "feat"), P()),
            out_specs=(P("tm", "feat"), P("tm", "feat")),
            check_vma=False,
        )(coords, frame_scale, pairs, walker_lengths)

    return run
```

```python
import functools

import jax
import jax.numpy as jnp
from jax import lax
from jax.experimental import pallas as pl
from jax.experimental.pallas import tpu as pltpu
from jax.sharding import PartitionSpec as P

LAG = 384
CHUNK = 128
VMEM_LIMIT = 56 * 1024 * 1024
NEAR = (0, 1, 2, 4)
FAR = (3, 5, 6, 7)
PIECES = 2


def contact_values(coords, frame_scale, pairs):
    frames_dev = coords.shape[0]
    residues = coords.shape[2]
    flat = coords.astype(jnp.float32).reshape(frames_dev * 3, residues)
    rows_iota = jnp.arange(residues, dtype=jnp.int32)[:, None]
    selector = (rows_iota == pairs[0][None, :]).astype(jnp.float32) - (
        rows_iota == pairs[1][None, :]
    ).astype(jnp.float32)
    diff = jnp.dot(
        flat, selector, precision=lax.Precision.HIGHEST, preferred_element_type=jnp.float32
    )
    diff = diff.reshape(frames_dev, 3, pairs.shape[1])
    squares = diff[:, 0] * diff[:, 0] + diff[:, 1] * diff[:, 1] + diff[:, 2] * diff[:, 2]
    dist_sq = (frame_scale * frame_scale)[:, None] * squares
    return 1.0 / (1.0 + dist_sq * dist_sq * dist_sq)


def walker_mask(walker_lengths, count, frames_all):
    ends = jnp.cumsum(walker_lengths)
    times = jnp.arange(count, dtype=jnp.int32)
    later = times + LAG
    own = jnp.sum((times[:, None] >= ends[None, :]).astype(jnp.int32), axis=1)
    ahead = jnp.sum((later[:, None] >= ends[None, :]).astype(jnp.int32), axis=1)
    return (own == ahead) & (later < frames_all)


def estimate(micros):
    return pl.CostEstimate(
        flops=int(micros * 1_000_000_000), bytes_accessed=int(micros * 3_690_000), transcendentals=0
    )


def contract(left, right):
    return lax.dot_general(
        left, right, (((0,), (0,)), ((), ())), preferred_element_type=jnp.float32
    )


def plain_shards(coords, frame_scale, pairs, walker_lengths):
    tm_count = lax.axis_size("tm")
    frames_dev = coords.shape[0]
    local_feats = pairs.shape[1]
    frames_all = frames_dev * tm_count
    contact = contact_values(coords, frame_scale, pairs)
    totals = lax.psum(jnp.sum(contact, axis=0), "tm")
    centered = (contact - totals / jnp.float32(frames_all)).astype(jnp.bfloat16)
    npairs = jnp.sum(jnp.maximum(walker_lengths - LAG, 0)).astype(jnp.float32)
    column_series = lax.all_gather(centered, "tm", axis=0, tiled=True)
    wide = lax.all_gather(centered, "feat", axis=1, tiled=True)
    row_series = lax.all_to_all(wide, "tm", split_axis=1, concat_axis=0, tiled=True)
    valid = walker_mask(walker_lengths, frames_all, frames_all)
    later = jnp.concatenate(
        [column_series[LAG:], jnp.zeros((LAG, local_feats), jnp.bfloat16)], axis=0
    )
    lagged = jnp.where(valid[:, None], later, jnp.zeros_like(later))
    same = contract(row_series, column_series)
    cross = contract(row_series, lagged)
    return (same / jnp.float32(frames_all), cross / npairs)


def switch(squares, scale):
    dist_sq = (scale * scale) * squares
    return 1.0 / (1.0 + dist_sq * dist_sq * dist_sq)


def as_column(row):
    return jnp.broadcast_to(row, (CHUNK, row.shape[1])).T


def gather_kernel(form, chunks, count, pairs_ref, scale_ref, *rest):
    sources, rest = rest[:count], rest[count:]
    if form == "first":
        out_ref, sums_ref, table_out, table, dense, part, held, arrived, left = rest
    elif form == "own":
        mean_ref, out_ref, table, dense, part, arrived = rest
    else:
        mean_ref, *piece_refs, table, dense, part, held, arrived = rest
        out_ref = None
    block = part.shape[0]
    stride = -(-3 * chunks // 8) * 8
    residues = table.shape[0] // stride
    group = dense.shape[0] // chunks
    step = pl.program_id(0)

    @pl.when(step == 0)
    def _():
        if form == "own":
            copy = pltpu.make_async_copy(sources[0], table, arrived)
            copy.start()
            copy.wait()
            return
        copies = [
            pltpu.make_async_copy(ref.at[k], held.at[n, k], arrived.at[n, k])
            for k in range(3)
            for n, ref in enumerate(sources)
        ]
        for copy in copies:
            copy.start()
        for k in range(3):
            for n in range(count):
                copies[k * count + n].wait()
            for c in range(chunks):
                if form == "first":
                    plane = held[0, k, :, c * CHUNK : (c + 1) * CHUNK]
                else:
                    plane = held[c, k].astype(jnp.int32)
                table[pl.ds(k * chunks + c, residues, stride=stride), :] = plane
        if form == "first":
            pltpu.make_async_copy(table, table_out, left).start()

    if form != "first":
        part[...] = as_column(mean_ref[...])
    sublane = lax.broadcasted_iota(jnp.int32, (8, CHUNK), 0)
    scale = jnp.concatenate([scale_ref[...]] * (8 // chunks), axis=0)

    def squares(f):
        first = pl.multiple_of(pairs_ref[0, f], 8)
        second = pl.multiple_of(pairs_ref[1, f], 8)
        diff = (table[pl.ds(first, stride), :] - table[pl.ds(second, stride), :]).astype(jnp.float32)
        diff = diff * diff
        total = diff[0:8] + jnp.where(sublane < 4, diff[8:16], 0.0)
        return total + pltpu.roll(total, 4, 0)

    def one_group(g, out_ref):
        at = pl.multiple_of(g * group, group)
        for f in range(0, group, 2):
            base = step * block + at + f
            value = jnp.where(sublane < 4, squares(base), squares(base + 1))
            dense[pl.ds(f * chunks, 8), :] = switch(value, scale)
        for h in range(group // 16):
            here = pl.ds(pl.multiple_of(at + h * 16, 16), 16)
            total = jnp.zeros((16, CHUNK), jnp.float32)
            for c in range(chunks):
                contact = dense[pl.ds(h * 16 * chunks + c, 16, stride=chunks), :]
                lanes = slice(c * CHUNK, (c + 1) * CHUNK)
                if form == "first":
                    out_ref[here, lanes] = contact
                    total = total + contact
                elif form == "own":
                    out_ref[here, lanes] = (contact - part[here, :]).astype(jnp.bfloat16)
                else:
                    out_ref[c, here, :] = (contact - part[here, :]).astype(jnp.bfloat16)
            if form == "first":
                part[here, :] = total

    if form == "sent":
        for p, ref in enumerate(piece_refs):
            pl.when(step == p)(lambda ref=ref: pl.loop(0, block // group)(lambda g: one_group(g, ref)))
    else:
        pl.loop(0, block // group)(lambda g: one_group(g, out_ref))

    if form == "first":
        sums_ref[...] = jnp.sum(part[...].T, axis=0, keepdims=True)

        @pl.when(step == pl.num_programs(0) - 1)
        def _():
            pltpu.make_async_copy(table, table_out, left).wait()


def contacts(form, pairs, sources, scale, mean=None, block=512, group=32):
    feats = pairs.shape[1]
    chunks = scale.shape[0]
    stride = -(-3 * chunks // 8) * 8
    rows = sources[0].shape[0] if form == "own" else sources[0].shape[1] * stride
    row_spec = pl.BlockSpec((1, block), lambda n: (0, n))
    any_spec = pl.BlockSpec(memory_space=pl.ANY)
    in_specs = [pl.BlockSpec(memory_space=pltpu.SMEM), pl.BlockSpec((chunks, CHUNK), lambda n: (0, 0))]
    in_specs += [any_spec] * len(sources)
    args = [pairs * stride, scale, *sources]
    scratch = [
        pltpu.VMEM((rows, CHUNK), jnp.int32),
        pltpu.VMEM((group * chunks, CHUNK), jnp.float32),
        pltpu.VMEM((block, CHUNK), jnp.float32),
    ]
    if form == "sent":
        out_shape = [jax.ShapeDtypeStruct((chunks, block, CHUNK), jnp.bfloat16)] * (feats // block)
        out_specs = [pl.BlockSpec((chunks, block, CHUNK), lambda n: (0, 0, 0))] * (feats // block)
    else:
        dtype = jnp.bfloat16 if form == "own" else jnp.float32
        out_shape = jax.ShapeDtypeStruct((feats, chunks * CHUNK), dtype)
        out_specs = pl.BlockSpec((block, chunks * CHUNK), lambda n: (n, 0))
    if form == "own":
        scratch.append(pltpu.SemaphoreType.DMA)
    else:
        scratch.append(pltpu.VMEM((len(sources),) + sources[0].shape, sources[0].dtype))
        scratch.append(pltpu.SemaphoreType.DMA((len(sources), 3)))
    if form == "first":
        out_shape = [
            out_shape,
            jax.ShapeDtypeStruct((1, feats), jnp.float32),
            jax.ShapeDtypeStruct((rows, CHUNK), jnp.int32),
        ]
        out_specs = [out_specs, row_spec, any_spec]
        scratch.append(pltpu.SemaphoreType.DMA)
    else:
        in_specs.append(row_spec)
        args.append(mean)
    return pl.pallas_call(
        functools.partial(gather_kernel, form, chunks, len(sources)),
        out_shape=out_shape,
        grid=(feats // block,),
        in_specs=in_specs,
        out_specs=out_specs,
        scratch_shapes=scratch,
        compiler_params=pltpu.CompilerParams(vmem_limit_bytes=VMEM_LIMIT),
        cost_estimate=estimate(0.01),
    )(*args)


def center_kernel(raw_ref, mean_ref, out_ref):
    for c in range(raw_ref.shape[1] // CHUNK):
        frames = slice(c * CHUNK, (c + 1) * CHUNK)
        out_ref[frames, :] = (raw_ref[:, frames].T - mean_ref[...]).astype(jnp.bfloat16)


def center(raw, mean, block=512):
    feats, frames = raw.shape
    return pl.pallas_call(
        center_kernel,
        out_shape=jax.ShapeDtypeStruct((frames, feats), jnp.bfloat16),
        grid=(feats // block,),
        in_specs=[
            pl.BlockSpec((block, frames), lambda n: (n, 0)),
            pl.BlockSpec((1, block), lambda n: (0, n)),
        ],
        out_specs=pl.BlockSpec((frames, block), lambda n: (0, n)),
        compiler_params=pltpu.CompilerParams(vmem_limit_bytes=VMEM_LIMIT),
        cost_estimate=estimate(0.01),
    )(raw, mean)


def product_kernel(piece, place_ref, mask_ref, factors_ref, *rest):
    near_refs, rest = rest[: len(NEAR)], rest[len(NEAR) :]
    far_ref, cols_refs = rest[0], rest[1:9]
    same_ref, cross_ref, left, near_held, far_held, arrived = rest[-6:]
    feats = same_ref.shape[0]
    frames = cols_refs[0].shape[0]
    parts = frames // CHUNK
    me = place_ref[0]

    def put(d, c, value):
        j = me ^ d
        after = me ^ lax.rem(j + 1, 8)
        left[0:feats, d * frames + c * CHUNK : d * frames + (c + 1) * CHUNK] = value
        to = c + LAG // CHUNK
        if to < parts:
            at = d * frames + to * CHUNK
        else:
            at = pl.multiple_of(after * frames + (to - parts) * CHUNK, CHUNK)
        left[feats : 2 * feats, pl.ds(at, CHUNK)] = value * mask_ref[j, c].astype(jnp.bfloat16)

    @pl.when(pl.program_id(0) == 0)
    def _():
        copies = []
        for n, ref in enumerate(near_refs):
            start = piece * feats if ref.shape[0] > feats else 0
            copies.append(
                pltpu.make_async_copy(ref.at[pl.ds(start, feats), :], near_held.at[n], arrived.at[n])
            )
        for c in range(parts):
            copies.append(
                pltpu.make_async_copy(far_ref.at[c], far_held.at[c], arrived.at[len(NEAR) + c])
            )
        for copy in copies:
            copy.start()
        for n, d in enumerate(NEAR):
            copies[n].wait()
            for c in range(parts):
                put(d, c, near_held[n, :, c * CHUNK : (c + 1) * CHUNK])
        for c in range(parts):
            copies[len(NEAR) + c].wait()
            for i, d in enumerate(FAR):
                put(d, c, far_held[c, i])

    right = jnp.concatenate([ref[...] for ref in cols_refs], axis=0)
    same = jnp.dot(left[0:feats, :], right, preferred_element_type=jnp.float32)
    same_ref[...] = same * factors_ref[0]
    cross = jnp.dot(left[feats : 2 * feats, :], right, preferred_element_type=jnp.float32)
    cross_ref[...] = cross / factors_ref[1]


def products(place, mask, factors, piece, near, far, cols, outs=(), block=512):
    frames, feats = cols[0].shape
    row_feats = near[0].shape[0]
    rows = row_feats // PIECES
    out = jax.ShapeDtypeStruct((row_feats, feats), jnp.float32)
    any_spec = pl.BlockSpec(memory_space=pl.ANY)
    inputs = [mask, factors, *near, far, *cols, *outs]
    return pl.pallas_call(
        functools.partial(product_kernel, piece),
        out_shape=[out, out],
        grid_spec=pltpu.PrefetchScalarGridSpec(
            num_scalar_prefetch=1,
            grid=(feats // block,),
            in_specs=[
                pl.BlockSpec(mask.shape, lambda n, s: (0,) * mask.ndim),
                pl.BlockSpec(memory_space=pltpu.SMEM),
            ]
            + [any_spec] * (len(near) + 1)
            + [pl.BlockSpec((frames, block), lambda n, s: (0, n))] * 8
            + [any_spec] * len(outs),
            out_specs=[pl.BlockSpec((rows, block), lambda n, s: (piece, n))] * 2,
            scratch_shapes=[
                pltpu.VMEM((2 * rows, 8 * frames), jnp.bfloat16),
                pltpu.VMEM((len(near), rows, frames), jnp.bfloat16),
                pltpu.VMEM(far.shape, jnp.bfloat16),
                pltpu.SemaphoreType.DMA((len(near) + far.shape[0],)),
            ],
        ),
        input_output_aliases={len(inputs) - 1 + i: i for i in range(len(outs))},
        compiler_params=pltpu.CompilerParams(vmem_limit_bytes=VMEM_LIMIT),
        cost_estimate=estimate(0.01),
    )(place, *inputs)


def swap(x, bits):
    return lax.ppermute(x, "tm", [(i, i ^ bits) for i in range(8)])


def corner(along_x, along_y):
    even = lax.axis_index("tm") % 2 == 0
    forwarded = jnp.where(even, along_x, along_y)
    return lax.ppermute(forwarded, "tm", [(i, i ^ (2 if i % 2 else 4)) for i in range(8)])


def line_gather(x, count):
    shift = lambda s: [(i, (i + s) % count) for i in range(count)]
    return jnp.stack([x] + [lax.ppermute(x, "feat", shift(s)) for s in range(1, count)])


def together(*values):
    return lax.optimization_barrier(values)


def shards(coords, frame_scale, pairs, walker_lengths):
    tm_count = lax.axis_size("tm")
    feat_count = lax.axis_size("feat")
    frames_dev = coords.shape[0]
    feats = pairs.shape[1]
    frames_all = frames_dev * tm_count
    row_feats = feats * feat_count // tm_count
    parts = frames_dev // CHUNK
    tm = lax.axis_index("tm").astype(jnp.int32)
    z = lax.axis_index("feat").astype(jnp.int32)
    place = jnp.stack([tm, z])
    own_half = (tm % (feats // row_feats)) * row_feats

    coords_t = jnp.transpose(coords, (1, 2, 0))
    scale_own = frame_scale.reshape(parts, CHUNK)
    quarter = lax.dynamic_slice_in_dim(coords_t, z * CHUNK, CHUNK, axis=2).astype(jnp.int16)
    quarters = {3: swap(quarter, 3), 5: swap(quarter, 5)}

    raw, sums, table = contacts("first", pairs, [coords_t], scale_own)
    note = jnp.concatenate([sums, frame_scale.reshape(1, frames_dev)], axis=1)
    other = swap(note, 1)
    note = jnp.concatenate([sums + other[:, :feats], note[:, feats:], other[:, feats:]], axis=1)
    note, quarters = together(note, quarters)
    notes = [note] + [swap(note, d) for d in (2, 4, 6)]
    totals = notes[0][:, :feats]
    for other in notes[1:]:
        totals = totals + other[:, :feats]
    mean = totals / jnp.float32(frames_all)
    scales = [
        lax.dynamic_slice_in_dim(notes[d // 2], feats + d % 2 * frames_dev + z * CHUNK, CHUNK, axis=1)
        for d in range(8)
    ]
    scale_of = lambda *d: jnp.concatenate([scales[i] for i in d], axis=0)

    quarters, mean = together(quarters, mean)
    quarters[7] = corner(quarters[3], quarters[5])
    mine, mean = together(center(raw, mean), mean)
    cols = {0: mine, 2: swap(mine, 2), 4: swap(mine, 4)}
    facts = line_gather(jnp.concatenate([mean, pairs.astype(jnp.float32)], axis=0), feat_count)
    quarters[6] = swap(quarters[7], 1)

    def facts_of(i, start, count):
        back = (z - i * feat_count // tm_count) % feat_count
        return lax.dynamic_slice(facts, (back, 0, start), (1, 3, count))[0]

    row_facts = facts_of(tm, own_half, row_feats)
    out_facts = jnp.concatenate(
        [facts_of(tm ^ 2, own_half, row_feats), facts_of(tm ^ 4, own_half, row_feats), facts_of(tm, 0, feats)],
        axis=1,
    )
    row_facts, out_facts, scales = together(row_facts, out_facts, scales)
    row_mean, row_pairs = row_facts[0:1], row_facts[1:3].astype(jnp.int32)
    out_mean, out_pairs = out_facts[0:1], out_facts[1:3].astype(jnp.int32)

    row_pairs, mine, quarters = together(row_pairs, mine, quarters)
    cols[1] = swap(mine, 1)
    rows = row_feats // PIECES
    pieces = contacts("sent", row_pairs, [quarters[d] for d in FAR], scale_of(*FAR), row_mean, block=rows)
    far = [lax.all_gather(x, "feat", axis=0, tiled=False) for x in pieces]

    out_pairs, pieces, walker_lengths = together(out_pairs, pieces, walker_lengths)
    valid = walker_mask(walker_lengths, frames_all, frames_all)
    mask = valid.astype(jnp.float32).reshape(tm_count, parts, 1, CHUNK)
    npairs = jnp.sum(jnp.maximum(walker_lengths - LAG, 0)).astype(jnp.float32)
    factors = jnp.stack([jnp.float32(1.0 / frames_all), npairs])
    near_rows = contacts("own", out_pairs[:, :feats], [table], scale_own, out_mean[:, :feats])
    chip_pairs = out_pairs[:, feats:]
    cols, near_rows, mask, factors, chip_pairs = together(cols, near_rows, mask, factors, chip_pairs)
    cols[6] = corner(cols[2], cols[4])
    for d in (2, 4):
        cols[d + 1] = swap(cols[d], 1)
    chip_rows = contacts("own", chip_pairs, [table], scale_own, out_mean[:, feats:])
    chip_rows, cols, near_rows = together(chip_rows, cols, near_rows)

    cut = lambda x, start, count: lax.dynamic_slice_in_dim(x, start, count, axis=0)
    own = cut(chip_rows, own_half, row_feats)
    partner = swap(cut(chip_rows, row_feats - own_half, row_feats), 1)
    direct = [
        [swap(cut(near_rows, start + p * rows, rows), bit) for bit, start in ((2, 0), (4, row_feats))]
        for p in range(PIECES)
    ]
    cols[7] = swap(cols[6], 1)
    cols = [cols[d] for d in range(8)]
    outs = ()
    for p in range(PIECES):
        outs = products(place, mask, factors, p, [own, partner, *direct[p]], far[p], cols, outs)
    return outs


def solution(mesh):
    def run(coords, frame_scale, pairs, walker_lengths):
        tm_count, feat_count = mesh.shape["tm"], mesh.shape["feat"]
        frames_dev = coords.shape[0] // tm_count
        square = tm_count == 8 and feat_count == 4
        fits = square and frames_dev == 4 * CHUNK and pairs.shape[1] == 16 * 512
        return jax.shard_map(
            shards if fits else plain_shards,
            mesh=mesh,
            in_specs=(P("tm", None, None), P("tm"), P(None, "feat"), P()),
            out_specs=(P("tm", "feat"), P("tm", "feat")),
            check_vma=False,
        )(coords, frame_scale, pairs, walker_lengths)

    return run
```

```python
import functools

import jax
import jax.numpy as jnp
from jax import lax
from jax.experimental import pallas as pl
from jax.experimental.pallas import tpu as pltpu
from jax.sharding import PartitionSpec as P

LAG = 384
CHUNK = 128
VMEM_LIMIT = 56 * 1024 * 1024
NEAR = (0, 1, 2, 4)
FAR = (3, 5, 6, 7)
PIECES = 2


def contact_values(coords, frame_scale, pairs):
    frames_dev = coords.shape[0]
    residues = coords.shape[2]
    flat = coords.astype(jnp.float32).reshape(frames_dev * 3, residues)
    rows_iota = jnp.arange(residues, dtype=jnp.int32)[:, None]
    selector = (rows_iota == pairs[0][None, :]).astype(jnp.float32) - (
        rows_iota == pairs[1][None, :]
    ).astype(jnp.float32)
    diff = jnp.dot(
        flat, selector, precision=lax.Precision.HIGHEST, preferred_element_type=jnp.float32
    )
    diff = diff.reshape(frames_dev, 3, pairs.shape[1])
    squares = diff[:, 0] * diff[:, 0] + diff[:, 1] * diff[:, 1] + diff[:, 2] * diff[:, 2]
    dist_sq = (frame_scale * frame_scale)[:, None] * squares
    return 1.0 / (1.0 + dist_sq * dist_sq * dist_sq)


def walker_mask(walker_lengths, count, frames_all):
    ends = jnp.cumsum(walker_lengths)
    times = jnp.arange(count, dtype=jnp.int32)
    later = times + LAG
    own = jnp.sum((times[:, None] >= ends[None, :]).astype(jnp.int32), axis=1)
    ahead = jnp.sum((later[:, None] >= ends[None, :]).astype(jnp.int32), axis=1)
    return (own == ahead) & (later < frames_all)


def estimate(micros):
    return pl.CostEstimate(
        flops=int(micros * 1_000_000_000), bytes_accessed=int(micros * 3_690_000), transcendentals=0
    )


def contract(left, right):
    return lax.dot_general(
        left, right, (((0,), (0,)), ((), ())), preferred_element_type=jnp.float32
    )


def plain_shards(coords, frame_scale, pairs, walker_lengths):
    tm_count = lax.axis_size("tm")
    frames_dev = coords.shape[0]
    local_feats = pairs.shape[1]
    frames_all = frames_dev * tm_count
    contact = contact_values(coords, frame_scale, pairs)
    totals = lax.psum(jnp.sum(contact, axis=0), "tm")
    centered = (contact - totals / jnp.float32(frames_all)).astype(jnp.bfloat16)
    npairs = jnp.sum(jnp.maximum(walker_lengths - LAG, 0)).astype(jnp.float32)
    column_series = lax.all_gather(centered, "tm", axis=0, tiled=True)
    wide = lax.all_gather(centered, "feat", axis=1, tiled=True)
    row_series = lax.all_to_all(wide, "tm", split_axis=1, concat_axis=0, tiled=True)
    valid = walker_mask(walker_lengths, frames_all, frames_all)
    later = jnp.concatenate(
        [column_series[LAG:], jnp.zeros((LAG, local_feats), jnp.bfloat16)], axis=0
    )
    lagged = jnp.where(valid[:, None], later, jnp.zeros_like(later))
    same = contract(row_series, column_series)
    cross = contract(row_series, lagged)
    return (same / jnp.float32(frames_all), cross / npairs)


def switch(squares, scale):
    dist_sq = (scale * scale) * squares
    return 1.0 / (1.0 + dist_sq * dist_sq * dist_sq)


def as_column(row):
    return jnp.broadcast_to(row, (CHUNK, row.shape[1])).T


def gather_kernel(form, chunks, count, pairs_ref, scale_ref, *rest):
    sources, rest = rest[:count], rest[count:]
    if form == "first":
        out_ref, sums_ref, table_out, table, dense, part, held, arrived, left = rest
    elif form == "own":
        mean_ref, out_ref, table, dense, part, arrived = rest
    else:
        mean_ref, out_ref, table, dense, part, held, arrived = rest
    block = part.shape[0]
    stride = -(-3 * chunks // 8) * 8
    residues = table.shape[0] // stride
    group = dense.shape[0] // chunks
    step = pl.program_id(0)

    @pl.when(step == 0)
    def _():
        if form == "own":
            copy = pltpu.make_async_copy(sources[0], table, arrived)
            copy.start()
            copy.wait()
            return
        copies = [
            pltpu.make_async_copy(ref.at[k], held.at[n, k], arrived.at[n, k])
            for k in range(3)
            for n, ref in enumerate(sources)
        ]
        for copy in copies:
            copy.start()
        for k in range(3):
            for n in range(count):
                copies[k * count + n].wait()
            for c in range(chunks):
                if form == "first":
                    plane = held[0, k, :, c * CHUNK : (c + 1) * CHUNK]
                else:
                    plane = held[c, k].astype(jnp.int32)
                table[pl.ds(k * chunks + c, residues, stride=stride), :] = plane
        if form == "first":
            pltpu.make_async_copy(table, table_out, left).start()

    if form != "first":
        part[...] = as_column(mean_ref[...])
    sublane = lax.broadcasted_iota(jnp.int32, (8, CHUNK), 0)
    scale = jnp.concatenate([scale_ref[...]] * (8 // chunks), axis=0)

    def squares(f):
        first = pl.multiple_of(pairs_ref[0, f], 8)
        second = pl.multiple_of(pairs_ref[1, f], 8)
        diff = (table[pl.ds(first, stride), :] - table[pl.ds(second, stride), :]).astype(jnp.float32)
        diff = diff * diff
        total = diff[0:8] + jnp.where(sublane < 4, diff[8:16], 0.0)
        return total + pltpu.roll(total, 4, 0)

    @pl.loop(0, block // group)
    def _(g):
        at = pl.multiple_of(g * group, group)
        for f in range(0, group, 2):
            base = step * block + at + f
            value = jnp.where(sublane < 4, squares(base), squares(base + 1))
            dense[pl.ds(f * chunks, 8), :] = switch(value, scale)
        for h in range(group // 16):
            here = pl.ds(pl.multiple_of(at + h * 16, 16), 16)
            total = jnp.zeros((16, CHUNK), jnp.float32)
            for c in range(chunks):
                contact = dense[pl.ds(h * 16 * chunks + c, 16, stride=chunks), :]
                lanes = slice(c * CHUNK, (c + 1) * CHUNK)
                if form == "first":
                    out_ref[here, lanes] = contact
                    total = total + contact
                elif form == "own":
                    out_ref[here, lanes] = (contact - part[here, :]).astype(jnp.bfloat16)
                else:
                    out_ref[0, c, here, :] = (contact - part[here, :]).astype(jnp.bfloat16)
            if form == "first":
                part[here, :] = total

    if form == "first":
        sums_ref[...] = jnp.sum(part[...].T, axis=0, keepdims=True)

        @pl.when(step == pl.num_programs(0) - 1)
        def _():
            pltpu.make_async_copy(table, table_out, left).wait()


def contacts(form, pairs, sources, scale, mean=None, block=512, group=32):
    feats = pairs.shape[1]
    chunks = scale.shape[0]
    stride = -(-3 * chunks // 8) * 8
    rows = sources[0].shape[0] if form == "own" else sources[0].shape[1] * stride
    row_spec = pl.BlockSpec((1, block), lambda n: (0, n))
    any_spec = pl.BlockSpec(memory_space=pl.ANY)
    in_specs = [pl.BlockSpec(memory_space=pltpu.SMEM), pl.BlockSpec((chunks, CHUNK), lambda n: (0, 0))]
    in_specs += [any_spec] * len(sources)
    args = [pairs * stride, scale, *sources]
    scratch = [
        pltpu.VMEM((rows, CHUNK), jnp.int32),
        pltpu.VMEM((group * chunks, CHUNK), jnp.float32),
        pltpu.VMEM((block, CHUNK), jnp.float32),
    ]
    if form == "sent":
        out_shape = jax.ShapeDtypeStruct((feats // block, chunks, block, CHUNK), jnp.bfloat16)
        out_specs = pl.BlockSpec((1, chunks, block, CHUNK), lambda n: (n, 0, 0, 0))
    else:
        dtype = jnp.bfloat16 if form == "own" else jnp.float32
        out_shape = jax.ShapeDtypeStruct((feats, chunks * CHUNK), dtype)
        out_specs = pl.BlockSpec((block, chunks * CHUNK), lambda n: (n, 0))
    if form == "own":
        scratch.append(pltpu.SemaphoreType.DMA)
    else:
        scratch.append(pltpu.VMEM((len(sources),) + sources[0].shape, sources[0].dtype))
        scratch.append(pltpu.SemaphoreType.DMA((len(sources), 3)))
    if form == "first":
        out_shape = [
            out_shape,
            jax.ShapeDtypeStruct((1, feats), jnp.float32),
            jax.ShapeDtypeStruct((rows, CHUNK), jnp.int32),
        ]
        out_specs = [out_specs, row_spec, any_spec]
        scratch.append(pltpu.SemaphoreType.DMA)
    else:
        in_specs.append(row_spec)
        args.append(mean)
    return pl.pallas_call(
        functools.partial(gather_kernel, form, chunks, len(sources)),
        out_shape=out_shape,
        grid=(feats // block,),
        in_specs=in_specs,
        out_specs=out_specs,
        scratch_shapes=scratch,
        compiler_params=pltpu.CompilerParams(vmem_limit_bytes=VMEM_LIMIT),
        cost_estimate=estimate(0.01),
    )(*args)


def center_kernel(raw_ref, mean_ref, out_ref):
    for c in range(raw_ref.shape[1] // CHUNK):
        frames = slice(c * CHUNK, (c + 1) * CHUNK)
        out_ref[frames, :] = (raw_ref[:, frames].T - mean_ref[...]).astype(jnp.bfloat16)


def center(raw, mean, block=512):
    feats, frames = raw.shape
    return pl.pallas_call(
        center_kernel,
        out_shape=jax.ShapeDtypeStruct((frames, feats), jnp.bfloat16),
        grid=(feats // block,),
        in_specs=[
            pl.BlockSpec((block, frames), lambda n: (n, 0)),
            pl.BlockSpec((1, block), lambda n: (0, n)),
        ],
        out_specs=pl.BlockSpec((frames, block), lambda n: (0, n)),
        compiler_params=pltpu.CompilerParams(vmem_limit_bytes=VMEM_LIMIT),
        cost_estimate=estimate(0.01),
    )(raw, mean)


def product_kernel(piece, place_ref, mask_ref, factors_ref, *rest):
    near_refs, rest = rest[: len(NEAR)], rest[len(NEAR) :]
    far_refs, cols_refs = rest[:7], rest[7:15]
    same_ref, cross_ref, left, near_held, far_held, arrived = rest[-6:]
    feats = same_ref.shape[0]
    frames = cols_refs[0].shape[0]
    parts = frames // CHUNK
    me, z = place_ref[0], place_ref[1]

    def put(d, c, value):
        j = me ^ d
        after = me ^ lax.rem(j + 1, 8)
        mask = mask_ref[j, c].astype(jnp.bfloat16)
        at = pl.multiple_of(d * frames + c * CHUNK, CHUNK)
        left[0:feats, pl.ds(at, CHUNK)] = value
        to = c + LAG // CHUNK
        at = jnp.where(to < parts, d * frames + to * CHUNK, after * frames + (to - parts) * CHUNK)
        left[feats : 2 * feats, pl.ds(pl.multiple_of(at, CHUNK), CHUNK)] = value * mask

    @pl.when(pl.program_id(0) == 0)
    def _():
        copies = []
        for n, ref in enumerate(near_refs):
            start = piece * feats if ref.shape[0] > feats else 0
            copies.append(
                pltpu.make_async_copy(ref.at[pl.ds(start, feats), :], near_held.at[n], arrived.at[n])
            )
        for n, ref in enumerate(far_refs):
            source = ref.at[piece if ref.shape[0] > 1 else 0]
            copies.append(pltpu.make_async_copy(source, far_held.at[n], arrived.at[len(NEAR) + n]))
        for copy in copies:
            copy.start()
        for n, d in enumerate(NEAR):
            copies[n].wait()
            for c in range(parts):
                put(d, c, near_held[n, :, c * CHUNK : (c + 1) * CHUNK])
        for n in range(len(far_refs)):
            copies[len(NEAR) + n].wait()
            hop = (n + 1) // 2
            c = z - hop if n % 2 else z + hop

            @pl.when((c >= 0) & (c < parts))
            def _():
                for i, d in enumerate(FAR):
                    put(d, c, far_held[n, i])

    right = jnp.concatenate([ref[...] for ref in cols_refs], axis=0)
    same = jnp.dot(left[0:feats, :], right, preferred_element_type=jnp.float32)
    same_ref[...] = same * factors_ref[0]
    cross = jnp.dot(left[feats : 2 * feats, :], right, preferred_element_type=jnp.float32)
    cross_ref[...] = cross / factors_ref[1]


def products(place, mask, factors, piece, near, far, cols, outs=(), block=256):
    frames, feats = cols[0].shape
    row_feats = near[0].shape[0]
    rows = row_feats // PIECES
    out = jax.ShapeDtypeStruct((row_feats, feats), jnp.float32)
    any_spec = pl.BlockSpec(memory_space=pl.ANY)
    inputs = [mask, factors, *near, *far, *cols, *outs]
    return pl.pallas_call(
        functools.partial(product_kernel, piece),
        out_shape=[out, out],
        grid_spec=pltpu.PrefetchScalarGridSpec(
            num_scalar_prefetch=1,
            grid=(feats // block,),
            in_specs=[
                pl.BlockSpec(mask.shape, lambda n, s: (0,) * mask.ndim),
                pl.BlockSpec(memory_space=pltpu.SMEM),
            ]
            + [any_spec] * (len(near) + len(far))
            + [pl.BlockSpec((frames, block), lambda n, s: (0, n))] * 8
            + [any_spec] * len(outs),
            out_specs=[pl.BlockSpec((rows, block), lambda n, s: (piece, n))] * 2,
            scratch_shapes=[
                pltpu.VMEM((2 * rows, 8 * frames), jnp.bfloat16),
                pltpu.VMEM((len(near), rows, frames), jnp.bfloat16),
                pltpu.VMEM((len(far), *far[0].shape[1:]), jnp.bfloat16),
                pltpu.SemaphoreType.DMA((len(near) + len(far),)),
            ],
        ),
        input_output_aliases={len(inputs) - 1 + i: i for i in range(len(outs))},
        compiler_params=pltpu.CompilerParams(vmem_limit_bytes=VMEM_LIMIT),
        cost_estimate=estimate(0.01),
    )(place, *inputs)


def swap(x, bits):
    return lax.ppermute(x, "tm", [(i, i ^ bits) for i in range(8)])


def corner(along_x, along_y):
    even = lax.axis_index("tm") % 2 == 0
    forwarded = jnp.where(even, along_x, along_y)
    return lax.ppermute(forwarded, "tm", [(i, i ^ (2 if i % 2 else 4)) for i in range(8)])


def line_gather(x, count):
    shift = lambda s: [(i, (i + s) % count) for i in range(count)]
    return jnp.stack([x] + [lax.ppermute(x, "feat", shift(s)) for s in range(1, count)])


def line_hop(up, down, hop, count):
    up = lax.ppermute(up, "feat", [(i, i + 1) for i in range(hop - 1, count - 1)])
    down = lax.ppermute(down, "feat", [(i + 1, i) for i in range(count - hop)])
    return up, down


def together(*values):
    return lax.optimization_barrier(values)


def shards(coords, frame_scale, pairs, walker_lengths):
    tm_count = lax.axis_size("tm")
    feat_count = lax.axis_size("feat")
    frames_dev = coords.shape[0]
    feats = pairs.shape[1]
    frames_all = frames_dev * tm_count
    row_feats = feats * feat_count // tm_count
    parts = frames_dev // CHUNK
    tm = lax.axis_index("tm").astype(jnp.int32)
    z = lax.axis_index("feat").astype(jnp.int32)
    place = jnp.stack([tm, z])
    own_half = (tm % (feats // row_feats)) * row_feats

    coords_t = jnp.transpose(coords, (1, 2, 0))
    scale_own = frame_scale.reshape(parts, CHUNK)
    quarter = lax.dynamic_slice_in_dim(coords_t, z * CHUNK, CHUNK, axis=2).astype(jnp.int16)
    quarters = {3: swap(quarter, 3), 5: swap(quarter, 5)}

    raw, sums, table = contacts("first", pairs, [coords_t], scale_own)
    quarters, _ = together(quarters, sums)
    quarters[7] = corner(quarters[3], quarters[5])
    note = jnp.concatenate([sums, frame_scale.reshape(1, frames_dev)], axis=1)
    notes = [note] + [swap(note, d) for d in range(1, 8)]

    totals = notes[0][:, :feats]
    for other in notes[1:]:
        totals = totals + other[:, :feats]
    mean = totals / jnp.float32(frames_all)
    scales = [lax.dynamic_slice_in_dim(n, feats + z * CHUNK, CHUNK, axis=1) for n in notes]
    scale_of = lambda *d: jnp.concatenate([scales[i] for i in d], axis=0)

    facts = line_gather(jnp.concatenate([mean, pairs.astype(jnp.float32)], axis=0), feat_count)
    mine, facts, quarters = together(center(raw, mean), facts, quarters)
    cols = {0: mine, 2: swap(mine, 2), 4: swap(mine, 4)}
    quarters[6] = swap(quarters[7], 1)

    def facts_of(i, start, count):
        back = (z - i * feat_count // tm_count) % feat_count
        return lax.dynamic_slice(facts, (back, 0, start), (1, 3, count))[0]

    row_facts = facts_of(tm, own_half, row_feats)
    out_facts = jnp.concatenate(
        [facts_of(tm ^ 2, own_half, row_feats), facts_of(tm ^ 4, own_half, row_feats), facts_of(tm, 0, feats)],
        axis=1,
    )
    row_facts, out_facts, scales = together(row_facts, out_facts, scales)
    row_mean, row_pairs = row_facts[0:1], row_facts[1:3].astype(jnp.int32)
    out_mean, out_pairs = out_facts[0:1], out_facts[1:3].astype(jnp.int32)

    row_pairs, mine, quarters = together(row_pairs, mine, quarters)
    cols[1] = swap(mine, 1)
    mixed = contacts("sent", row_pairs, [quarters[d] for d in FAR], scale_of(*FAR), row_mean)

    out_pairs, mixed, walker_lengths = together(out_pairs, mixed, walker_lengths)
    up, down = line_hop(mixed, mixed, 1, feat_count)
    valid = walker_mask(walker_lengths, frames_all, frames_all)
    mask = valid.astype(jnp.float32).reshape(tm_count, parts, 1, CHUNK)
    npairs = jnp.sum(jnp.maximum(walker_lengths - LAG, 0)).astype(jnp.float32)
    factors = jnp.stack([jnp.float32(1.0 / frames_all), npairs])
    near_rows = contacts("own", out_pairs[:, :feats], [table], scale_own, out_mean[:, :feats])
    near_rows, mask, factors, up, down, cols = together(near_rows, mask, factors, up, down, cols)
    far = [mixed, up, down]

    cols[6] = corner(cols[2], cols[4])
    up, down = line_hop(up, down, 2, feat_count)
    for d in (2, 4):
        cols[d + 1] = swap(cols[d], 1)
    chip_pairs, _ = together(out_pairs[:, feats:], near_rows)
    chip_rows = contacts("own", chip_pairs, [table], scale_own, out_mean[:, feats:])
    chip_rows, near_rows, cols, up, down = together(chip_rows, near_rows, cols, up, down)
    far += [up, down]

    rows = row_feats // PIECES
    cut = lambda x, start, count: lax.dynamic_slice_in_dim(x, start, count, axis=0)
    own = cut(chip_rows, own_half, row_feats)
    cols[7] = swap(cols[6], 1)
    partner, cols = together(cut(chip_rows, row_feats - own_half, row_feats), cols)
    partner = swap(partner, 1)
    cols = [cols[d] for d in range(8)]
    arrived = []
    for p in range(PIECES):
        last = line_hop(up[p : p + 1], down[p : p + 1], 3, feat_count)
        sides = [swap(cut(near_rows, start + p * rows, rows), bit) for bit, start in ((2, 0), (4, row_feats))]
        if p < PIECES - 1:
            last, sides, up, down, near_rows = together(last, sides, up, down, near_rows)
        arrived.append((sides, last))
    outs = ()
    for p, (sides, last) in enumerate(arrived):
        outs = products(place, mask, factors, p, [own, partner, *sides], [*far, *last], cols, outs)
    return outs


def solution(mesh):
    def run(coords, frame_scale, pairs, walker_lengths):
        tm_count, feat_count = mesh.shape["tm"], mesh.shape["feat"]
        frames_dev = coords.shape[0] // tm_count
        square = tm_count == 8 and feat_count == 4
        fits = square and frames_dev == 4 * CHUNK and pairs.shape[1] == 16 * 512
        return jax.shard_map(
            shards if fits else plain_shards,
            mesh=mesh,
            in_specs=(P("tm", None, None), P("tm"), P(None, "feat"), P()),
            out_specs=(P("tm", "feat"), P("tm", "feat")),
            check_vma=False,
        )(coords, frame_scale, pairs, walker_lengths)

    return run
```

```python
import functools

import jax
import jax.numpy as jnp
from jax import lax
from jax.experimental import pallas as pl
from jax.experimental.pallas import tpu as pltpu
from jax.sharding import PartitionSpec as P

LAG = 384
CHUNK = 128
VMEM_LIMIT = 56 * 1024 * 1024
NEAR = (0, 1, 2, 4)
FAR = (3, 5, 6, 7)


def contact_values(coords, frame_scale, pairs):
    frames_dev = coords.shape[0]
    residues = coords.shape[2]
    flat = coords.astype(jnp.float32).reshape(frames_dev * 3, residues)
    rows_iota = jnp.arange(residues, dtype=jnp.int32)[:, None]
    selector = (rows_iota == pairs[0][None, :]).astype(jnp.float32) - (
        rows_iota == pairs[1][None, :]
    ).astype(jnp.float32)
    diff = jnp.dot(
        flat, selector, precision=lax.Precision.HIGHEST, preferred_element_type=jnp.float32
    )
    diff = diff.reshape(frames_dev, 3, pairs.shape[1])
    squares = diff[:, 0] * diff[:, 0] + diff[:, 1] * diff[:, 1] + diff[:, 2] * diff[:, 2]
    dist_sq = (frame_scale * frame_scale)[:, None] * squares
    return 1.0 / (1.0 + dist_sq * dist_sq * dist_sq)


def walker_mask(walker_lengths, count, frames_all):
    ends = jnp.cumsum(walker_lengths)
    times = jnp.arange(count, dtype=jnp.int32)
    later = times + LAG
    own = jnp.sum((times[:, None] >= ends[None, :]).astype(jnp.int32), axis=1)
    ahead = jnp.sum((later[:, None] >= ends[None, :]).astype(jnp.int32), axis=1)
    return (own == ahead) & (later < frames_all)


def estimate(micros):
    return pl.CostEstimate(
        flops=int(micros * 1_000_000_000), bytes_accessed=int(micros * 3_690_000), transcendentals=0
    )


def contract(left, right):
    return lax.dot_general(
        left, right, (((0,), (0,)), ((), ())), preferred_element_type=jnp.float32
    )


def plain_shards(coords, frame_scale, pairs, walker_lengths):
    tm_count = lax.axis_size("tm")
    frames_dev = coords.shape[0]
    local_feats = pairs.shape[1]
    frames_all = frames_dev * tm_count
    contact = contact_values(coords, frame_scale, pairs)
    totals = lax.psum(jnp.sum(contact, axis=0), "tm")
    centered = (contact - totals / jnp.float32(frames_all)).astype(jnp.bfloat16)
    npairs = jnp.sum(jnp.maximum(walker_lengths - LAG, 0)).astype(jnp.float32)
    column_series = lax.all_gather(centered, "tm", axis=0, tiled=True)
    wide = lax.all_gather(centered, "feat", axis=1, tiled=True)
    row_series = lax.all_to_all(wide, "tm", split_axis=1, concat_axis=0, tiled=True)
    valid = walker_mask(walker_lengths, frames_all, frames_all)
    later = jnp.concatenate(
        [column_series[LAG:], jnp.zeros((LAG, local_feats), jnp.bfloat16)], axis=0
    )
    lagged = jnp.where(valid[:, None], later, jnp.zeros_like(later))
    same = contract(row_series, column_series)
    cross = contract(row_series, lagged)
    return (same / jnp.float32(frames_all), cross / npairs)


def switch(squares, scale):
    dist_sq = (scale * scale) * squares
    return 1.0 / (1.0 + dist_sq * dist_sq * dist_sq)


def as_column(row):
    return jnp.broadcast_to(row, (CHUNK, row.shape[1])).T


def gather_kernel(form, chunks, count, pairs_ref, scale_ref, *rest):
    sources, rest = rest[:count], rest[count:]
    if form == "first":
        out_ref, sums_ref, table_out, table, dense, part, held, arrived, left = rest
    elif form == "own":
        mean_ref, out_ref, table, dense, part, arrived = rest
    else:
        mean_ref, out_ref, table, dense, part, held, arrived = rest
    block = part.shape[0]
    stride = -(-3 * chunks // 8) * 8
    residues = table.shape[0] // stride
    group = dense.shape[0] // chunks
    step = pl.program_id(0)

    @pl.when(step == 0)
    def _():
        if form == "own":
            copy = pltpu.make_async_copy(sources[0], table, arrived)
            copy.start()
            copy.wait()
            return
        copies = [
            pltpu.make_async_copy(ref.at[k], held.at[n, k], arrived.at[n, k])
            for k in range(3)
            for n, ref in enumerate(sources)
        ]
        for copy in copies:
            copy.start()
        for k in range(3):
            for n in range(count):
                copies[k * count + n].wait()
            for c in range(chunks):
                if form == "first":
                    plane = held[0, k, :, c * CHUNK : (c + 1) * CHUNK]
                else:
                    plane = held[c, k].astype(jnp.int32)
                table[pl.ds(k * chunks + c, residues, stride=stride), :] = plane
        if form == "first":
            pltpu.make_async_copy(table, table_out, left).start()

    if form != "first":
        part[...] = as_column(mean_ref[...])
    sublane = lax.broadcasted_iota(jnp.int32, (8, CHUNK), 0)
    scale = jnp.concatenate([scale_ref[...]] * (8 // chunks), axis=0)

    def squares(f):
        first = pl.multiple_of(pairs_ref[0, f], 8)
        second = pl.multiple_of(pairs_ref[1, f], 8)
        diff = (table[pl.ds(first, stride), :] - table[pl.ds(second, stride), :]).astype(jnp.float32)
        diff = diff * diff
        total = diff[0:8] + jnp.where(sublane < 4, diff[8:16], 0.0)
        return total + pltpu.roll(total, 4, 0)

    @pl.loop(0, block // group)
    def _(g):
        at = pl.multiple_of(g * group, group)
        for f in range(0, group, 2):
            base = step * block + at + f
            value = jnp.where(sublane < 4, squares(base), squares(base + 1))
            dense[pl.ds(f * chunks, 8), :] = switch(value, scale)
        for h in range(group // 16):
            here = pl.ds(pl.multiple_of(at + h * 16, 16), 16)
            total = jnp.zeros((16, CHUNK), jnp.float32)
            for c in range(chunks):
                contact = dense[pl.ds(h * 16 * chunks + c, 16, stride=chunks), :]
                lanes = slice(c * CHUNK, (c + 1) * CHUNK)
                if form == "first":
                    out_ref[here, lanes] = contact
                    total = total + contact
                elif form == "own":
                    out_ref[here, lanes] = (contact - part[here, :]).astype(jnp.bfloat16)
                else:
                    out_ref[c, here, :] = (contact - part[here, :]).astype(jnp.bfloat16)
            if form == "first":
                part[here, :] = total

    if form == "first":
        sums_ref[...] = jnp.sum(part[...].T, axis=0, keepdims=True)

        @pl.when(step == pl.num_programs(0) - 1)
        def _():
            pltpu.make_async_copy(table, table_out, left).wait()


def contacts(form, pairs, sources, scale, mean=None, block=512, group=32):
    feats = pairs.shape[1]
    chunks = scale.shape[0]
    stride = -(-3 * chunks // 8) * 8
    rows = sources[0].shape[0] if form == "own" else sources[0].shape[1] * stride
    row_spec = pl.BlockSpec((1, block), lambda n: (0, n))
    any_spec = pl.BlockSpec(memory_space=pl.ANY)
    in_specs = [pl.BlockSpec(memory_space=pltpu.SMEM), pl.BlockSpec((chunks, CHUNK), lambda n: (0, 0))]
    in_specs += [any_spec] * len(sources)
    args = [pairs * stride, scale, *sources]
    scratch = [
        pltpu.VMEM((rows, CHUNK), jnp.int32),
        pltpu.VMEM((group * chunks, CHUNK), jnp.float32),
        pltpu.VMEM((block, CHUNK), jnp.float32),
    ]
    if form == "sent":
        out_shape = jax.ShapeDtypeStruct((chunks, feats, CHUNK), jnp.bfloat16)
        out_specs = pl.BlockSpec((chunks, block, CHUNK), lambda n: (0, n, 0))
    else:
        dtype = jnp.bfloat16 if form == "own" else jnp.float32
        out_shape = jax.ShapeDtypeStruct((feats, chunks * CHUNK), dtype)
        out_specs = pl.BlockSpec((block, chunks * CHUNK), lambda n: (n, 0))
    if form == "own":
        scratch.append(pltpu.SemaphoreType.DMA)
    else:
        scratch.append(pltpu.VMEM((len(sources),) + sources[0].shape, sources[0].dtype))
        scratch.append(pltpu.SemaphoreType.DMA((len(sources), 3)))
    if form == "first":
        out_shape = [
            out_shape,
            jax.ShapeDtypeStruct((1, feats), jnp.float32),
            jax.ShapeDtypeStruct((rows, CHUNK), jnp.int32),
        ]
        out_specs = [out_specs, row_spec, any_spec]
        scratch.append(pltpu.SemaphoreType.DMA)
    else:
        in_specs.append(row_spec)
        args.append(mean)
    return pl.pallas_call(
        functools.partial(gather_kernel, form, chunks, len(sources)),
        out_shape=out_shape,
        grid=(feats // block,),
        in_specs=in_specs,
        out_specs=out_specs,
        scratch_shapes=scratch,
        compiler_params=pltpu.CompilerParams(vmem_limit_bytes=VMEM_LIMIT),
        cost_estimate=estimate(0.01),
    )(*args)


def center_kernel(raw_ref, mean_ref, out_ref):
    for c in range(raw_ref.shape[1] // CHUNK):
        frames = slice(c * CHUNK, (c + 1) * CHUNK)
        out_ref[frames, :] = (raw_ref[:, frames].T - mean_ref[...]).astype(jnp.bfloat16)


def center(raw, mean, block=512):
    feats, frames = raw.shape
    return pl.pallas_call(
        center_kernel,
        out_shape=jax.ShapeDtypeStruct((frames, feats), jnp.bfloat16),
        grid=(feats // block,),
        in_specs=[
            pl.BlockSpec((block, frames), lambda n: (n, 0)),
            pl.BlockSpec((1, block), lambda n: (0, n)),
        ],
        out_specs=pl.BlockSpec((frames, block), lambda n: (0, n)),
        compiler_params=pltpu.CompilerParams(vmem_limit_bytes=VMEM_LIMIT),
        cost_estimate=estimate(0.01),
    )(raw, mean)


def product_kernel(place_ref, mask_ref, factors_ref, *rest):
    near_refs, rest = rest[: len(NEAR)], rest[len(NEAR) :]
    far_refs, cols_refs = rest[:7], rest[7:15]
    same_ref, cross_ref, left, near_held, far_held, arrived = rest[15:]
    feats = same_ref.shape[0]
    frames = cols_refs[0].shape[0]
    parts = frames // CHUNK
    me, z = place_ref[0], place_ref[1]

    def slot_of(d):
        crossed = (d >= 2) & (d <= 5) & ((d & 1) != (me & 1))
        return jnp.where(crossed, 6 + 2 * (d & 1) - d, d)

    def put(d, c, value):
        j = me ^ d
        after = slot_of(me ^ lax.rem(j + 1, 8))
        mask = mask_ref[j, c].astype(jnp.bfloat16)
        own = slot_of(jnp.int32(d)) * frames
        left[0:feats, pl.ds(pl.multiple_of(own + c * CHUNK, CHUNK), CHUNK)] = value
        to = c + LAG // CHUNK
        at = jnp.where(to < parts, own + to * CHUNK, after * frames + (to - parts) * CHUNK)
        left[feats : 2 * feats, pl.ds(pl.multiple_of(at, CHUNK), CHUNK)] = value * mask

    @pl.when(pl.program_id(0) == 0)
    def _():
        copies = [
            pltpu.make_async_copy(ref, near_held.at[n], arrived.at[n]) for n, ref in enumerate(near_refs)
        ]
        copies += [
            pltpu.make_async_copy(ref, far_held.at[n], arrived.at[len(NEAR) + n])
            for n, ref in enumerate(far_refs)
        ]
        for copy in copies:
            copy.start()
        for n, d in enumerate(NEAR):
            copies[n].wait()
            for c in range(parts):
                put(d, c, near_held[n, :, c * CHUNK : (c + 1) * CHUNK])
        for n in range(len(far_refs)):
            copies[len(NEAR) + n].wait()
            hop = (n + 1) // 2
            c = z - hop if n % 2 else z + hop

            @pl.when((c >= 0) & (c < parts))
            def _():
                for i, d in enumerate(FAR):
                    put(d, c, far_held[n, i])

    right = jnp.concatenate([ref[...] for ref in cols_refs], axis=0)
    for m in range(0, feats, 512):
        here = slice(m, m + 512)
        same = jnp.dot(left[here, :], right, preferred_element_type=jnp.float32)
        same_ref[here, :] = same * factors_ref[0]
    for m in range(0, feats, 512):
        here = slice(m, m + 512)
        cross = jnp.dot(left[feats + m : feats + m + 512, :], right, preferred_element_type=jnp.float32)
        cross_ref[here, :] = cross / factors_ref[1]


def products(place, mask, factors, near, far, cols, block=256):
    frames, feats = cols[0].shape
    rows = near[0].shape[0]
    out = jax.ShapeDtypeStruct((rows, feats), jnp.float32)
    inputs = [mask, factors, *near, *far, *cols]
    return pl.pallas_call(
        product_kernel,
        out_shape=[out, out],
        grid_spec=pltpu.PrefetchScalarGridSpec(
            num_scalar_prefetch=1,
            grid=(feats // block,),
            in_specs=[
                pl.BlockSpec(mask.shape, lambda n, s: (0,) * mask.ndim),
                pl.BlockSpec(memory_space=pltpu.SMEM),
            ]
            + [pl.BlockSpec(memory_space=pl.ANY)] * (len(near) + len(far))
            + [pl.BlockSpec((frames, block), lambda n, s: (0, n))] * 8,
            out_specs=[pl.BlockSpec((rows, block), lambda n, s: (0, n))] * 2,
            scratch_shapes=[
                pltpu.VMEM((2 * rows, 8 * frames), jnp.bfloat16),
                pltpu.VMEM((len(near),) + near[0].shape, jnp.bfloat16),
                pltpu.VMEM((len(far),) + far[0].shape, jnp.bfloat16),
                pltpu.SemaphoreType.DMA((len(near) + len(far),)),
            ],
        ),
        compiler_params=pltpu.CompilerParams(vmem_limit_bytes=VMEM_LIMIT),
        cost_estimate=estimate(0.01),
    )(place, *inputs)


def swap(x, bits):
    return lax.ppermute(x, "tm", [(i, i ^ bits) for i in range(8)])


def swap_by_parity(x, even, odd):
    return lax.ppermute(x, "tm", [(i, i ^ (odd if i % 2 else even)) for i in range(8)])


def corner(along_x, along_y):
    even = lax.axis_index("tm") % 2 == 0
    return swap_by_parity(jnp.where(even, along_x, along_y), 4, 2)


def line_gather(x, count):
    shift = lambda s: [(i, (i + s) % count) for i in range(count)]
    return jnp.stack([x] + [lax.ppermute(x, "feat", shift(s)) for s in range(1, count)])


def line_hop(up, down, hop, count):
    up = lax.ppermute(up, "feat", [(i, i + 1) for i in range(hop - 1, count - 1)])
    down = lax.ppermute(down, "feat", [(i + 1, i) for i in range(count - hop)])
    return up, down


def together(*values):
    return lax.optimization_barrier(values)


def shards(coords, frame_scale, pairs, walker_lengths):
    tm_count = lax.axis_size("tm")
    feat_count = lax.axis_size("feat")
    frames_dev = coords.shape[0]
    feats = pairs.shape[1]
    frames_all = frames_dev * tm_count
    row_feats = feats * feat_count // tm_count
    parts = frames_dev // CHUNK
    tm = lax.axis_index("tm").astype(jnp.int32)
    z = lax.axis_index("feat").astype(jnp.int32)
    place = jnp.stack([tm, z])
    own_half = (tm % (feats // row_feats)) * row_feats

    coords_t = jnp.transpose(coords, (1, 2, 0))
    scale_own = frame_scale.reshape(parts, CHUNK)
    quarter = lax.dynamic_slice_in_dim(coords_t, z * CHUNK, CHUNK, axis=2).astype(jnp.int16)
    quarters = {3: swap(quarter, 3), 5: swap(quarter, 5)}

    raw, sums, table = contacts("first", pairs, [coords_t], scale_own)
    quarters, _ = together(quarters, sums)
    quarters[7] = corner(quarters[3], quarters[5])
    note = jnp.concatenate([sums, frame_scale.reshape(1, frames_dev)], axis=1)
    notes = [note] + [swap(note, d) for d in range(1, 8)]

    totals = notes[0][:, :feats]
    for other in notes[1:]:
        totals = totals + other[:, :feats]
    mean = totals / jnp.float32(frames_all)
    scales = [lax.dynamic_slice_in_dim(n, feats + z * CHUNK, CHUNK, axis=1) for n in notes]
    scale_of = lambda *d: jnp.concatenate([scales[i] for i in d], axis=0)

    facts = line_gather(jnp.concatenate([mean, pairs.astype(jnp.float32)], axis=0), feat_count)
    mine, facts, quarters = together(center(raw, mean), facts, quarters)
    cols = [mine, None, swap_by_parity(mine, 2, 4), None, swap_by_parity(mine, 4, 2)]
    quarters[6] = swap(quarters[7], 1)

    def facts_of(i, start, count):
        back = (z - i * feat_count // tm_count) % feat_count
        return lax.dynamic_slice(facts, (back, 0, start), (1, 3, count))[0]

    row_facts = facts_of(tm, own_half, row_feats)
    out_facts = jnp.concatenate(
        [facts_of(tm ^ 2, own_half, row_feats), facts_of(tm ^ 4, own_half, row_feats), facts_of(tm, 0, feats)],
        axis=1,
    )
    row_facts, out_facts, scales = together(row_facts, out_facts, scales)
    row_mean, row_pairs = row_facts[0:1], row_facts[1:3].astype(jnp.int32)
    out_mean, out_pairs = out_facts[0:1], out_facts[1:3].astype(jnp.int32)

    row_pairs, mine, quarters = together(row_pairs, mine, quarters)
    cols[1] = swap(mine, 1)
    mixed = contacts("sent", row_pairs, [quarters[d] for d in FAR], scale_of(*FAR), row_mean)

    out_pairs, mixed, walker_lengths = together(out_pairs, mixed, walker_lengths)
    up, down = line_hop(mixed, mixed, 1, feat_count)
    valid = walker_mask(walker_lengths, frames_all, frames_all)
    mask = valid.astype(jnp.float32).reshape(tm_count, parts, 1, CHUNK)
    npairs = jnp.sum(jnp.maximum(walker_lengths - LAG, 0)).astype(jnp.float32)
    factors = jnp.stack([jnp.float32(1.0 / frames_all), npairs])
    near_rows = contacts("own", out_pairs[:, :feats], [table], scale_own, out_mean[:, :feats])
    near_x, near_y = near_rows[:row_feats], near_rows[row_feats:]
    near_x, near_y, mask, factors, up, down, cols = together(near_x, near_y, mask, factors, up, down, cols)
    far = [mixed, up, down]

    across = swap_by_parity(cols[2], 4, 2)
    up, down = line_hop(up, down, 2, feat_count)
    cols[3] = swap(cols[2], 1)
    their_last = swap(cols[4], 1)
    chip_pairs, _ = together(out_pairs[:, feats:], near_x)
    chip_rows = contacts("own", chip_pairs, [table], scale_own, out_mean[:, feats:])
    cols += [their_last, across]
    chip_rows, near_x, near_y, cols, up, down = together(chip_rows, near_x, near_y, cols, up, down)
    far += [up, down, *line_hop(up, down, 3, feat_count)]

    cut = lambda x, start: lax.dynamic_slice_in_dim(x, start, row_feats, axis=0)
    near_x, near_y = swap(near_x, 2), swap(near_y, 4)
    cols.append(swap(cols[6], 1))
    partner, cols = together(cut(chip_rows, row_feats - own_half), cols)
    near = [cut(chip_rows, own_half), swap(partner, 1), near_x, near_y]
    return products(place, mask, factors, near, far, cols)


def solution(mesh):
    def run(coords, frame_scale, pairs, walker_lengths):
        tm_count, feat_count = mesh.shape["tm"], mesh.shape["feat"]
        frames_dev = coords.shape[0] // tm_count
        square = tm_count == 8 and feat_count == 4
        fits = square and frames_dev == 4 * CHUNK and pairs.shape[1] == 16 * 512
        return jax.shard_map(
            shards if fits else plain_shards,
            mesh=mesh,
            in_specs=(P("tm", None, None), P("tm"), P(None, "feat"), P()),
            out_specs=(P("tm", "feat"), P("tm", "feat")),
            check_vma=False,
        )(coords, frame_scale, pairs, walker_lengths)

    return run
```

```python
import functools

import jax
import jax.numpy as jnp
from jax import lax
from jax.experimental import pallas as pl
from jax.experimental.pallas import tpu as pltpu
from jax.sharding import PartitionSpec as P

LAG = 384
CHUNK = 128
VMEM_LIMIT = 56 * 1024 * 1024
NEAR = (0, 1, 2, 4)
FAR = (3, 5, 6, 7)
TABLE_ROWS = 16


def contact_values(coords, frame_scale, pairs):
    frames_dev = coords.shape[0]
    residues = coords.shape[2]
    flat = coords.astype(jnp.float32).reshape(frames_dev * 3, residues)
    rows_iota = jnp.arange(residues, dtype=jnp.int32)[:, None]
    selector = (rows_iota == pairs[0][None, :]).astype(jnp.float32) - (
        rows_iota == pairs[1][None, :]
    ).astype(jnp.float32)
    diff = jnp.dot(
        flat, selector, precision=lax.Precision.HIGHEST, preferred_element_type=jnp.float32
    )
    diff = diff.reshape(frames_dev, 3, pairs.shape[1])
    squares = diff[:, 0] * diff[:, 0] + diff[:, 1] * diff[:, 1] + diff[:, 2] * diff[:, 2]
    dist_sq = (frame_scale * frame_scale)[:, None] * squares
    return 1.0 / (1.0 + dist_sq * dist_sq * dist_sq)


def walker_mask(walker_lengths, count, frames_all):
    ends = jnp.cumsum(walker_lengths)
    times = jnp.arange(count, dtype=jnp.int32)
    later = times + LAG
    own = jnp.sum((times[:, None] >= ends[None, :]).astype(jnp.int32), axis=1)
    ahead = jnp.sum((later[:, None] >= ends[None, :]).astype(jnp.int32), axis=1)
    return (own == ahead) & (later < frames_all)


def estimate(micros):
    return pl.CostEstimate(
        flops=int(micros * 1_000_000_000), bytes_accessed=int(micros * 3_690_000), transcendentals=0
    )


def contract(left, right):
    return lax.dot_general(
        left, right, (((0,), (0,)), ((), ())), preferred_element_type=jnp.float32
    )


def plain_shards(coords, frame_scale, pairs, walker_lengths):
    tm_count = lax.axis_size("tm")
    frames_dev = coords.shape[0]
    local_feats = pairs.shape[1]
    frames_all = frames_dev * tm_count
    contact = contact_values(coords, frame_scale, pairs)
    totals = lax.psum(jnp.sum(contact, axis=0), "tm")
    centered = (contact - totals / jnp.float32(frames_all)).astype(jnp.bfloat16)
    npairs = jnp.sum(jnp.maximum(walker_lengths - LAG, 0)).astype(jnp.float32)
    column_series = lax.all_gather(centered, "tm", axis=0, tiled=True)
    wide = lax.all_gather(centered, "feat", axis=1, tiled=True)
    row_series = lax.all_to_all(wide, "tm", split_axis=1, concat_axis=0, tiled=True)
    valid = walker_mask(walker_lengths, frames_all, frames_all)
    later = jnp.concatenate(
        [column_series[LAG:], jnp.zeros((LAG, local_feats), jnp.bfloat16)], axis=0
    )
    lagged = jnp.where(valid[:, None], later, jnp.zeros_like(later))
    same = contract(row_series, column_series)
    cross = contract(row_series, lagged)
    return (same / jnp.float32(frames_all), cross / npairs)


def switch(squares, scale):
    dist_sq = (scale * scale) * squares
    return 1.0 / (1.0 + dist_sq * dist_sq * dist_sq)


def as_column(row):
    return jnp.broadcast_to(row, (CHUNK, row.shape[1])).T


def gather_kernel(form, chunks, count, pairs_ref, scale_ref, *rest):
    sources, rest = rest[:count], rest[count:]
    if form == "first":
        out_ref, sums_ref, table_out, table, dense, part, held, arrived, left = rest
    elif form == "own":
        mean_ref, out_ref, table, dense, part, arrived = rest
    else:
        mean_ref, out_ref, table, dense, part, held, arrived = rest
    block = part.shape[0]
    stride = -(-3 * chunks // 8) * 8
    residues = table.shape[0] // stride
    group = dense.shape[0] // chunks
    step = pl.program_id(0)

    @pl.when(step == 0)
    def _():
        if form == "own":
            copy = pltpu.make_async_copy(sources[0], table, arrived)
            copy.start()
            copy.wait()
            return
        copies = [
            pltpu.make_async_copy(ref.at[k], held.at[n, k], arrived.at[n, k])
            for k in range(3)
            for n, ref in enumerate(sources)
        ]
        for copy in copies:
            copy.start()
        for k in range(3):
            for n in range(count):
                copies[k * count + n].wait()
            for c in range(chunks):
                if form == "first":
                    plane = held[0, k, :, c * CHUNK : (c + 1) * CHUNK]
                else:
                    plane = held[c, k].astype(jnp.int32)
                table[pl.ds(k * chunks + c, residues, stride=stride), :] = plane
        if form == "first":
            pltpu.make_async_copy(table, table_out, left).start()

    if form != "first":
        part[...] = as_column(mean_ref[...])
    sublane = lax.broadcasted_iota(jnp.int32, (8, CHUNK), 0)
    scale = jnp.concatenate([scale_ref[...]] * (8 // chunks), axis=0)

    def squares(f):
        first = pl.multiple_of(pairs_ref[0, f], 8)
        second = pl.multiple_of(pairs_ref[1, f], 8)
        diff = (table[pl.ds(first, stride), :] - table[pl.ds(second, stride), :]).astype(jnp.float32)
        diff = diff * diff
        total = diff[0:8] + jnp.where(sublane < 4, diff[8:16], 0.0)
        return total + pltpu.roll(total, 4, 0)

    @pl.loop(0, block // group)
    def _(g):
        at = pl.multiple_of(g * group, group)
        for f in range(0, group, 2):
            base = step * block + at + f
            value = jnp.where(sublane < 4, squares(base), squares(base + 1))
            dense[pl.ds(f * chunks, 8), :] = switch(value, scale)
        for h in range(group // 16):
            here = pl.ds(pl.multiple_of(at + h * 16, 16), 16)
            total = jnp.zeros((16, CHUNK), jnp.float32)
            for c in range(chunks):
                contact = dense[pl.ds(h * 16 * chunks + c, 16, stride=chunks), :]
                lanes = slice(c * CHUNK, (c + 1) * CHUNK)
                if form == "first":
                    out_ref[here, lanes] = contact
                    total = total + contact
                elif form == "own":
                    out_ref[here, lanes] = (contact - part[here, :]).astype(jnp.bfloat16)
                else:
                    out_ref[c, here, :] = (contact - part[here, :]).astype(jnp.bfloat16)
            if form == "first":
                part[here, :] = total

    if form == "first":
        sums_ref[...] = jnp.sum(part[...].T, axis=0, keepdims=True)

        @pl.when(step == pl.num_programs(0) - 1)
        def _():
            pltpu.make_async_copy(table, table_out, left).wait()


def contacts(form, pairs, sources, scale, mean=None, block=512, group=128):
    feats = pairs.shape[1]
    chunks = scale.shape[0]
    stride = -(-3 * chunks // 8) * 8
    rows = sources[0].shape[0] if form == "own" else sources[0].shape[1] * stride
    row_spec = pl.BlockSpec((1, block), lambda n: (0, n))
    any_spec = pl.BlockSpec(memory_space=pl.ANY)
    in_specs = [pl.BlockSpec(memory_space=pltpu.SMEM), pl.BlockSpec((chunks, CHUNK), lambda n: (0, 0))]
    in_specs += [any_spec] * len(sources)
    args = [pairs, scale, *sources]
    scratch = [
        pltpu.VMEM((rows, CHUNK), jnp.int32),
        pltpu.VMEM((group * chunks, CHUNK), jnp.float32),
        pltpu.VMEM((block, CHUNK), jnp.float32),
    ]
    if form == "sent":
        out_shape = jax.ShapeDtypeStruct((chunks, feats, CHUNK), jnp.bfloat16)
        out_specs = pl.BlockSpec((chunks, block, CHUNK), lambda n: (0, n, 0))
    else:
        dtype = jnp.bfloat16 if form == "own" else jnp.float32
        out_shape = jax.ShapeDtypeStruct((feats, chunks * CHUNK), dtype)
        out_specs = pl.BlockSpec((block, chunks * CHUNK), lambda n: (n, 0))
    if form == "own":
        scratch.append(pltpu.SemaphoreType.DMA)
    else:
        scratch.append(pltpu.VMEM((len(sources),) + sources[0].shape, sources[0].dtype))
        scratch.append(pltpu.SemaphoreType.DMA((len(sources), 3)))
    if form == "first":
        out_shape = [
            out_shape,
            jax.ShapeDtypeStruct((1, feats), jnp.float32),
            jax.ShapeDtypeStruct((rows, CHUNK), jnp.int32),
        ]
        out_specs = [out_specs, row_spec, any_spec]
        scratch.append(pltpu.SemaphoreType.DMA)
    else:
        in_specs.append(row_spec)
        args.append(mean)
    return pl.pallas_call(
        functools.partial(gather_kernel, form, chunks, len(sources)),
        out_shape=out_shape,
        grid=(feats // block,),
        in_specs=in_specs,
        out_specs=out_specs,
        scratch_shapes=scratch,
        compiler_params=pltpu.CompilerParams(vmem_limit_bytes=VMEM_LIMIT),
        cost_estimate=estimate(0.01),
    )(*args)


def center_kernel(raw_ref, mean_ref, out_ref):
    for c in range(raw_ref.shape[1] // CHUNK):
        frames = slice(c * CHUNK, (c + 1) * CHUNK)
        out_ref[frames, :] = (raw_ref[:, frames].T - mean_ref[...]).astype(jnp.bfloat16)


def center(raw, mean, block=512):
    feats, frames = raw.shape
    return pl.pallas_call(
        center_kernel,
        out_shape=jax.ShapeDtypeStruct((frames, feats), jnp.bfloat16),
        grid=(feats // block,),
        in_specs=[
            pl.BlockSpec((block, frames), lambda n: (n, 0)),
            pl.BlockSpec((1, block), lambda n: (0, n)),
        ],
        out_specs=pl.BlockSpec((frames, block), lambda n: (0, n)),
        compiler_params=pltpu.CompilerParams(vmem_limit_bytes=VMEM_LIMIT),
        cost_estimate=estimate(0.01),
    )(raw, mean)


def product_kernel(place_ref, mask_ref, factors_ref, *rest):
    near_refs, rest = rest[: len(NEAR)], rest[len(NEAR) :]
    far_refs, cols_refs = rest[:7], rest[7:15]
    same_ref, cross_ref, left, near_held, far_held, arrived = rest[15:]
    feats = same_ref.shape[0]
    frames = cols_refs[0].shape[0]
    parts = frames // CHUNK
    me, z = place_ref[0], place_ref[1]

    def slot_of(d):
        crossed = (d >= 2) & (d <= 5) & ((d & 1) != (me & 1))
        return jnp.where(crossed, 6 + 2 * (d & 1) - d, d)

    def put(d, c, value):
        j = me ^ d
        after = slot_of(me ^ lax.rem(j + 1, 8))
        mask = mask_ref[j, c].astype(jnp.bfloat16)
        own = slot_of(jnp.int32(d)) * frames
        left[0:feats, pl.ds(pl.multiple_of(own + c * CHUNK, CHUNK), CHUNK)] = value
        to = c + LAG // CHUNK
        at = jnp.where(to < parts, own + to * CHUNK, after * frames + (to - parts) * CHUNK)
        left[feats : 2 * feats, pl.ds(pl.multiple_of(at, CHUNK), CHUNK)] = value * mask

    @pl.when(pl.program_id(0) == 0)
    def _():
        copies = [
            pltpu.make_async_copy(ref, near_held.at[n], arrived.at[n]) for n, ref in enumerate(near_refs)
        ]
        copies += [
            pltpu.make_async_copy(ref, far_held.at[n], arrived.at[len(NEAR) + n])
            for n, ref in enumerate(far_refs)
        ]
        for copy in copies:
            copy.start()
        for n, d in enumerate(NEAR):
            copies[n].wait()
            for c in range(parts):
                put(d, c, near_held[n, :, c * CHUNK : (c + 1) * CHUNK])
        for n in range(len(far_refs)):
            copies[len(NEAR) + n].wait()
            hop = (n + 1) // 2
            c = z - hop if n % 2 else z + hop

            @pl.when((c >= 0) & (c < parts))
            def _():
                for i, d in enumerate(FAR):
                    put(d, c, far_held[n, i])

    right = jnp.concatenate([ref[...] for ref in cols_refs], axis=0)
    for m in range(0, feats, 512):
        here = slice(m, m + 512)
        same = jnp.dot(left[here, :], right, preferred_element_type=jnp.float32)
        same_ref[here, :] = same * factors_ref[0]
    for m in range(0, feats, 512):
        here = slice(m, m + 512)
        cross = jnp.dot(left[feats + m : feats + m + 512, :], right, preferred_element_type=jnp.float32)
        cross_ref[here, :] = cross / factors_ref[1]


def products(place, mask, factors, near, far, cols, block=256):
    frames, feats = cols[0].shape
    rows = near[0].shape[0]
    out = jax.ShapeDtypeStruct((rows, feats), jnp.float32)
    inputs = [mask, factors, *near, *far, *cols]
    return pl.pallas_call(
        product_kernel,
        out_shape=[out, out],
        grid_spec=pltpu.PrefetchScalarGridSpec(
            num_scalar_prefetch=1,
            grid=(feats // block,),
            in_specs=[
                pl.BlockSpec(mask.shape, lambda n, s: (0,) * mask.ndim),
                pl.BlockSpec(memory_space=pltpu.SMEM),
            ]
            + [pl.BlockSpec(memory_space=pl.ANY)] * (len(near) + len(far))
            + [pl.BlockSpec((frames, block), lambda n, s: (0, n))] * 8,
            out_specs=[pl.BlockSpec((rows, block), lambda n, s: (0, n))] * 2,
            scratch_shapes=[
                pltpu.VMEM((2 * rows, 8 * frames), jnp.bfloat16),
                pltpu.VMEM((len(near),) + near[0].shape, jnp.bfloat16),
                pltpu.VMEM((len(far),) + far[0].shape, jnp.bfloat16),
                pltpu.SemaphoreType.DMA((len(near) + len(far),)),
            ],
        ),
        compiler_params=pltpu.CompilerParams(vmem_limit_bytes=VMEM_LIMIT),
        cost_estimate=estimate(0.01),
    )(place, *inputs)


def swap(x, bits):
    return lax.ppermute(x, "tm", [(i, i ^ bits) for i in range(8)])


def swap_by_parity(x, even, odd):
    return lax.ppermute(x, "tm", [(i, i ^ (odd if i % 2 else even)) for i in range(8)])


def corner(along_x, along_y):
    even = lax.axis_index("tm") % 2 == 0
    return swap_by_parity(jnp.where(even, along_x, along_y), 4, 2)


def line_gather(x, count):
    shift = lambda s: [(i, (i + s) % count) for i in range(count)]
    return jnp.stack([x] + [lax.ppermute(x, "feat", shift(s)) for s in range(1, count)])


def line_hop(up, down, hop, count):
    up = lax.ppermute(up, "feat", [(i, i + 1) for i in range(hop - 1, count - 1)])
    down = lax.ppermute(down, "feat", [(i + 1, i) for i in range(count - hop)])
    return up, down


def together(*values):
    return lax.optimization_barrier(values)


def shards(coords, frame_scale, pairs, walker_lengths):
    tm_count = lax.axis_size("tm")
    feat_count = lax.axis_size("feat")
    frames_dev = coords.shape[0]
    feats = pairs.shape[1]
    frames_all = frames_dev * tm_count
    row_feats = feats * feat_count // tm_count
    parts = frames_dev // CHUNK
    tm = lax.axis_index("tm").astype(jnp.int32)
    z = lax.axis_index("feat").astype(jnp.int32)
    place = jnp.stack([tm, z])
    own_half = (tm % (feats // row_feats)) * row_feats

    coords_t = jnp.transpose(coords, (1, 2, 0))
    scale_own = frame_scale.reshape(parts, CHUNK)
    quarter = lax.dynamic_slice_in_dim(coords_t, z * CHUNK, CHUNK, axis=2).astype(jnp.int16)
    quarters = {3: swap(quarter, 3), 5: swap(quarter, 5)}

    raw, sums, table = contacts("first", pairs * TABLE_ROWS, [coords_t], scale_own)
    quarters, _ = together(quarters, sums)
    quarters[7] = corner(quarters[3], quarters[5])
    note = jnp.concatenate([sums, frame_scale.reshape(1, frames_dev)], axis=1)
    notes = [note] + [swap(note, d) for d in range(1, 8)]

    totals = notes[0][:, :feats]
    for other in notes[1:]:
        totals = totals + other[:, :feats]
    mean = totals / jnp.float32(frames_all)
    scales = [lax.dynamic_slice_in_dim(n, feats + z * CHUNK, CHUNK, axis=1) for n in notes]
    scale_of = lambda *d: jnp.concatenate([scales[i] for i in d], axis=0)

    facts = line_gather(jnp.concatenate([mean, pairs.astype(jnp.float32)], axis=0), feat_count)
    mine, facts, quarters = together(center(raw, mean), facts, quarters)
    cols = [mine, None, swap_by_parity(mine, 2, 4), None, swap_by_parity(mine, 4, 2)]
    quarters[6] = swap(quarters[7], 1)

    def facts_of(i, start, count):
        back = (z - i * feat_count // tm_count) % feat_count
        return lax.dynamic_slice(facts, (back, 0, start), (1, 3, count))[0]

    row_facts = facts_of(tm, own_half, row_feats)
    out_facts = jnp.concatenate(
        [facts_of(tm ^ 2, own_half, row_feats), facts_of(tm ^ 4, own_half, row_feats), facts_of(tm, 0, feats)],
        axis=1,
    )
    row_facts, out_facts, scales = together(row_facts, out_facts, scales)
    row_mean, row_pairs = row_facts[0:1], row_facts[1:3].astype(jnp.int32) * TABLE_ROWS
    out_mean, out_pairs = out_facts[0:1], out_facts[1:3].astype(jnp.int32) * TABLE_ROWS
    mixed_scale = scale_of(*FAR)

    row_pairs, row_mean, mixed_scale, mine, quarters = together(row_pairs, row_mean, mixed_scale, mine, quarters)
    cols[1] = swap(mine, 1)
    mixed = contacts("sent", row_pairs, [quarters[d] for d in FAR], mixed_scale, row_mean)

    out_pairs, mixed, walker_lengths = together(out_pairs, mixed, walker_lengths)
    up, down = line_hop(mixed, mixed, 1, feat_count)
    valid = walker_mask(walker_lengths, frames_all, frames_all)
    mask = valid.astype(jnp.float32).reshape(tm_count, parts, 1, CHUNK)
    npairs = jnp.sum(jnp.maximum(walker_lengths - LAG, 0)).astype(jnp.float32)
    factors = jnp.stack([jnp.float32(1.0 / frames_all), npairs])
    near_rows = contacts("own", out_pairs[:, :feats], [table], scale_own, out_mean[:, :feats])
    near_x, near_y = near_rows[:row_feats], near_rows[row_feats:]
    near_x, near_y, mask, factors, up, down, cols = together(near_x, near_y, mask, factors, up, down, cols)
    far = [mixed, up, down]

    across = swap_by_parity(cols[2], 4, 2)
    up, down = line_hop(up, down, 2, feat_count)
    cols[3] = swap(cols[2], 1)
    their_last = swap(cols[4], 1)
    chip_pairs, _ = together(out_pairs[:, feats:], near_x)
    chip_rows = contacts("own", chip_pairs, [table], scale_own, out_mean[:, feats:])
    cols += [their_last, across]
    chip_rows, near_x, near_y, cols, up, down = together(chip_rows, near_x, near_y, cols, up, down)
    far += [up, down, *line_hop(up, down, 3, feat_count)]

    cut = lambda x, start: lax.dynamic_slice_in_dim(x, start, row_feats, axis=0)
    near_x, near_y = swap(near_x, 2), swap(near_y, 4)
    cols.append(swap(cols[6], 1))
    partner, cols = together(cut(chip_rows, row_feats - own_half), cols)
    near = [cut(chip_rows, own_half), swap(partner, 1), near_x, near_y]
    return products(place, mask, factors, near, far, cols)


def solution(mesh):
    def run(coords, frame_scale, pairs, walker_lengths):
        tm_count, feat_count = mesh.shape["tm"], mesh.shape["feat"]
        frames_dev = coords.shape[0] // tm_count
        square = tm_count == 8 and feat_count == 4
        fits = square and frames_dev == 4 * CHUNK and pairs.shape[1] == 16 * 512
        return jax.shard_map(
            shards if fits else plain_shards,
            mesh=mesh,
            in_specs=(P("tm", None, None), P("tm"), P(None, "feat"), P()),
            out_specs=(P("tm", "feat"), P("tm", "feat")),
            check_vma=False,
        )(coords, frame_scale, pairs, walker_lengths)

    return run
```

```python
import functools

import jax
import jax.numpy as jnp
from jax import lax
from jax.experimental import pallas as pl
from jax.experimental.pallas import tpu as pltpu
from jax.sharding import PartitionSpec as P

LAG = 384
CHUNK = 128
VMEM_LIMIT = 63 * 1024 * 1024
NEAR = (0, 1, 2, 4)
FAR = (3, 5, 6, 7)
TABLE_ROWS = 16


def contact_values(coords, frame_scale, pairs):
    frames_dev = coords.shape[0]
    residues = coords.shape[2]
    flat = coords.astype(jnp.float32).reshape(frames_dev * 3, residues)
    rows_iota = jnp.arange(residues, dtype=jnp.int32)[:, None]
    selector = (rows_iota == pairs[0][None, :]).astype(jnp.float32) - (
        rows_iota == pairs[1][None, :]
    ).astype(jnp.float32)
    diff = jnp.dot(
        flat, selector, precision=lax.Precision.HIGHEST, preferred_element_type=jnp.float32
    )
    diff = diff.reshape(frames_dev, 3, pairs.shape[1])
    squares = diff[:, 0] * diff[:, 0] + diff[:, 1] * diff[:, 1] + diff[:, 2] * diff[:, 2]
    dist_sq = (frame_scale * frame_scale)[:, None] * squares
    return 1.0 / (1.0 + dist_sq * dist_sq * dist_sq)


def walker_mask(walker_lengths, count, frames_all):
    ends = jnp.cumsum(walker_lengths)
    times = jnp.arange(count, dtype=jnp.int32)
    later = times + LAG
    own = jnp.sum((times[:, None] >= ends[None, :]).astype(jnp.int32), axis=1)
    ahead = jnp.sum((later[:, None] >= ends[None, :]).astype(jnp.int32), axis=1)
    return (own == ahead) & (later < frames_all)


def estimate(micros):
    return pl.CostEstimate(
        flops=int(micros * 1_000_000_000), bytes_accessed=int(micros * 3_690_000), transcendentals=0
    )


def contract(left, right):
    return lax.dot_general(
        left, right, (((0,), (0,)), ((), ())), preferred_element_type=jnp.float32
    )


def plain_shards(coords, frame_scale, pairs, walker_lengths):
    tm_count = lax.axis_size("tm")
    frames_dev = coords.shape[0]
    local_feats = pairs.shape[1]
    frames_all = frames_dev * tm_count
    contact = contact_values(coords, frame_scale, pairs)
    totals = lax.psum(jnp.sum(contact, axis=0), "tm")
    centered = (contact - totals / jnp.float32(frames_all)).astype(jnp.bfloat16)
    npairs = jnp.sum(jnp.maximum(walker_lengths - LAG, 0)).astype(jnp.float32)
    column_series = lax.all_gather(centered, "tm", axis=0, tiled=True)
    wide = lax.all_gather(centered, "feat", axis=1, tiled=True)
    row_series = lax.all_to_all(wide, "tm", split_axis=1, concat_axis=0, tiled=True)
    valid = walker_mask(walker_lengths, frames_all, frames_all)
    later = jnp.concatenate(
        [column_series[LAG:], jnp.zeros((LAG, local_feats), jnp.bfloat16)], axis=0
    )
    lagged = jnp.where(valid[:, None], later, jnp.zeros_like(later))
    same = contract(row_series, column_series)
    cross = contract(row_series, lagged)
    return (same / jnp.float32(frames_all), cross / npairs)


def switch(squares, scale):
    dist_sq = (scale * scale) * squares
    return 1.0 / (1.0 + dist_sq * dist_sq * dist_sq)


def as_column(row):
    return jnp.broadcast_to(row, (CHUNK, row.shape[1])).T


def gather_kernel(form, chunks, count, pairs_ref, scale_ref, *rest):
    sources, rest = rest[:count], rest[count:]
    if form == "first":
        out_ref, sums_ref, table_out, table, dense, part, held, arrived, left = rest
    elif form == "own":
        mean_ref, out_ref, table, dense, part, arrived = rest
    else:
        mean_ref, out_ref, table, dense, part, held, arrived = rest
    block = part.shape[0]
    stride = -(-3 * chunks // 8) * 8
    residues = table.shape[0] // stride
    group = dense.shape[0] // chunks
    step = pl.program_id(0)

    @pl.when(step == 0)
    def _():
        if form == "own":
            copy = pltpu.make_async_copy(sources[0], table, arrived)
            copy.start()
            copy.wait()
            return
        copies = [
            pltpu.make_async_copy(ref.at[k], held.at[n, k], arrived.at[n, k])
            for k in range(3)
            for n, ref in enumerate(sources)
        ]
        for copy in copies:
            copy.start()
        for k in range(3):
            for n in range(count):
                copies[k * count + n].wait()
            for c in range(chunks):
                if form == "first":
                    plane = held[0, k, :, c * CHUNK : (c + 1) * CHUNK]
                else:
                    plane = held[c, k].astype(jnp.int32)
                table[pl.ds(k * chunks + c, residues, stride=stride), :] = plane
        if form == "first":
            pltpu.make_async_copy(table, table_out, left).start()

    if form != "first":
        part[...] = as_column(mean_ref[...])
    sublane = lax.broadcasted_iota(jnp.int32, (8, CHUNK), 0)
    scale = jnp.concatenate([scale_ref[...]] * (8 // chunks), axis=0)

    def squares(f):
        first = pl.multiple_of(pairs_ref[0, f], 8)
        second = pl.multiple_of(pairs_ref[1, f], 8)
        diff = (table[pl.ds(first, stride), :] - table[pl.ds(second, stride), :]).astype(jnp.float32)
        diff = diff * diff
        total = diff[0:8] + jnp.where(sublane < 4, diff[8:16], 0.0)
        return total + pltpu.roll(total, 4, 0)

    @pl.loop(0, block // group)
    def _(g):
        at = pl.multiple_of(g * group, group)
        for f in range(0, group, 2):
            base = step * block + at + f
            value = jnp.where(sublane < 4, squares(base), squares(base + 1))
            dense[pl.ds(f * chunks, 8), :] = switch(value, scale)
        for h in range(group // 16):
            here = pl.ds(pl.multiple_of(at + h * 16, 16), 16)
            total = jnp.zeros((16, CHUNK), jnp.float32)
            for c in range(chunks):
                contact = dense[pl.ds(h * 16 * chunks + c, 16, stride=chunks), :]
                lanes = slice(c * CHUNK, (c + 1) * CHUNK)
                if form == "first":
                    out_ref[here, lanes] = contact
                    total = total + contact
                elif form == "own":
                    out_ref[here, lanes] = (contact - part[here, :]).astype(jnp.bfloat16)
                else:
                    out_ref[c, here, :] = (contact - part[here, :]).astype(jnp.bfloat16)
            if form == "first":
                part[here, :] = total

    if form == "first":
        sums_ref[...] = jnp.sum(part[...].T, axis=0, keepdims=True)

        @pl.when(step == pl.num_programs(0) - 1)
        def _():
            pltpu.make_async_copy(table, table_out, left).wait()


def contacts(form, pairs, sources, scale, mean=None, block=512, group=128):
    feats = pairs.shape[1]
    chunks = scale.shape[0]
    stride = -(-3 * chunks // 8) * 8
    rows = sources[0].shape[0] if form == "own" else sources[0].shape[1] * stride
    row_spec = pl.BlockSpec((1, block), lambda n: (0, n))
    any_spec = pl.BlockSpec(memory_space=pl.ANY)
    in_specs = [pl.BlockSpec(memory_space=pltpu.SMEM), pl.BlockSpec((chunks, CHUNK), lambda n: (0, 0))]
    in_specs += [any_spec] * len(sources)
    args = [pairs, scale, *sources]
    scratch = [
        pltpu.VMEM((rows, CHUNK), jnp.int32),
        pltpu.VMEM((group * chunks, CHUNK), jnp.float32),
        pltpu.VMEM((block, CHUNK), jnp.float32),
    ]
    if form == "sent":
        out_shape = jax.ShapeDtypeStruct((chunks, feats, CHUNK), jnp.bfloat16)
        out_specs = pl.BlockSpec((chunks, block, CHUNK), lambda n: (0, n, 0))
    else:
        dtype = jnp.bfloat16 if form == "own" else jnp.float32
        out_shape = jax.ShapeDtypeStruct((feats, chunks * CHUNK), dtype)
        out_specs = pl.BlockSpec((block, chunks * CHUNK), lambda n: (n, 0))
    if form == "own":
        scratch.append(pltpu.SemaphoreType.DMA)
    else:
        scratch.append(pltpu.VMEM((len(sources),) + sources[0].shape, sources[0].dtype))
        scratch.append(pltpu.SemaphoreType.DMA((len(sources), 3)))
    if form == "first":
        out_shape = [
            out_shape,
            jax.ShapeDtypeStruct((1, feats), jnp.float32),
            jax.ShapeDtypeStruct((rows, CHUNK), jnp.int32),
        ]
        out_specs = [out_specs, row_spec, any_spec]
        scratch.append(pltpu.SemaphoreType.DMA)
    else:
        in_specs.append(row_spec)
        args.append(mean)
    return pl.pallas_call(
        functools.partial(gather_kernel, form, chunks, len(sources)),
        out_shape=out_shape,
        grid=(feats // block,),
        in_specs=in_specs,
        out_specs=out_specs,
        scratch_shapes=scratch,
        compiler_params=pltpu.CompilerParams(vmem_limit_bytes=VMEM_LIMIT),
        cost_estimate=estimate(0.01),
    )(*args)


def center_kernel(raw_ref, mean_ref, out_ref):
    for c in range(raw_ref.shape[1] // CHUNK):
        frames = slice(c * CHUNK, (c + 1) * CHUNK)
        out_ref[frames, :] = (raw_ref[:, frames].T - mean_ref[...]).astype(jnp.bfloat16)


def center(raw, mean, block=512):
    feats, frames = raw.shape
    return pl.pallas_call(
        center_kernel,
        out_shape=jax.ShapeDtypeStruct((frames, feats), jnp.bfloat16),
        grid=(feats // block,),
        in_specs=[
            pl.BlockSpec((block, frames), lambda n: (n, 0)),
            pl.BlockSpec((1, block), lambda n: (0, n)),
        ],
        out_specs=pl.BlockSpec((frames, block), lambda n: (0, n)),
        compiler_params=pltpu.CompilerParams(vmem_limit_bytes=VMEM_LIMIT),
        cost_estimate=estimate(0.01),
    )(raw, mean)


def product_kernel(place_ref, mask_ref, factors_ref, *rest):
    near_refs, rest = rest[: len(NEAR)], rest[len(NEAR) :]
    far_refs, cols_refs = rest[:7], rest[7:15]
    same_ref, cross_ref, left, near_held, far_held, arrived = rest[15:]
    feats = same_ref.shape[0]
    frames = cols_refs[0].shape[0]
    parts = frames // CHUNK
    me, z = place_ref[0], place_ref[1]

    def slot_of(d):
        crossed = (d >= 2) & (d <= 5) & ((d & 1) != (me & 1))
        return jnp.where(crossed, 6 + 2 * (d & 1) - d, d)

    def put(d, c, value):
        j = me ^ d
        after = slot_of(me ^ lax.rem(j + 1, 8))
        mask = mask_ref[j, c].astype(jnp.bfloat16)
        own = slot_of(jnp.int32(d)) * frames
        left[0:feats, pl.ds(pl.multiple_of(own + c * CHUNK, CHUNK), CHUNK)] = value
        to = c + LAG // CHUNK
        at = jnp.where(to < parts, own + to * CHUNK, after * frames + (to - parts) * CHUNK)
        left[feats : 2 * feats, pl.ds(pl.multiple_of(at, CHUNK), CHUNK)] = value * mask

    @pl.when(pl.program_id(0) == 0)
    def _():
        copies = [
            pltpu.make_async_copy(ref, near_held.at[n], arrived.at[n]) for n, ref in enumerate(near_refs)
        ]
        copies += [
            pltpu.make_async_copy(ref, far_held.at[n], arrived.at[len(NEAR) + n])
            for n, ref in enumerate(far_refs)
        ]
        for copy in copies:
            copy.start()
        for n, d in enumerate(NEAR):
            copies[n].wait()
            for c in range(parts):
                put(d, c, near_held[n, :, c * CHUNK : (c + 1) * CHUNK])
        for n in range(len(far_refs)):
            copies[len(NEAR) + n].wait()
            hop = (n + 1) // 2
            c = z - hop if n % 2 else z + hop

            @pl.when((c >= 0) & (c < parts))
            def _():
                for i, d in enumerate(FAR):
                    put(d, c, far_held[n, i])

    right = jnp.concatenate([ref[...] for ref in cols_refs], axis=0)
    for m in range(0, feats, 512):
        here = slice(m, m + 512)
        same = jnp.dot(left[here, :], right, preferred_element_type=jnp.float32)
        same_ref[here, :] = same * factors_ref[0]
    for m in range(0, feats, 512):
        here = slice(m, m + 512)
        cross = jnp.dot(left[feats + m : feats + m + 512, :], right, preferred_element_type=jnp.float32)
        cross_ref[here, :] = cross / factors_ref[1]


def products(place, mask, factors, near, far, cols, block=256):
    frames, feats = cols[0].shape
    rows = near[0].shape[0]
    out = jax.ShapeDtypeStruct((rows, feats), jnp.float32)
    inputs = [mask, factors, *near, *far, *cols]
    return pl.pallas_call(
        product_kernel,
        out_shape=[out, out],
        grid_spec=pltpu.PrefetchScalarGridSpec(
            num_scalar_prefetch=1,
            grid=(feats // block,),
            in_specs=[
                pl.BlockSpec(mask.shape, lambda n, s: (0,) * mask.ndim),
                pl.BlockSpec(memory_space=pltpu.SMEM),
            ]
            + [pl.BlockSpec(memory_space=pl.ANY)] * (len(near) + len(far))
            + [pl.BlockSpec((frames, block), lambda n, s: (0, n))] * 8,
            out_specs=[pl.BlockSpec((rows, block), lambda n, s: (0, n))] * 2,
            scratch_shapes=[
                pltpu.VMEM((2 * rows, 8 * frames), jnp.bfloat16),
                pltpu.VMEM((len(near),) + near[0].shape, jnp.bfloat16),
                pltpu.VMEM((len(far),) + far[0].shape, jnp.bfloat16),
                pltpu.SemaphoreType.DMA((len(near) + len(far),)),
            ],
        ),
        compiler_params=pltpu.CompilerParams(vmem_limit_bytes=VMEM_LIMIT),
        cost_estimate=estimate(0.01),
    )(place, *inputs)


def swap(x, bits):
    return lax.ppermute(x, "tm", [(i, i ^ bits) for i in range(8)])


def swap_by_parity(x, even, odd):
    return lax.ppermute(x, "tm", [(i, i ^ (odd if i % 2 else even)) for i in range(8)])


def corner(along_x, along_y):
    even = lax.axis_index("tm") % 2 == 0
    return swap_by_parity(jnp.where(even, along_x, along_y), 4, 2)


def line_gather(x, count):
    shift = lambda s: [(i, (i + s) % count) for i in range(count)]
    return jnp.stack([x] + [lax.ppermute(x, "feat", shift(s)) for s in range(1, count)])


def line_hop(up, down, hop, count):
    up = lax.ppermute(up, "feat", [(i, i + 1) for i in range(hop - 1, count - 1)])
    down = lax.ppermute(down, "feat", [(i + 1, i) for i in range(count - hop)])
    return up, down


def together(*values):
    return lax.optimization_barrier(values)


def shards(coords, frame_scale, pairs, walker_lengths):
    tm_count = lax.axis_size("tm")
    feat_count = lax.axis_size("feat")
    frames_dev = coords.shape[0]
    feats = pairs.shape[1]
    frames_all = frames_dev * tm_count
    row_feats = feats * feat_count // tm_count
    parts = frames_dev // CHUNK
    tm = lax.axis_index("tm").astype(jnp.int32)
    z = lax.axis_index("feat").astype(jnp.int32)
    place = jnp.stack([tm, z])
    own_half = (tm % (feats // row_feats)) * row_feats

    coords_t = jnp.transpose(coords, (1, 2, 0))
    scale_own = frame_scale.reshape(parts, CHUNK)
    quarter = lax.dynamic_slice_in_dim(coords_t, z * CHUNK, CHUNK, axis=2).astype(jnp.int16)
    quarters = {3: swap(quarter, 3), 5: swap(quarter, 5)}

    raw, sums, table = contacts("first", pairs * TABLE_ROWS, [coords_t], scale_own)
    quarters, _ = together(quarters, sums)
    quarters[7] = corner(quarters[3], quarters[5])
    note = jnp.concatenate([sums, frame_scale.reshape(1, frames_dev)], axis=1)
    notes = [note] + [swap(note, d) for d in range(1, 8)]

    totals = notes[0][:, :feats]
    for other in notes[1:]:
        totals = totals + other[:, :feats]
    mean = totals / jnp.float32(frames_all)
    scales = [lax.dynamic_slice_in_dim(n, feats + z * CHUNK, CHUNK, axis=1) for n in notes]
    scale_of = lambda *d: jnp.concatenate([scales[i] for i in d], axis=0)

    facts = line_gather(jnp.concatenate([mean, pairs.astype(jnp.float32)], axis=0), feat_count)
    mine, facts, quarters = together(center(raw, mean), facts, quarters)
    cols = [mine, None, swap_by_parity(mine, 2, 4), None, swap_by_parity(mine, 4, 2)]
    quarters[6] = swap(quarters[7], 1)

    def facts_of(i, start, count):
        back = (z - i * feat_count // tm_count) % feat_count
        return lax.dynamic_slice(facts, (back, 0, start), (1, 3, count))[0]

    row_facts = facts_of(tm, own_half, row_feats)
    out_facts = jnp.concatenate(
        [facts_of(tm ^ 2, own_half, row_feats), facts_of(tm ^ 4, own_half, row_feats), facts_of(tm, 0, feats)],
        axis=1,
    )
    row_facts, out_facts, scales = together(row_facts, out_facts, scales)
    row_mean, row_pairs = row_facts[0:1], row_facts[1:3].astype(jnp.int32) * TABLE_ROWS
    out_mean, out_pairs = out_facts[0:1], out_facts[1:3].astype(jnp.int32) * TABLE_ROWS
    mixed_scale = scale_of(*FAR)

    row_pairs, row_mean, mixed_scale, mine, quarters = together(row_pairs, row_mean, mixed_scale, mine, quarters)
    cols[1] = swap(mine, 1)
    mixed = contacts("sent", row_pairs, [quarters[d] for d in FAR], mixed_scale, row_mean)

    out_pairs, mixed, walker_lengths = together(out_pairs, mixed, walker_lengths)
    up, down = line_hop(mixed, mixed, 1, feat_count)
    valid = walker_mask(walker_lengths, frames_all, frames_all)
    mask = valid.astype(jnp.float32).reshape(tm_count, parts, 1, CHUNK)
    npairs = jnp.sum(jnp.maximum(walker_lengths - LAG, 0)).astype(jnp.float32)
    factors = jnp.stack([jnp.float32(1.0 / frames_all), npairs])
    near_rows = contacts("own", out_pairs[:, :feats], [table], scale_own, out_mean[:, :feats])
    near_x, near_y = near_rows[:row_feats], near_rows[row_feats:]
    near_x, near_y, mask, factors, up, down, cols = together(near_x, near_y, mask, factors, up, down, cols)
    far = [mixed, up, down]

    across = swap_by_parity(cols[2], 4, 2)
    up, down = line_hop(up, down, 2, feat_count)
    cols[3] = swap(cols[2], 1)
    their_last = swap(cols[4], 1)
    chip_pairs, _ = together(out_pairs[:, feats:], near_x)
    chip_rows = contacts("own", chip_pairs, [table], scale_own, out_mean[:, feats:])
    cols += [their_last, across]
    chip_rows, near_x, near_y, cols, up, down = together(chip_rows, near_x, near_y, cols, up, down)
    far += [up, down, *line_hop(up, down, 3, feat_count)]

    cut = lambda x, start: lax.dynamic_slice_in_dim(x, start, row_feats, axis=0)
    near_x, near_y = swap(near_x, 2), swap(near_y, 4)
    cols.append(swap(cols[6], 1))
    partner, cols = together(cut(chip_rows, row_feats - own_half), cols)
    near = [cut(chip_rows, own_half), swap(partner, 1), near_x, near_y]
    return products(place, mask, factors, near, far, cols)


def solution(mesh):
    def run(coords, frame_scale, pairs, walker_lengths):
        tm_count, feat_count = mesh.shape["tm"], mesh.shape["feat"]
        frames_dev = coords.shape[0] // tm_count
        square = tm_count == 8 and feat_count == 4
        fits = square and frames_dev == 4 * CHUNK and pairs.shape[1] == 16 * 512
        return jax.shard_map(
            shards if fits else plain_shards,
            mesh=mesh,
            in_specs=(P("tm", None, None), P("tm"), P(None, "feat"), P()),
            out_specs=(P("tm", "feat"), P("tm", "feat")),
            check_vma=False,
        )(coords, frame_scale, pairs, walker_lengths)

    return run
```

```python
import functools

import jax
import jax.numpy as jnp
from jax import lax
from jax.experimental import pallas as pl
from jax.experimental.pallas import tpu as pltpu
from jax.sharding import PartitionSpec as P

LAG = 384
CHUNK = 128
VMEM_LIMIT = 48 * 1024 * 1024
NEAR = (0, 1, 2, 4)
FAR = (3, 5, 6, 7)
TABLE_ROWS = 16


def contact_values(coords, frame_scale, pairs):
    frames_dev = coords.shape[0]
    residues = coords.shape[2]
    flat = coords.astype(jnp.float32).reshape(frames_dev * 3, residues)
    rows_iota = jnp.arange(residues, dtype=jnp.int32)[:, None]
    selector = (rows_iota == pairs[0][None, :]).astype(jnp.float32) - (
        rows_iota == pairs[1][None, :]
    ).astype(jnp.float32)
    diff = jnp.dot(
        flat, selector, precision=lax.Precision.HIGHEST, preferred_element_type=jnp.float32
    )
    diff = diff.reshape(frames_dev, 3, pairs.shape[1])
    squares = diff[:, 0] * diff[:, 0] + diff[:, 1] * diff[:, 1] + diff[:, 2] * diff[:, 2]
    dist_sq = (frame_scale * frame_scale)[:, None] * squares
    return 1.0 / (1.0 + dist_sq * dist_sq * dist_sq)


def walker_mask(walker_lengths, count, frames_all):
    ends = jnp.cumsum(walker_lengths)
    times = jnp.arange(count, dtype=jnp.int32)
    later = times + LAG
    own = jnp.sum((times[:, None] >= ends[None, :]).astype(jnp.int32), axis=1)
    ahead = jnp.sum((later[:, None] >= ends[None, :]).astype(jnp.int32), axis=1)
    return (own == ahead) & (later < frames_all)


def estimate(micros):
    return pl.CostEstimate(
        flops=int(micros * 1_000_000_000), bytes_accessed=int(micros * 3_690_000), transcendentals=0
    )


def contract(left, right):
    return lax.dot_general(
        left, right, (((0,), (0,)), ((), ())), preferred_element_type=jnp.float32
    )


def plain_shards(coords, frame_scale, pairs, walker_lengths):
    tm_count = lax.axis_size("tm")
    frames_dev = coords.shape[0]
    local_feats = pairs.shape[1]
    frames_all = frames_dev * tm_count
    contact = contact_values(coords, frame_scale, pairs)
    totals = lax.psum(jnp.sum(contact, axis=0), "tm")
    centered = (contact - totals / jnp.float32(frames_all)).astype(jnp.bfloat16)
    npairs = jnp.sum(jnp.maximum(walker_lengths - LAG, 0)).astype(jnp.float32)
    column_series = lax.all_gather(centered, "tm", axis=0, tiled=True)
    wide = lax.all_gather(centered, "feat", axis=1, tiled=True)
    row_series = lax.all_to_all(wide, "tm", split_axis=1, concat_axis=0, tiled=True)
    valid = walker_mask(walker_lengths, frames_all, frames_all)
    later = jnp.concatenate(
        [column_series[LAG:], jnp.zeros((LAG, local_feats), jnp.bfloat16)], axis=0
    )
    lagged = jnp.where(valid[:, None], later, jnp.zeros_like(later))
    same = contract(row_series, column_series)
    cross = contract(row_series, lagged)
    return (same / jnp.float32(frames_all), cross / npairs)


def switch(squares, scale):
    dist_sq = (scale * scale) * squares
    return 1.0 / (1.0 + dist_sq * dist_sq * dist_sq)


def as_column(row):
    return jnp.broadcast_to(row, (CHUNK, row.shape[1])).T


def gather_kernel(form, chunks, count, pairs_ref, scale_ref, *rest):
    sources, rest = rest[:count], rest[count:]
    if form == "first":
        out_ref, sums_ref, table_out, table, dense, part, held, arrived, left = rest
    elif form == "own":
        mean_ref, out_ref, table, dense, part, arrived = rest
    else:
        mean_ref, out_ref, table, dense, part, held, arrived = rest
    block = part.shape[0]
    stride = -(-3 * chunks // 8) * 8
    residues = table.shape[0] // stride
    group = dense.shape[0] // chunks
    step = pl.program_id(0)

    @pl.when(step == 0)
    def _():
        if form == "own":
            copy = pltpu.make_async_copy(sources[0], table, arrived)
            copy.start()
            copy.wait()
            return
        copies = [
            pltpu.make_async_copy(ref.at[k], held.at[n, k], arrived.at[n, k])
            for k in range(3)
            for n, ref in enumerate(sources)
        ]
        for copy in copies:
            copy.start()
        for k in range(3):
            for n in range(count):
                copies[k * count + n].wait()
            for c in range(chunks):
                if form == "first":
                    plane = held[0, k, :, c * CHUNK : (c + 1) * CHUNK]
                else:
                    plane = held[c, k].astype(jnp.int32)
                table[pl.ds(k * chunks + c, residues, stride=stride), :] = plane
        if form == "first":
            pltpu.make_async_copy(table, table_out, left).start()

    if form != "first":
        part[...] = as_column(mean_ref[...])
    sublane = lax.broadcasted_iota(jnp.int32, (8, CHUNK), 0)
    scale = jnp.concatenate([scale_ref[...]] * (8 // chunks), axis=0)

    def squares(f):
        first = pl.multiple_of(pairs_ref[0, f], 8)
        second = pl.multiple_of(pairs_ref[1, f], 8)
        diff = (table[pl.ds(first, stride), :] - table[pl.ds(second, stride), :]).astype(jnp.float32)
        diff = diff * diff
        total = diff[0:8] + jnp.where(sublane < 4, diff[8:16], 0.0)
        return total + pltpu.roll(total, 4, 0)

    @pl.loop(0, block // group)
    def _(g):
        at = pl.multiple_of(g * group, group)
        for f in range(0, group, 2):
            base = step * block + at + f
            value = jnp.where(sublane < 4, squares(base), squares(base + 1))
            dense[pl.ds(f * chunks, 8), :] = switch(value, scale)
        for h in range(group // 16):
            here = pl.ds(pl.multiple_of(at + h * 16, 16), 16)
            total = jnp.zeros((16, CHUNK), jnp.float32)
            for c in range(chunks):
                contact = dense[pl.ds(h * 16 * chunks + c, 16, stride=chunks), :]
                lanes = slice(c * CHUNK, (c + 1) * CHUNK)
                if form == "first":
                    out_ref[here, lanes] = contact
                    total = total + contact
                elif form == "own":
                    out_ref[here, lanes] = (contact - part[here, :]).astype(jnp.bfloat16)
                else:
                    out_ref[c, here, :] = (contact - part[here, :]).astype(jnp.bfloat16)
            if form == "first":
                part[here, :] = total

    if form == "first":
        sums_ref[...] = jnp.sum(part[...].T, axis=0, keepdims=True)

        @pl.when(step == pl.num_programs(0) - 1)
        def _():
            pltpu.make_async_copy(table, table_out, left).wait()


def contacts(form, pairs, sources, scale, mean=None, block=512, group=128):
    feats = pairs.shape[1]
    chunks = scale.shape[0]
    stride = -(-3 * chunks // 8) * 8
    rows = sources[0].shape[0] if form == "own" else sources[0].shape[1] * stride
    row_spec = pl.BlockSpec((1, block), lambda n: (0, n))
    any_spec = pl.BlockSpec(memory_space=pl.ANY)
    in_specs = [pl.BlockSpec(memory_space=pltpu.SMEM), pl.BlockSpec((chunks, CHUNK), lambda n: (0, 0))]
    in_specs += [any_spec] * len(sources)
    args = [pairs, scale, *sources]
    scratch = [
        pltpu.VMEM((rows, CHUNK), jnp.int32),
        pltpu.VMEM((group * chunks, CHUNK), jnp.float32),
        pltpu.VMEM((block, CHUNK), jnp.float32),
    ]
    if form == "sent":
        out_shape = jax.ShapeDtypeStruct((chunks, feats, CHUNK), jnp.bfloat16)
        out_specs = pl.BlockSpec((chunks, block, CHUNK), lambda n: (0, n, 0))
    else:
        dtype = jnp.bfloat16 if form == "own" else jnp.float32
        out_shape = jax.ShapeDtypeStruct((feats, chunks * CHUNK), dtype)
        out_specs = pl.BlockSpec((block, chunks * CHUNK), lambda n: (n, 0))
    if form == "own":
        scratch.append(pltpu.SemaphoreType.DMA)
    else:
        scratch.append(pltpu.VMEM((len(sources),) + sources[0].shape, sources[0].dtype))
        scratch.append(pltpu.SemaphoreType.DMA((len(sources), 3)))
    if form == "first":
        out_shape = [
            out_shape,
            jax.ShapeDtypeStruct((1, feats), jnp.float32),
            jax.ShapeDtypeStruct((rows, CHUNK), jnp.int32),
        ]
        out_specs = [out_specs, row_spec, any_spec]
        scratch.append(pltpu.SemaphoreType.DMA)
    else:
        in_specs.append(row_spec)
        args.append(mean)
    return pl.pallas_call(
        functools.partial(gather_kernel, form, chunks, len(sources)),
        out_shape=out_shape,
        grid=(feats // block,),
        in_specs=in_specs,
        out_specs=out_specs,
        scratch_shapes=scratch,
        compiler_params=pltpu.CompilerParams(vmem_limit_bytes=VMEM_LIMIT),
        cost_estimate=estimate(0.01),
    )(*args)


def center_kernel(raw_ref, mean_ref, out_ref):
    for c in range(raw_ref.shape[1] // CHUNK):
        frames = slice(c * CHUNK, (c + 1) * CHUNK)
        out_ref[frames, :] = (raw_ref[:, frames].T - mean_ref[...]).astype(jnp.bfloat16)


def center(raw, mean, block=512):
    feats, frames = raw.shape
    return pl.pallas_call(
        center_kernel,
        out_shape=jax.ShapeDtypeStruct((frames, feats), jnp.bfloat16),
        grid=(feats // block,),
        in_specs=[
            pl.BlockSpec((block, frames), lambda n: (n, 0)),
            pl.BlockSpec((1, block), lambda n: (0, n)),
        ],
        out_specs=pl.BlockSpec((frames, block), lambda n: (0, n)),
        compiler_params=pltpu.CompilerParams(vmem_limit_bytes=VMEM_LIMIT),
        cost_estimate=estimate(0.01),
    )(raw, mean)


def product_kernel(place_ref, mask_ref, factors_ref, *rest):
    near_refs, rest = rest[: len(NEAR)], rest[len(NEAR) :]
    far_refs, cols_refs = rest[:7], rest[7:15]
    same_ref, cross_ref, left, near_held, far_held, arrived = rest[15:]
    feats = same_ref.shape[0]
    frames = cols_refs[0].shape[0]
    parts = frames // CHUNK
    me, z = place_ref[0], place_ref[1]

    def slot_of(d):
        crossed = (d >= 2) & (d <= 5) & ((d & 1) != (me & 1))
        return jnp.where(crossed, 6 + 2 * (d & 1) - d, d)

    def put(d, c, value):
        j = me ^ d
        after = slot_of(me ^ lax.rem(j + 1, 8))
        mask = mask_ref[j, c].astype(jnp.bfloat16)
        own = slot_of(jnp.int32(d)) * frames
        left[0:feats, pl.ds(pl.multiple_of(own + c * CHUNK, CHUNK), CHUNK)] = value
        to = c + LAG // CHUNK
        at = jnp.where(to < parts, own + to * CHUNK, after * frames + (to - parts) * CHUNK)
        left[feats : 2 * feats, pl.ds(pl.multiple_of(at, CHUNK), CHUNK)] = value * mask

    @pl.when(pl.program_id(0) == 0)
    def _():
        copies = [
            pltpu.make_async_copy(ref, near_held.at[n], arrived.at[n]) for n, ref in enumerate(near_refs)
        ]
        copies += [
            pltpu.make_async_copy(ref, far_held.at[n], arrived.at[len(NEAR) + n])
            for n, ref in enumerate(far_refs)
        ]
        for copy in copies:
            copy.start()
        for n, d in enumerate(NEAR):
            copies[n].wait()
            for c in range(parts):
                put(d, c, near_held[n, :, c * CHUNK : (c + 1) * CHUNK])
        for n in range(len(far_refs)):
            copies[len(NEAR) + n].wait()
            hop = (n + 1) // 2
            c = z - hop if n % 2 else z + hop

            @pl.when((c >= 0) & (c < parts))
            def _():
                for i, d in enumerate(FAR):
                    put(d, c, far_held[n, i])

    right = jnp.concatenate([ref[...] for ref in cols_refs], axis=0)
    for m in range(0, feats, 512):
        here = slice(m, m + 512)
        same = jnp.dot(left[here, :], right, preferred_element_type=jnp.float32)
        same_ref[here, :] = same * factors_ref[0]
    for m in range(0, feats, 512):
        here = slice(m, m + 512)
        cross = jnp.dot(left[feats + m : feats + m + 512, :], right, preferred_element_type=jnp.float32)
        cross_ref[here, :] = cross / factors_ref[1]


def products(place, mask, factors, near, far, cols, block=256):
    frames, feats = cols[0].shape
    rows = near[0].shape[0]
    out = jax.ShapeDtypeStruct((rows, feats), jnp.float32)
    inputs = [mask, factors, *near, *far, *cols]
    return pl.pallas_call(
        product_kernel,
        out_shape=[out, out],
        grid_spec=pltpu.PrefetchScalarGridSpec(
            num_scalar_prefetch=1,
            grid=(feats // block,),
            in_specs=[
                pl.BlockSpec(mask.shape, lambda n, s: (0,) * mask.ndim),
                pl.BlockSpec(memory_space=pltpu.SMEM),
            ]
            + [pl.BlockSpec(memory_space=pl.ANY)] * (len(near) + len(far))
            + [pl.BlockSpec((frames, block), lambda n, s: (0, n))] * 8,
            out_specs=[pl.BlockSpec((rows, block), lambda n, s: (0, n))] * 2,
            scratch_shapes=[
                pltpu.VMEM((2 * rows, 8 * frames), jnp.bfloat16),
                pltpu.VMEM((len(near),) + near[0].shape, jnp.bfloat16),
                pltpu.VMEM((len(far),) + far[0].shape, jnp.bfloat16),
                pltpu.SemaphoreType.DMA((len(near) + len(far),)),
            ],
        ),
        compiler_params=pltpu.CompilerParams(vmem_limit_bytes=VMEM_LIMIT),
        cost_estimate=estimate(0.01),
    )(place, *inputs)


def swap(x, bits):
    return lax.ppermute(x, "tm", [(i, i ^ bits) for i in range(8)])


def swap_by_parity(x, even, odd):
    return lax.ppermute(x, "tm", [(i, i ^ (odd if i % 2 else even)) for i in range(8)])


def corner(along_x, along_y):
    even = lax.axis_index("tm") % 2 == 0
    return swap_by_parity(jnp.where(even, along_x, along_y), 4, 2)


def line_gather(x, count):
    shift = lambda s: [(i, (i + s) % count) for i in range(count)]
    return jnp.stack([x] + [lax.ppermute(x, "feat", shift(s)) for s in range(1, count)])


def line_hop(up, down, hop, count):
    up = lax.ppermute(up, "feat", [(i, i + 1) for i in range(hop - 1, count - 1)])
    down = lax.ppermute(down, "feat", [(i + 1, i) for i in range(count - hop)])
    return up, down


def together(*values):
    return lax.optimization_barrier(values)


def shards(coords, frame_scale, pairs, walker_lengths):
    tm_count = lax.axis_size("tm")
    feat_count = lax.axis_size("feat")
    frames_dev = coords.shape[0]
    feats = pairs.shape[1]
    frames_all = frames_dev * tm_count
    row_feats = feats * feat_count // tm_count
    parts = frames_dev // CHUNK
    tm = lax.axis_index("tm").astype(jnp.int32)
    z = lax.axis_index("feat").astype(jnp.int32)
    place = jnp.stack([tm, z])
    own_half = (tm % (feats // row_feats)) * row_feats

    coords_t = jnp.transpose(coords, (1, 2, 0))
    scale_own = frame_scale.reshape(parts, CHUNK)
    quarter = lax.dynamic_slice_in_dim(coords_t, z * CHUNK, CHUNK, axis=2).astype(jnp.int16)
    quarters = {3: swap(quarter, 3), 5: swap(quarter, 5)}

    raw, sums, table = contacts("first", pairs * TABLE_ROWS, [coords_t], scale_own)
    quarters, _ = together(quarters, sums)
    quarters[7] = corner(quarters[3], quarters[5])
    note = jnp.concatenate([sums, frame_scale.reshape(1, frames_dev)], axis=1)
    notes = [note] + [swap(note, d) for d in range(1, 8)]

    totals = notes[0][:, :feats]
    for other in notes[1:]:
        totals = totals + other[:, :feats]
    mean = totals / jnp.float32(frames_all)
    scales = [lax.dynamic_slice_in_dim(n, feats + z * CHUNK, CHUNK, axis=1) for n in notes]
    scale_of = lambda *d: jnp.concatenate([scales[i] for i in d], axis=0)

    facts = line_gather(jnp.concatenate([mean, pairs.astype(jnp.float32)], axis=0), feat_count)
    mine, facts, quarters = together(center(raw, mean), facts, quarters)
    cols = [mine, None, swap_by_parity(mine, 2, 4), None, swap_by_parity(mine, 4, 2)]
    quarters[6] = swap(quarters[7], 1)

    def facts_of(i, start, count):
        back = (z - i * feat_count // tm_count) % feat_count
        return lax.dynamic_slice(facts, (back, 0, start), (1, 3, count))[0]

    row_facts = facts_of(tm, own_half, row_feats)
    out_facts = jnp.concatenate(
        [facts_of(tm ^ 2, own_half, row_feats), facts_of(tm ^ 4, own_half, row_feats), facts_of(tm, 0, feats)],
        axis=1,
    )
    row_facts, out_facts, scales = together(row_facts, out_facts, scales)
    row_mean, row_pairs = row_facts[0:1], row_facts[1:3].astype(jnp.int32) * TABLE_ROWS
    out_mean, out_pairs = out_facts[0:1], out_facts[1:3].astype(jnp.int32) * TABLE_ROWS
    mixed_scale = scale_of(*FAR)

    row_pairs, row_mean, mixed_scale, mine, quarters = together(row_pairs, row_mean, mixed_scale, mine, quarters)
    cols[1] = swap(mine, 1)
    mixed = contacts("sent", row_pairs, [quarters[d] for d in FAR], mixed_scale, row_mean)

    out_pairs, mixed, walker_lengths = together(out_pairs, mixed, walker_lengths)
    up, down = line_hop(mixed, mixed, 1, feat_count)
    valid = walker_mask(walker_lengths, frames_all, frames_all)
    mask = valid.astype(jnp.float32).reshape(tm_count, parts, 1, CHUNK)
    npairs = jnp.sum(jnp.maximum(walker_lengths - LAG, 0)).astype(jnp.float32)
    factors = jnp.stack([jnp.float32(1.0 / frames_all), npairs])
    near_rows = contacts("own", out_pairs[:, :feats], [table], scale_own, out_mean[:, :feats])
    near_x, near_y = near_rows[:row_feats], near_rows[row_feats:]
    near_x, near_y, mask, factors, up, down, cols = together(near_x, near_y, mask, factors, up, down, cols)
    far = [mixed, up, down]

    across = swap_by_parity(cols[2], 4, 2)
    up, down = line_hop(up, down, 2, feat_count)
    cols[3] = swap(cols[2], 1)
    their_last = swap(cols[4], 1)
    chip_pairs, _ = together(out_pairs[:, feats:], near_x)
    chip_rows = contacts("own", chip_pairs, [table], scale_own, out_mean[:, feats:])
    cols += [their_last, across]
    chip_rows, near_x, near_y, cols, up, down = together(chip_rows, near_x, near_y, cols, up, down)
    far += [up, down, *line_hop(up, down, 3, feat_count)]

    cut = lambda x, start: lax.dynamic_slice_in_dim(x, start, row_feats, axis=0)
    near_x, near_y = swap(near_x, 2), swap(near_y, 4)
    cols.append(swap(cols[6], 1))
    partner, cols = together(cut(chip_rows, row_feats - own_half), cols)
    near = [cut(chip_rows, own_half), swap(partner, 1), near_x, near_y]
    return products(place, mask, factors, near, far, cols)


def solution(mesh):
    def run(coords, frame_scale, pairs, walker_lengths):
        tm_count, feat_count = mesh.shape["tm"], mesh.shape["feat"]
        frames_dev = coords.shape[0] // tm_count
        square = tm_count == 8 and feat_count == 4
        fits = square and frames_dev == 4 * CHUNK and pairs.shape[1] == 16 * 512
        return jax.shard_map(
            shards if fits else plain_shards,
            mesh=mesh,
            in_specs=(P("tm", None, None), P("tm"), P(None, "feat"), P()),
            out_specs=(P("tm", "feat"), P("tm", "feat")),
            check_vma=False,
        )(coords, frame_scale, pairs, walker_lengths)

    return run
```
